128 devices in a mesh: batch: 16 (over y_hi, z, core), tensor: 8 (over x, y_lo).
Axes of the slice: x: 4, y: 4 (y_hi: 2, y_lo: 2; y = y_hi * 2 + y_lo), z: 4, core: 2. Of those that a mesh axis runs over, the one named last changes fastest.
Arguments:
- tokens: bfloat16 [2, 5120, 2048], P(None, 'batch'), may hold values from -6 to 6
- target: bfloat16 [2, 5120, 2048], P(None, 'batch'), may hold values from -6 to 6
- domain_ids: int32 [2], replicated, may hold values from 0 to 3
- domain_counts: int32 [4], replicated, may hold values from 5120 to 20479
- weight_index: int32 [4], replicated, may hold values from 0 to 7
- loss_weights: float32 [8], replicated, may hold values from 0.5 to 4
- w_query: bfloat16 [2048, 2048], P('batch', 'tensor'), may hold values from -0.125 to 0.125
- w_key: bfloat16 [2048, 1024], P('batch', 'tensor'), may hold values from -0.125 to 0.125
- w_value: bfloat16 [2048, 1024], P('batch', 'tensor'), may hold values from -0.125 to 0.125
- w_gate_out: bfloat16 [2048, 2048], P('batch', 'tensor'), may hold values from -0.125 to 0.125
- w_output: bfloat16 [2048, 2048], P('tensor', 'batch'), may hold values from -1.5 to 1.5
- w_gate: bfloat16 [2048, 6144], P('batch', 'tensor'), may hold values from -0.125 to 0.125
- w_up: bfloat16 [2048, 6144], P('batch', 'tensor'), may hold values from -0.125 to 0.125
- w_down: bfloat16 [6144, 2048], P('tensor', 'batch'), may hold values from -0.078125 to 0.078125
- norm_attn: bfloat16 [2048], P('batch'), may hold values from 0.099609375 to 1.8984375
- norm_mlp: bfloat16 [2048], P('batch'), may hold values from 0.099609375 to 1.8984375
- gain_query: bfloat16 [128], P('batch'), may hold values from 0.099609375 to 1.8984375
- gain_key: bfloat16 [128], P('batch'), may hold values from 0.099609375 to 1.8984375
Outputs:
- output: bfloat16 [2, 5120, 2048], P(None, 'batch')
- grad_tokens: float32 [2, 5120, 2048], P(None, 'batch')
- grad_query: float32 [2048, 2048], P('batch', 'tensor')
- grad_key: float32 [2048, 1024], P('batch', 'tensor')
- grad_value: float32 [2048, 1024], P('batch', 'tensor')
- grad_gate_out: float32 [2048, 2048], P('batch', 'tensor')
- grad_output: float32 [2048, 2048], P('tensor', 'batch')
- grad_gate: float32 [2048, 6144], P('batch', 'tensor')
- grad_up: float32 [2048, 6144], P('batch', 'tensor')
- grad_down: float32 [6144, 2048], P('tensor', 'batch')
- grad_norm_attn: float32 [2048], P('batch')
- grad_norm_mlp: float32 [2048], P('batch')
- grad_gain_query: float32 [128], P('batch')
- grad_gain_key: float32 [128], P('batch')
The draws below stay inside these ranges and needn't reach their ends.
All inputs are finite; a program needn't handle non-finite values.
Results may differ from the reference program's by a relative error of at most 0.03.
Values may be sent and summed in bfloat16 or wider, within the bound.
A program may use at most 256 MiB of HBM per device.

```python
import math
import jax
import jax.numpy as jnp
from jax import lax

D = 2048
HQ = 16
HK = 8
HD = 128
FF = 6144
SEQS = 2
DOMAINS = 4
LEVELS = 8
SEQ_LEN = 5120


def place_ends(drawn, rng, low, top_value):
    place = [jax.random.randint(jax.random.fold_in(rng, axis), (), 0, length) for axis, length in enumerate(drawn.shape)]
    longest = drawn.shape.index(max(drawn.shape))
    neighbour = place[:longest] + [(place[longest] + 1) % drawn.shape[longest]] + place[longest + 1:]
    return drawn.at[tuple(place)].set(low).at[tuple(neighbour)].set(top_value)


def level_of(rng, extent, cuts, least, top_value):
    loudness = 1.0
    for axis_at, shards_of in cuts:
        steps = jax.random.uniform(jax.random.fold_in(jax.random.fold_in(rng, 6), axis_at), (shards_of,), jnp.float32, least / len(cuts), top_value / len(cuts))
        loudness = loudness * jnp.repeat(jnp.exp(steps), extent[axis_at] // shards_of).reshape((-1,) + (1,) * (len(extent) - 1 - axis_at))
    return loudness


def scatter_about(own_key, dims, spread, reach, split=(), held_as=jnp.bfloat16):
    gain = level_of(own_key, dims, split, -0.22, 0.18) if split else 1.0
    result = jax.random.normal(own_key, dims, jnp.float32) * spread * gain
    return jnp.minimum(jnp.maximum(result, -reach), reach).astype(held_as)


def setup_inputs(seed: int = 0) -> dict:
    streams_of = jax.random.split(jax.random.key(seed), 19)
    tokens = scatter_about(streams_of[0], (SEQS, SEQ_LEN, D), 1.0, 6.0, ((1, 16),))
    target = scatter_about(streams_of[1], (SEQS, SEQ_LEN, D), 1.0, 6.0, ((1, 16),))
    domain_ids = jax.random.randint(streams_of[2], (SEQS,), 0, DOMAINS).astype(jnp.int32)
    domain_counts = place_ends(jax.random.randint(streams_of[3], (DOMAINS,), SEQ_LEN, 4 * SEQ_LEN), jax.random.fold_in(streams_of[3], 1), SEQ_LEN, (4 * SEQ_LEN) - 1).astype(jnp.int32)
    weight_index = place_ends(jax.random.randint(streams_of[4], (DOMAINS,), 0, LEVELS), jax.random.fold_in(streams_of[4], 1), 0, LEVELS - 1).astype(jnp.int32)
    loss_weights = jnp.clip(jnp.exp(jax.random.uniform(streams_of[5], (LEVELS,), jnp.float32, math.log(0.5), math.log(4.0))), 0.5, 4.0)
    w_query = scatter_about(streams_of[6], (D, HQ * HD), D ** -0.5, 0.125, ((0, 16), (1, 8)))
    w_key = scatter_about(streams_of[7], (D, HK * HD), D ** -0.5, 0.125, ((0, 16), (1, 8)))
    w_value = scatter_about(streams_of[8], (D, HK * HD), D ** -0.5, 0.125, ((0, 16), (1, 8)))
    w_gate_out = scatter_about(streams_of[9], (D, HQ * HD), D ** -0.5, 0.125, ((0, 16), (1, 8)))
    w_output = scatter_about(streams_of[10], (HQ * HD, D), HQ ** -0.5, 1.5, ((0, 8), (1, 16)))
    w_gate = scatter_about(streams_of[11], (D, FF), D ** -0.5, 0.125, ((0, 16), (1, 8)))
    w_up = scatter_about(streams_of[12], (D, FF), D ** -0.5, 0.125, ((0, 16), (1, 8)))
    w_down = scatter_about(streams_of[13], (FF, D), FF ** -0.5, 0.078125, ((0, 8), (1, 16)))
    norm_attn = jnp.clip(1.0 + 0.18 * jax.random.normal(streams_of[14], (D,), jnp.float32), 0.099609375, 1.8984375).astype(jnp.bfloat16)
    norm_mlp = jnp.clip(1.0 + 0.18 * jax.random.normal(streams_of[15], (D,), jnp.float32), 0.099609375, 1.8984375).astype(jnp.bfloat16)
    gain_query = jnp.clip(1.0 + 0.18 * jax.random.normal(streams_of[16], (HD,), jnp.float32), 0.099609375, 1.8984375).astype(jnp.bfloat16)
    gain_key = jnp.clip(1.0 + 0.18 * jax.random.normal(streams_of[17], (HD,), jnp.float32), 0.099609375, 1.8984375).astype(jnp.bfloat16)
    return dict(tokens=tokens, target=target, domain_ids=domain_ids, domain_counts=domain_counts, weight_index=weight_index, loss_weights=loss_weights, w_query=w_query, w_key=w_key, w_value=w_value, w_gate_out=w_gate_out, w_output=w_output, w_gate=w_gate, w_up=w_up, w_down=w_down, norm_attn=norm_attn, norm_mlp=norm_mlp, gain_query=gain_query, gain_key=gain_key)


epsilon = 1e-06
rope_base = 1000000.0
highest = lax.Precision.HIGHEST

@jax.custom_vjp
def low(v):
    return lax.optimization_barrier(v.astype(jnp.bfloat16)).astype(jnp.float32)

@jax.custom_vjp
def low_back(v):
    return v

def low_keep(v):
    return (low(v), None)

def low_pass(kept, grad):
    return (grad,)

def back_keep(v):
    return (v, None)

def back_low(kept, grad):
    return (low(grad),)
low.defvjp(low_keep, low_pass)
low_back.defvjp(back_keep, back_low)

def rms_scale(values, scales):
    return values * lax.rsqrt(lax.optimization_barrier(jnp.mean(values * values, axis=-1, keepdims=True)) + epsilon) * scales

def rotate(values, cosine, sine):
    half_size = values.shape[-1] // 2
    first = values[..., :half_size]
    second = values[..., half_size:]
    return jnp.concatenate([first * cosine - second * sine, second * cosine + first * sine], axis=-1)

def matmul(left, right):
    return jnp.dot(left, right, precision=highest, preferred_element_type=jnp.float32)

def layer(inputs, w_query, w_key, w_value, w_gate_out, w_output, w_gate, w_up, w_down, norm_attn, norm_mlp, gain_query, gain_key):
    length = inputs.shape[0]
    half_size = HD // 2
    positions = jnp.arange(length, dtype=jnp.float32)
    inverse_freq = rope_base ** (-jnp.arange(half_size, dtype=jnp.float32) / half_size)
    angles = positions[:, None] * inverse_freq[None, :]
    cosine = jnp.cos(angles)[:, None, :]
    sine = jnp.sin(angles)[:, None, :]
    normed = low(rms_scale(inputs, norm_attn))
    query_raw = low_back(matmul(normed, w_query)).reshape(length, HQ, HD)
    key_raw = low_back(matmul(normed, w_key)).reshape(length, HK, HD)
    value_low = low(low_back(matmul(normed, w_value))).reshape(length, HK, HD)
    gate_raw = low_back(matmul(normed, w_gate_out))
    group_size = HQ // HK
    query_low = low(rotate(rms_scale(query_raw, gain_query), cosine, sine)).reshape(length, HK, group_size, HD)
    key_low = low(rotate(rms_scale(key_raw, gain_key), cosine, sine))
    raw_scores = low_back(jnp.einsum('qkgd,skd->kgqs', query_low, key_low, precision=highest))
    causal = jnp.arange(length)[None, :] <= jnp.arange(length)[:, None]
    scores = jnp.where(causal, raw_scores * HD ** (-0.5), -jnp.inf)
    prob_low = low(jax.nn.softmax(scores, axis=-1))
    attended = jnp.einsum('kgqs,skd->qkgd', prob_low, value_low, precision=highest).reshape(length, HQ * HD)
    attended = low_back(attended)
    gated = low(attended * jax.nn.sigmoid(gate_raw))
    resid = inputs + low_back(matmul(gated, w_output))
    normed_mlp = low(rms_scale(resid, norm_mlp))
    gate_act = low_back(matmul(normed_mlp, w_gate))
    up_act = low_back(matmul(normed_mlp, w_up))
    hidden = low(jax.nn.silu(gate_act) * up_act)
    return resid + low_back(matmul(hidden, w_down))

def reference(tokens, target, domain_ids, domain_counts, weight_index, loss_weights, w_query, w_key, w_value, w_gate_out, w_output, w_gate, w_up, w_down, norm_attn, norm_mlp, gain_query, gain_key):
    params = tuple((item.astype(jnp.float32) for item in (w_query, w_key, w_value, w_gate_out, w_output, w_gate, w_up, w_down, norm_attn, norm_mlp, gain_query, gain_key)))
    inputs = tokens.astype(jnp.float32)

    def forward(values, *weights):
        checked = jax.checkpoint(lambda sequence: layer(sequence, *weights))

        def scan_step(carry_value, sequence):
            return (carry_value, checked(sequence))
        _, results = lax.scan(scan_step, jnp.zeros((), jnp.float32), values)
        return results
    final, pullback = jax.vjp(forward, inputs, *params)
    domain_factor = loss_weights[weight_index] * SEQ_LEN / domain_counts.astype(jnp.float32)
    seq_weight = domain_factor[domain_ids]
    grad_final = target.astype(jnp.float32) * seq_weight[:, None, None]
    grads = pullback(grad_final)
    return (final.astype(jnp.bfloat16), grads[0], grads[1], grads[2], grads[3], grads[4], grads[5], grads[6], grads[7], grads[8], grads[9], grads[10], grads[11], grads[12])
```

```python
import functools
import math

import jax
import jax.numpy as jnp
from jax import lax
from jax.experimental import pallas as pl
from jax.experimental.pallas import tpu as pltpu
from jax.sharding import PartitionSpec as P

MESH = pl.DeviceIdType.MESH
epsilon = 1e-06
rope_base = 1000000.0
f32 = jnp.float32
bf16 = jnp.bfloat16
MIB = 2**20
ANY = pl.BlockSpec(memory_space=pl.ANY)
VM = pl.BlockSpec(memory_space=pltpu.VMEM)


class Group:
    def __init__(self, kind):
        b = lax.axis_index("batch")
        t = lax.axis_index("tensor")
        if kind == "tensor":
            r, q = lax.div(t, 2), lax.rem(t, 2)
            self.slot = lambda dr, dq: lax.rem(r + dr, 4) * 2 + lax.rem(q + dq, 2)
            at = lambda dr, dq: (b, self.slot(dr, dq))
            self.core = None
        else:
            c = lax.rem(b, 2)
            q, r = lax.div(b, 8), lax.rem(lax.div(b, 2), 4)
            self.slot = lambda dr, dq, dc=0: (
                lax.rem(q + dq, 2) * 4 + lax.rem(r + dr, 4)
            ) * 2 + lax.rem(c + dc, 2)
            at = lambda dr, dq: (self.slot(dr, dq), t)
            self.core = (self.slot(0, 0, 1), t)
        self.right, self.left, self.mate = at(1, 0), at(3, 0), at(0, 1)

    def neighbours(self):
        near = [self.right, self.left, self.mate]
        return near + ([self.core] if self.core is not None else [])


def enter(groups):
    barrier = pltpu.get_barrier_semaphore()
    near = [device for group in groups for device in group.neighbours()]
    for device in near:
        pl.semaphore_signal(barrier, inc=1, device_id=device, device_id_type=MESH)
    pl.semaphore_wait(barrier, len(near))


class Copies:
    def __init__(self, send_sem, recv_sem, local_sem):
        self.send_sem, self.recv_sem, self.local_sem = send_sem, recv_sem, local_sem
        self.count = 0
        self.locals = 0

    def send(self, source, target, device):
        copy = pltpu.make_async_remote_copy(
            src_ref=source,
            dst_ref=target,
            send_sem=self.send_sem.at[self.count],
            recv_sem=self.recv_sem.at[self.count],
            device_id=device,
            device_id_type=MESH,
        )
        self.count += 1
        copy.start()
        return copy

    def local(self, source, target):
        copy = pltpu.make_async_copy(source, target, self.local_sem.at[self.locals])
        self.locals += 1
        copy.start()
        return copy


def half_of(ref, which):
    width = ref.shape[-1] // 2
    return ref.at[:, pl.ds(which * width, width)]


def run_all(*steps):
    waiting = list(steps)
    while waiting:
        for step in list(waiting):
            try:
                next(step)
            except StopIteration:
                waiting.remove(step)


def gather(copies, group, own, slot, split=True):
    s = group.slot
    core_copies = []
    sent = []

    def push(ref, *devices):
        out = [copies.send(ref, ref, device) for device in devices]
        sent.extend(out)
        return out

    def to_core(ref):
        if group.core is not None:
            core_copies.extend(push(ref, group.core))

    home = slot(s(0, 0))
    first = [copies.send(own, home, d) for d in (group.right, group.left, group.mate)]
    sent.extend(first)
    if group.core is not None:
        core_copies.append(copies.send(own, home, group.core))
        sent.append(core_copies[0])
    kept = copies.local(own, home)
    from_left, from_right, from_mate = first
    yield
    from_left.wait_recv()
    left_unit = slot(s(3, 0))
    far = push(half_of(left_unit, 0) if split else left_unit, group.right)
    to_core(left_unit)
    from_right.wait_recv()
    right_unit = slot(s(1, 0))
    if split:
        far += push(half_of(right_unit, 1), group.left)
    to_core(right_unit)
    from_mate.wait_recv()
    mate_unit = slot(s(0, 1))
    mate_left, mate_right = push(mate_unit, group.right, group.left)
    to_core(mate_unit)
    yield
    mate_left.wait_recv()
    left_unit = slot(s(3, 1))
    mate_far = push(half_of(left_unit, 0) if split else left_unit, group.right)
    to_core(left_unit)
    mate_right.wait_recv()
    right_unit = slot(s(1, 1))
    if split:
        mate_far += push(half_of(right_unit, 1), group.left)
    to_core(right_unit)
    yield
    for copy in far:
        copy.wait_recv()
    to_core(slot(s(2, 0)))
    yield
    for copy in mate_far:
        copy.wait_recv()
    to_core(slot(s(2, 1)))
    yield
    for copy in core_copies:
        copy.wait_recv()
    for copy in sent:
        copy.wait_send()
    kept.wait()


def add_rows(target, sources, step=16):
    rows = target.shape[0]

    def body(i, carry):
        at = pl.ds(pl.multiple_of(i * step, step), step)
        total = sources[0][at, :].astype(f32)
        for source in sources[1:]:
            total = total + source[at, :].astype(f32)
        target[at, :] = total.astype(target.dtype)
        return carry

    lax.fori_loop(0, rows // step, body, 0)


def reduce_scratch(rows, width, core):
    unit = pltpu.VMEM((4, rows, width), bf16)
    shapes = [
        pltpu.VMEM((4, rows, width // 2), bf16),
        unit,
        unit,
        pltpu.VMEM((2, rows, width), bf16),
    ]
    if core:
        shapes += [
            pltpu.VMEM((8, rows, width), bf16),
            pltpu.VMEM((2, rows, width), bf16),
        ]
    return shapes


def reduce(copies, group, part, scratch, result):
    far, near, outgoing, mates = scratch[:4]
    core = group.core is not None
    sent = []

    def send(source, target, device):
        copy = copies.send(source, target, device)
        sent.append(copy)
        return copy

    order = [(2, 1), (2, 0), (1, 1), (3, 1), (1, 0), (3, 0), (0, 1), (0, 0)]
    arrived = {}
    if core:
        from_core, far_units = scratch[4:]
        for n, (dr, dq) in enumerate(order):
            arrived[dr, dq] = (send(part(dr, dq, 1), from_core.at[n], group.core), n)
        yield

    def terms(dr, dq):
        if not core:
            return [part(dr, dq)]
        copy, n = arrived[dr, dq]
        copy.wait_recv()
        return [part(dr, dq, 0), from_core.at[n]]

    far_copies = {}
    for dq in (1, 0):
        unit = terms(2, dq)
        if core:
            add_rows(far_units.at[dq], unit)
            unit = [far_units.at[dq]]
        far_copies[dq, 0] = send(half_of(unit[0], 0), far.at[dq * 2], group.right)
        far_copies[dq, 1] = send(half_of(unit[0], 1), far.at[dq * 2 + 1], group.left)
    yield
    near_copies = {}
    for dq in (1, 0):
        for way, (dr, device) in enumerate(((1, group.right), (3, group.left))):
            unit = terms(dr, dq)
            far_copies[dq, way].wait_recv()
            held = outgoing.at[dq * 2 + way]
            there = far.at[dq * 2 + way]
            add_rows(half_of(held, way), [half_of(u, way) for u in unit] + [there])
            add_rows(half_of(held, 1 - way), [half_of(u, 1 - way) for u in unit])
            near_copies[dq, way] = send(held, near.at[dq * 2 + way], device)
        yield
    unit = terms(0, 1)
    for way in (0, 1):
        near_copies[1, way].wait_recv()
    add_rows(mates.at[0], unit + [near.at[2], near.at[3]])
    to_mate = send(mates.at[0], mates.at[1], group.mate)
    yield
    unit = terms(0, 0)
    for way in (0, 1):
        near_copies[0, way].wait_recv()
    to_mate.wait_recv()
    add_rows(result, unit + [near.at[0], near.at[1], mates.at[1]])
    for copy in sent:
        copy.wait_send()


def sems(remote, local):
    return [
        pltpu.SemaphoreType.DMA((remote,)),
        pltpu.SemaphoreType.DMA((remote,)),
        pltpu.SemaphoreType.DMA((max(local, 1),)),
    ]


def params(collective, limit=48):
    return pltpu.CompilerParams(
        collective_id=collective, has_side_effects=True, vmem_limit_bytes=limit * MIB
    )


def batch_gather_kernel(count, *refs):
    own, out = refs[:count], refs[count : 2 * count]
    copies = Copies(*refs[2 * count :])
    group = Group("batch")
    enter([group])
    run_all(
        *[
            gather(copies, group, own[n], functools.partial(lambda o, s: o.at[s], out[n]), n == 0)
            for n in range(count)
        ]
    )


def batch_gather(name, collective, *arrays):
    count = len(arrays)
    return pl.pallas_call(
        functools.partial(batch_gather_kernel, count),
        out_shape=[jax.ShapeDtypeStruct((16,) + a.shape, a.dtype) for a in arrays],
        in_specs=[ANY] * count,
        out_specs=[ANY] * count,
        scratch_shapes=sems(24 * count, count),
        name=name,
        compiler_params=params(collective, 16),
    )(*arrays)


def forward_kernel(scale, q_ref, kv_ref, out_ref, sum_ref, acc_ref):
    b = lax.axis_index("batch")
    seqs, rows, head = q_ref.shape
    seq_dev = kv_ref.shape[1] // seqs
    factor = scale * math.log2(math.e)
    ones = jnp.ones((2 * seq_dev, head), bf16)
    last = lax.div(b, 2)
    tile = rows // 4
    for s in range(seqs):
        at = pl.ds(s * seq_dev, seq_dev)

        def block(pair, masked):
            first, second = pair * 2, pair * 2 + 1
            keys = jnp.concatenate([kv_ref[first, at, :head], kv_ref[second, at, :head]], axis=0)
            values = jnp.concatenate([kv_ref[first, at, head:], kv_ref[second, at, head:]], axis=0)
            wide = jnp.concatenate([values, ones], axis=1)
            for i in range(4):
                here = pl.ds(i * tile, tile)
                scores = lax.dot_general(
                    q_ref[s, here, :], keys, (((1,), (1,)), ((), ())), preferred_element_type=f32
                )
                weights = jnp.exp2(scores * factor)
                if masked:
                    row = lax.broadcasted_iota(jnp.int32, scores.shape, 0) + (i * tile) % seq_dev
                    col = lax.broadcasted_iota(jnp.int32, scores.shape, 1)
                    weights = jnp.where(col + first * seq_dev <= row + b * seq_dev, weights, 0.0)
                acc_ref[here, :] += jnp.dot(weights.astype(bf16), wide, preferred_element_type=f32)

        acc_ref[...] = jnp.zeros_like(acc_ref)

        def body(pair, carry):
            block(pair, False)
            return carry

        lax.fori_loop(0, last, body, 0)
        block(last, True)
        out_ref[s] = acc_ref[:, :head] / acc_ref[:, head:]
        sum_ref[s] = acc_ref[:, head:]


def attention_forward(queries, kv_all, scale):
    shape = jax.ShapeDtypeStruct(queries.shape, f32)
    return pl.pallas_call(
        functools.partial(forward_kernel, scale),
        out_shape=[shape, shape],
        in_specs=[VM, VM],
        out_specs=[VM, VM],
        scratch_shapes=[pltpu.VMEM((queries.shape[1], 2 * queries.shape[2]), f32)],
        name="attention_forward",
        compiler_params=pltpu.CompilerParams(vmem_limit_bytes=40 * MIB),
    )(queries, kv_all)


def backward_kernel(
    scale, q_ref, qt_ref, do_ref, dot_ref, lse_ref, delta_ref, kv_ref, dq_ref, dkv_ref, acc_ref
):
    b = lax.axis_index("batch")
    seqs, rows, head = q_ref.shape
    slots, both, _ = kv_ref.shape
    seq_dev = both // seqs
    factor = scale * math.log2(math.e)

    def clear(slot, carry):
        dkv_ref[slot] = jnp.zeros(dkv_ref.shape[1:], dkv_ref.dtype)
        return carry

    lax.fori_loop(b + 1, slots, clear, 0)
    for s in range(seqs):
        at = pl.ds(s * seq_dev, seq_dev)

        def block(slot, masked):
            keys = kv_ref[slot, at, :head]
            values = kv_ref[slot, at, head:]
            scores = jnp.dot(keys, qt_ref[s], preferred_element_type=f32)
            probs = jnp.exp2(scores * factor - lse_ref[s])
            if masked:
                key = lax.broadcasted_iota(jnp.int32, scores.shape, 0)
                col = lax.broadcasted_iota(jnp.int32, scores.shape, 1)
                row = jnp.where(col >= seq_dev, col - seq_dev, col)
                probs = jnp.where(key <= row, probs, 0.0)
            grad_probs = jnp.dot(values, dot_ref[s], preferred_element_type=f32)
            grad_scores = (probs * (grad_probs - delta_ref[s]) * scale).astype(bf16)
            dkv_ref[slot, at, :head] = jnp.dot(
                grad_scores, q_ref[s], preferred_element_type=f32
            ).astype(bf16)
            dkv_ref[slot, at, head:] = jnp.dot(
                probs.astype(bf16), do_ref[s], preferred_element_type=f32
            ).astype(bf16)
            acc_ref[...] += lax.dot_general(
                keys, grad_scores, (((0,), (0,)), ((), ())), preferred_element_type=f32
            )

        acc_ref[...] = jnp.zeros_like(acc_ref)

        def body(slot, carry):
            block(slot, False)
            return carry

        lax.fori_loop(0, b, body, 0)
        block(b, True)
        dq_ref[s] = acc_ref[...].T


def attention_backward(queries, grad_att, lse, delta, kv_all, scale):
    return pl.pallas_call(
        functools.partial(backward_kernel, scale),
        out_shape=[
            jax.ShapeDtypeStruct(queries.shape, f32),
            jax.ShapeDtypeStruct(kv_all.shape, bf16),
        ],
        in_specs=[VM] * 7,
        out_specs=[VM] * 2,
        scratch_shapes=[pltpu.VMEM((queries.shape[2], queries.shape[1]), f32)],
        name="attention_backward",
        compiler_params=pltpu.CompilerParams(vmem_limit_bytes=48 * MIB),
    )(
        queries,
        queries.transpose(0, 2, 1),
        grad_att,
        grad_att.transpose(0, 2, 1),
        lse,
        delta,
        kv_all,
    )


def rows_at(i, step=16):
    return pl.ds(pl.multiple_of(i * step, step), step)


def residual_kernel(
    part, inputs, gain, pack_a, pack_b, pack_c, normed, resid, wide_a, wide_b, wide_c, *rest
):
    scratch, own, (send_sem, recv_sem, local_sem) = rest[:4], rest[4], rest[5:]
    copies = Copies(send_sem, recv_sem, local_sem)
    tensor, batch = Group("tensor"), Group("batch")
    rows = resid.shape[0]
    enter([tensor, batch])

    def along():
        def unit(dr, dq):
            return part.at[pl.ds(pl.multiple_of(tensor.slot(dr, dq) * rows, 16), rows), :]

        yield from reduce(copies, tensor, unit, scratch, resid)

        def body(i, carry):
            at = rows_at(i)
            total = inputs[at, :] + resid[at, :]
            resid[at, :] = total
            mean = jnp.mean(total * total, axis=-1, keepdims=True)
            own[at, :] = (total * lax.rsqrt(mean + epsilon) * gain[...]).astype(bf16)
            return carry

        lax.fori_loop(0, rows // 16, body, 0)
        yield from gather(
            copies,
            tensor,
            own,
            lambda s: normed.at[pl.ds(pl.multiple_of(s * rows, 16), rows), :],
        )

    run_all(
        gather(copies, batch, pack_a, lambda s: wide_a.at[s]),
        gather(copies, batch, pack_b, lambda s: wide_b.at[s]),
        gather(copies, batch, pack_c, lambda s: wide_c.at[s]),
        along(),
    )


def residual(part, inputs, gain, packs):
    rows, width = inputs.shape
    return pl.pallas_call(
        residual_kernel,
        out_shape=[
            jax.ShapeDtypeStruct(part.shape, bf16),
            jax.ShapeDtypeStruct(inputs.shape, f32),
        ]
        + [jax.ShapeDtypeStruct((16,) + p.shape, bf16) for p in packs],
        in_specs=[VM] * 3 + [ANY] * len(packs),
        out_specs=[ANY, VM] + [ANY] * len(packs),
        scratch_shapes=reduce_scratch(rows, width, False)
        + [pltpu.VMEM((rows, width), bf16)]
        + sems(24 * 5, 5),
        name="residual_and_weights",
        compiler_params=params(3, 40),
    )(part, inputs, gain, *packs)


def norm_back(values, gain, grad):
    inverse = lax.rsqrt(jnp.mean(values * values, axis=-1, keepdims=True) + epsilon)
    scaled = grad * gain
    unit = values * inverse
    inner = jnp.mean(scaled * unit, axis=-1, keepdims=True)
    return (scaled - unit * inner) * inverse, grad * unit


def mlp_back_kernel(
    part, resid, grad_final, gain, weight_part, low, grad_resid, gain_grad, weight_grad, *rest
):
    scratch, scratch_w = rest[:4], rest[4:10]
    own, total = rest[10], rest[11]
    copies = Copies(*rest[12:])
    tensor, batch = Group("tensor"), Group("batch")
    rows = resid.shape[0]
    depth = weight_grad.shape[0]
    enter([tensor, batch])

    def along():
        def unit(dr, dq):
            return part.at[pl.ds(pl.multiple_of(tensor.slot(dr, dq) * rows, 16), rows), :]

        yield from reduce(copies, tensor, unit, scratch, grad_resid)
        total[...] = jnp.zeros_like(total)

        def body(i, carry):
            at = rows_at(i)
            back, terms = norm_back(resid[at, :], gain[...], grad_resid[at, :])
            back = grad_final[at, :] + back
            total[...] += terms
            grad_resid[at, :] = back
            own[at, :] = back.astype(bf16)
            return carry

        lax.fori_loop(0, rows // 16, body, 0)
        gain_grad[...] = jnp.sum(total[...], axis=0, keepdims=True)
        yield from gather(
            copies, tensor, own, lambda s: low.at[pl.ds(pl.multiple_of(s * rows, 16), rows), :]
        )

    def weight_unit(dr, dq, dc):
        return weight_part.at[
            pl.ds(pl.multiple_of(batch.slot(dr, dq, dc) * depth, 16), depth), :
        ]

    run_all(reduce(copies, batch, weight_unit, scratch_w, weight_grad), along())


def mlp_back(part, resid, grad_final, gain, weight_part):
    rows, width = resid.shape
    depth, columns = weight_part.shape[0] // 16, weight_part.shape[1]
    return pl.pallas_call(
        mlp_back_kernel,
        out_shape=[
            jax.ShapeDtypeStruct(part.shape, bf16),
            jax.ShapeDtypeStruct(resid.shape, f32),
            jax.ShapeDtypeStruct((1, width), f32),
            jax.ShapeDtypeStruct((depth, columns), f32),
        ],
        in_specs=[VM] * 5,
        out_specs=[ANY, VM, VM, VM],
        scratch_shapes=reduce_scratch(rows, width, False)
        + reduce_scratch(depth, columns, True)
        + [pltpu.VMEM((rows, width), bf16), pltpu.VMEM((16, width), f32)]
        + sems(24 * 3, 1),
        name="mlp_grad_and_weights",
        compiler_params=params(4, 56),
    )(part, resid, grad_final, gain, weight_part)


def output_kernel(part, resid, kv_part, output, kv_grad, *rest):
    scratch, scratch_kv = rest[:4], rest[4:10]
    own, final = rest[10], rest[11]
    copies = Copies(*rest[12:])
    tensor, batch = Group("tensor"), Group("batch")
    rows = resid.shape[0]
    enter([tensor, batch])

    def along():
        def unit(dr, dq):
            return part.at[pl.ds(pl.multiple_of(tensor.slot(dr, dq) * rows, 16), rows), :]

        yield from reduce(copies, tensor, unit, scratch, final)
        add_rows(own, [final, resid])
        yield from gather(
            copies, tensor, own, lambda s: output.at[pl.ds(pl.multiple_of(s * rows, 16), rows), :]
        )

    run_all(
        reduce(
            copies,
            batch,
            lambda dr, dq, dc: kv_part.at[batch.slot(dr, dq, dc)],
            scratch_kv,
            kv_grad,
        ),
        along(),
    )


def output_and_kv(part, resid, kv_part):
    rows, width = resid.shape
    return pl.pallas_call(
        output_kernel,
        out_shape=[
            jax.ShapeDtypeStruct(part.shape, bf16),
            jax.ShapeDtypeStruct(kv_part.shape[1:], f32),
        ],
        in_specs=[VM] * 3,
        out_specs=[ANY, VM],
        scratch_shapes=reduce_scratch(rows, width, False)
        + reduce_scratch(kv_part.shape[1], kv_part.shape[2], True)
        + [pltpu.VMEM((rows, width), bf16), pltpu.VMEM((rows, width), f32)]
        + sems(24 * 3, 1),
        name="output_and_kv_grads",
        compiler_params=params(5, 48),
    )(part, resid, kv_part)


def last_kernel(
    part, inputs, grad_resid, gain, gain_terms, weight_part, tokens, weight_grad, sums, *rest
):
    scratch, scratch_w = rest[:4], rest[4:10]
    own, held, total, mine, over_tensor, mine_too, over_batch = rest[10:17]
    copies = Copies(*rest[17:])
    tensor, batch = Group("tensor"), Group("batch")
    rows, width = inputs.shape
    depth = weight_grad.shape[0]
    enter([tensor, batch])

    def small():
        yield from gather(copies, tensor, mine, lambda s: over_tensor.at[s], False)
        total_t = over_tensor[0]
        for n in range(1, 8):
            total_t = total_t + over_tensor[n]
        mine_too[...] = total_t
        yield from gather(copies, batch, mine_too, lambda s: over_batch.at[s], False)
        total_b = over_batch[0]
        for n in range(1, 16):
            total_b = total_b + over_batch[n]
        sums[...] = total_b

    def along():
        def unit(dr, dq):
            return part.at[pl.ds(pl.multiple_of(tensor.slot(dr, dq) * rows, 16), rows), :]

        yield from reduce(copies, tensor, unit, scratch, held)
        total[...] = jnp.zeros_like(total)

        def body(i, carry):
            at = rows_at(i)
            back, terms = norm_back(inputs[at, :], gain[...], held[at, :])
            total[...] += terms
            own[at, :] = (grad_resid[at, :] + back).astype(bf16)
            return carry

        lax.fori_loop(0, rows // 16, body, 0)
        gain_row = jnp.sum(total[...], axis=0, keepdims=True)
        mine[...] = gain_terms[...]
        for n in range(width // 128):
            mine[pl.ds(n, 1), :] = gain_row[:, n * 128 : (n + 1) * 128]
        big = gather(
            copies, tensor, own, lambda s: tokens.at[pl.ds(pl.multiple_of(s * rows, 16), rows), :]
        )
        few = small()
        for _ in big:
            next(few, None)
            yield
        yield from few

    def weight_unit(dr, dq, dc):
        return weight_part.at[
            pl.ds(pl.multiple_of(batch.slot(dr, dq, dc) * depth, 16), depth), :
        ]

    run_all(reduce(copies, batch, weight_unit, scratch_w, weight_grad), along())


def last_step(part, inputs, grad_resid, gain, gain_terms, weight_part):
    rows, width = inputs.shape
    depth, columns = weight_part.shape[0] // 16, weight_part.shape[1]
    few = gain_terms.shape
    return pl.pallas_call(
        last_kernel,
        out_shape=[
            jax.ShapeDtypeStruct(part.shape, bf16),
            jax.ShapeDtypeStruct((depth, columns), f32),
            jax.ShapeDtypeStruct(few, f32),
        ],
        in_specs=[VM] * 6,
        out_specs=[ANY, VM, VM],
        scratch_shapes=reduce_scratch(rows, width, False)
        + reduce_scratch(depth, columns, True)
        + [
            pltpu.VMEM((rows, width), bf16),
            pltpu.VMEM((rows, width), f32),
            pltpu.VMEM((16, width), f32),
            pltpu.VMEM(few, f32),
            pltpu.VMEM((8,) + few, f32),
            pltpu.VMEM(few, f32),
            pltpu.VMEM((16,) + few, f32),
        ]
        + sems(24 * 5, 3),
        name="input_grad_and_weights",
        compiler_params=params(6, 48),
    )(part, inputs, grad_resid, gain, gain_terms, weight_part)


def rms_scale(values, scales):
    return values * lax.rsqrt(jnp.mean(values * values, axis=-1, keepdims=True) + epsilon) * scales


def rotate(values, cosine, sine):
    half_size = values.shape[-1] // 2
    first = values[..., :half_size]
    second = values[..., half_size:]
    return jnp.concatenate(
        [first * cosine - second * sine, second * cosine + first * sine], axis=-1
    )


def head_prepare(values, scales, cosine, sine):
    head_size = scales.shape[0]
    shaped = values.reshape(values.shape[0], values.shape[1] // head_size, head_size)
    return rotate(rms_scale(shaped, scales), cosine, sine).reshape(values.shape)


def gate_apply(attended, gate_raw):
    return attended * jax.nn.sigmoid(gate_raw)


def swiglu(gate_act, up_act):
    return jax.nn.silu(gate_act) * up_act


def dot(left, right):
    return jnp.dot(left, right, preferred_element_type=f32)


def dot_t(left, right):
    return lax.dot_general(left, right, (((1,), (1,)), ((), ())), preferred_element_type=f32)


def t_dot(left, right):
    return lax.dot_general(left, right, (((0,), (0,)), ((), ())), preferred_element_type=f32)


def shards(
    tokens,
    target,
    domain_ids,
    domain_counts,
    weight_index,
    loss_weights,
    w_query,
    w_key,
    w_value,
    w_gate_out,
    w_output,
    w_gate,
    w_up,
    w_down,
    norm_attn,
    norm_mlp,
    gain_query,
    gain_key,
):
    seq_count, seq_dev, width = tokens.shape
    rows = seq_count * seq_dev
    members = lax.axis_size("tensor")
    batch_count = lax.axis_size("batch")
    b, t = lax.axis_index("batch"), lax.axis_index("tensor")
    own_rows = rows // members
    seq_len = seq_dev * batch_count
    head = gain_query.shape[0] * batch_count
    scale = head ** (-0.5)
    q_cols, k_cols = w_query.shape[1], w_key.shape[1]
    heads = q_cols // head

    pack_attn = jnp.concatenate([w_query, w_key, w_value, w_gate_out, w_output.T], axis=1)
    few = jnp.zeros((16, norm_attn.shape[0]), bf16)
    few = few.at[0].set(norm_attn).at[1].set(norm_mlp)
    few = few.at[2, : gain_query.shape[0]].set(gain_query)
    few = few.at[3, : gain_key.shape[0]].set(gain_key)
    wide_attn, wide_few = batch_gather("attention_weights", 1, pack_attn, few)
    wide_attn = wide_attn.reshape(width, pack_attn.shape[1])
    proj_cols = 2 * q_cols + 2 * k_cols
    w_proj = wide_attn[:, :proj_cols]
    w_out_t = wide_attn[:, proj_cols:]
    gain_attn = wide_few[:, 0].reshape(1, width).astype(f32)
    gain_mlp = wide_few[:, 1].reshape(1, width).astype(f32)
    gain_q = wide_few[:, 2, : gain_query.shape[0]].reshape(head).astype(f32)
    gain_k = wide_few[:, 3, : gain_key.shape[0]].reshape(head).astype(f32)

    half_size = head // 2
    pos_local = b * seq_dev + jnp.arange(seq_dev, dtype=jnp.int32)
    inverse_freq = rope_base ** (-jnp.arange(half_size, dtype=f32) / half_size)
    row_pos = jnp.tile(pos_local, seq_count).astype(f32)
    angles = row_pos[:, None] * inverse_freq[None, :]
    cosine = jnp.cos(angles)[:, None, :]
    sine = jnp.sin(angles)[:, None, :]

    tokens_low = tokens.reshape(rows, width)
    normed_low = rms_scale(tokens_low.astype(f32), gain_attn).astype(bf16)
    proj = dot(normed_low, w_proj)
    query_raw = proj[:, :q_cols]
    key_raw = proj[:, q_cols : q_cols + k_cols]
    value_raw = proj[:, q_cols + k_cols : q_cols + 2 * k_cols]
    gate_raw = proj[:, q_cols + 2 * k_cols :]

    def prepare(values, scales):
        return head_prepare(values, scales, cosine, sine)

    query_low = prepare(query_raw, gain_q).astype(bf16)
    key_low = prepare(key_raw, gain_k).astype(bf16)
    kv_own = jnp.concatenate([key_low, value_raw.astype(bf16)], axis=1)
    (kv_all,) = batch_gather("keys_and_values", 2, kv_own)

    def by_head(values):
        shaped = values.reshape(seq_count, seq_dev, heads, head)
        return shaped.transpose(0, 2, 1, 3).reshape(seq_count, heads * seq_dev, head)

    def by_row(values):
        shaped = values.reshape(seq_count, heads, seq_dev, head)
        return shaped.transpose(0, 2, 1, 3).reshape(rows, heads * head)

    queries = by_head(query_low)
    attended_heads, sums = attention_forward(queries, kv_all, scale)
    attended = by_row(attended_heads)
    lse = jnp.log2(sums[:, :, 0])[:, None, :]
    gated_low = gate_apply(attended, gate_raw).astype(bf16)
    attn_part = dot_t(gated_low, w_out_t).astype(bf16)

    inputs_own = lax.dynamic_slice_in_dim(tokens_low, t * own_rows, own_rows, 0).astype(f32)
    packs = (w_gate, w_up, w_down.T)
    normed_mlp_low, resid_own, wide_gate, wide_up, wide_down = residual(
        attn_part, inputs_own, gain_mlp, packs
    )
    ff = w_gate.shape[1]
    wide_gate, wide_up, wide_down = (
        w.reshape(width, ff) for w in (wide_gate, wide_up, wide_down)
    )

    domain_range = jnp.arange(domain_counts.shape[0], dtype=jnp.int32)
    level_pick = (
        weight_index[:, None] == jnp.arange(loss_weights.shape[0], dtype=jnp.int32)[None, :]
    ).astype(f32)
    domain_factor = (
        jnp.sum(level_pick * loss_weights[None, :], axis=1) * seq_len / domain_counts.astype(f32)
    )
    seq_pick = (domain_ids[:, None] == domain_range[None, :]).astype(f32)
    seq_weight = jnp.sum(seq_pick * domain_factor[None, :], axis=1)
    row_weight = jnp.repeat(seq_weight, seq_dev)[:, None]
    target_low = target.reshape(rows, width)
    grad_final_low = (target_low.astype(f32) * row_weight).astype(bf16)
    grad_final_own = lax.dynamic_slice_in_dim(target_low, t * own_rows, own_rows, 0).astype(
        f32
    ) * lax.dynamic_slice_in_dim(row_weight, t * own_rows, own_rows, 0)

    gate_act = dot(normed_mlp_low, wide_gate)
    up_act = dot(normed_mlp_low, wide_up)
    hidden_low = swiglu(gate_act, up_act).astype(bf16)
    down_part = dot_t(hidden_low, wide_down).astype(bf16)
    grad_hidden = dot(grad_final_low, wide_down)
    _, swiglu_back = jax.vjp(swiglu, gate_act, up_act)
    grad_gate_act, grad_up_act = swiglu_back(grad_hidden)
    grad_gate_low = grad_gate_act.astype(bf16)
    grad_up_low = grad_up_act.astype(bf16)
    mlp_input_part = (dot_t(grad_gate_low, wide_gate) + dot_t(grad_up_low, wide_up)).astype(bf16)
    mlp_weight_part = jnp.concatenate(
        [
            t_dot(normed_mlp_low, grad_gate_low).astype(bf16),
            t_dot(normed_mlp_low, grad_up_low).astype(bf16),
            t_dot(grad_final_low, hidden_low).astype(bf16),
        ],
        axis=1,
    )
    grad_resid_low, grad_resid_own, norm_mlp_terms, mlp_weight_grad = mlp_back(
        mlp_input_part, resid_own, grad_final_own, gain_mlp, mlp_weight_part
    )

    grad_gated = dot(grad_resid_low, w_out_t)
    _, gate_back = jax.vjp(gate_apply, attended, gate_raw)
    grad_attended, grad_gate_raw = gate_back(grad_gated)
    grad_att_low = grad_attended.astype(bf16)
    grad_gate_raw_low = grad_gate_raw.astype(bf16)
    grad_att_heads = by_head(grad_att_low)
    delta = jnp.sum(grad_att_heads.astype(f32) * attended_heads, axis=-1)[:, None, :]
    grad_query_heads, kv_part = attention_backward(
        queries, grad_att_heads, lse, delta, kv_all, scale
    )
    output, kv_grad = output_and_kv(down_part, resid_own, kv_part)

    _, query_back = jax.vjp(prepare, query_raw, gain_q)
    query_pre, grad_gain_q = query_back(by_row(grad_query_heads))
    _, key_back = jax.vjp(prepare, key_raw, gain_k)
    key_pre, grad_gain_k = key_back(kv_grad[:, :k_cols])
    proj_grad_low = jnp.concatenate(
        [
            query_pre.astype(bf16),
            key_pre.astype(bf16),
            kv_grad[:, k_cols:].astype(bf16),
            grad_gate_raw_low,
        ],
        axis=1,
    )
    attn_input_part = dot_t(proj_grad_low, w_proj).astype(bf16)
    attn_weight_part = jnp.concatenate(
        [
            t_dot(normed_low, proj_grad_low).astype(bf16),
            t_dot(grad_resid_low, gated_low).astype(bf16),
        ],
        axis=1,
    )
    norm_rows = width // 128
    gain_terms = jnp.zeros((2 * norm_rows + 8, 128), f32)
    gain_terms = gain_terms.at[norm_rows : 2 * norm_rows].set(norm_mlp_terms.reshape(norm_rows, 128))
    gain_terms = gain_terms.at[2 * norm_rows].set(grad_gain_q)
    gain_terms = gain_terms.at[2 * norm_rows + 1].set(grad_gain_k)
    grad_tokens, attn_weight_grad, sums_all = last_step(
        attn_input_part, inputs_own, grad_resid_own, gain_attn, gain_terms, attn_weight_part
    )

    def own_part(flat, like):
        return lax.dynamic_slice_in_dim(flat, b * like.shape[0], like.shape[0], 0)

    pieces = [0, q_cols, q_cols + k_cols, q_cols + 2 * k_cols, proj_cols, pack_attn.shape[1]]
    grads = [attn_weight_grad[:, lo:hi] for lo, hi in zip(pieces[:-1], pieces[1:])]
    return (
        output.reshape(tokens.shape),
        grad_tokens.astype(f32).reshape(tokens.shape),
        grads[0],
        grads[1],
        grads[2],
        grads[3],
        grads[4].T,
        mlp_weight_grad[:, :ff],
        mlp_weight_grad[:, ff : 2 * ff],
        mlp_weight_grad[:, 2 * ff :].T,
        own_part(sums_all[:norm_rows].reshape(-1), norm_attn),
        own_part(sums_all[norm_rows : 2 * norm_rows].reshape(-1), norm_mlp),
        own_part(sums_all[2 * norm_rows], gain_query),
        own_part(sums_all[2 * norm_rows + 1], gain_key),
    )


def solution(mesh):
    in_specs = (
        P(None, "batch", None),
        P(None, "batch", None),
        P(),
        P(),
        P(),
        P(),
        P("batch", "tensor"),
        P("batch", "tensor"),
        P("batch", "tensor"),
        P("batch", "tensor"),
        P("tensor", "batch"),
        P("batch", "tensor"),
        P("batch", "tensor"),
        P("tensor", "batch"),
        P("batch"),
        P("batch"),
        P("batch"),
        P("batch"),
    )
    out_specs = (
        P(None, "batch", None),
        P(None, "batch", None),
        P("batch", "tensor"),
        P("batch", "tensor"),
        P("batch", "tensor"),
        P("batch", "tensor"),
        P("tensor", "batch"),
        P("batch", "tensor"),
        P("batch", "tensor"),
        P("tensor", "batch"),
        P("batch"),
        P("batch"),
        P("batch"),
        P("batch"),
    )
    return jax.shard_map(shards, mesh=mesh, in_specs=in_specs, out_specs=out_specs, check_vma=False)
```

```python
import functools
import itertools
import math

import jax
import jax.numpy as jnp
from jax import lax
from jax.experimental import pallas as pl
from jax.experimental.pallas import tpu as pltpu
from jax.sharding import PartitionSpec as P

MESH = pl.DeviceIdType.MESH
epsilon = 1e-06
rope_base = 1000000.0
f32 = jnp.float32
bf16 = jnp.bfloat16
MIB = 2**20
ANY = pl.BlockSpec(memory_space=pl.ANY)
VM = pl.BlockSpec(memory_space=pltpu.VMEM)


class Group:
    def __init__(self, kind, core=True):
        b = lax.axis_index("batch")
        t = lax.axis_index("tensor")
        c = lax.rem(b, 2)
        self.c, self.t = c, t
        if kind == "tensor":
            r, q = lax.div(t, 2), lax.rem(t, 2)
            self.slot = lambda dr, dq: lax.rem(r + dr, 4) * 2 + lax.rem(q + dq, 2)
            at = lambda dr, dq: (b, self.slot(dr, dq))
        else:
            q, r = lax.div(b, 8), lax.rem(lax.div(b, 2), 4)
            self.chip = lambda dr, dq: lax.rem(q + dq, 2) * 4 + lax.rem(r + dr, 4)
            self.slot = lambda dr, dq, dc=0: self.chip(dr, dq) * 2 + lax.rem(c + dc, 2)
            at = lambda dr, dq: (self.slot(dr, dq), t)
        self.core = (b + 1 - 2 * c, t) if core else None
        self.right, self.left, self.mate = at(1, 0), at(3, 0), at(0, 1)
        self.others = [at(dr, dq) for dr in range(4) for dq in range(2) if dr or dq]
        self.steps = [(dr, dq) for dr in range(4) for dq in range(2) if dr or dq]


def enter(devices):
    barrier = pltpu.get_barrier_semaphore()
    for device in devices:
        pl.semaphore_signal(barrier, inc=1, device_id=device, device_id_type=MESH)
    pl.semaphore_wait(barrier, len(devices))


def near(*groups):
    devices = [d for g in groups for d in (g.right, g.left, g.mate)]
    cores = [g.core for g in groups if g.core is not None]
    return devices + cores[:1]


class Copies:
    def __init__(self, send_sem, recv_sem, local_sem):
        self.send_sem, self.recv_sem, self.local_sem = send_sem, recv_sem, local_sem
        self.count = 0
        self.locals = 0

    def send(self, source, target, device):
        copy = pltpu.make_async_remote_copy(
            src_ref=source,
            dst_ref=target,
            send_sem=self.send_sem.at[self.count],
            recv_sem=self.recv_sem.at[self.count],
            device_id=device,
            device_id_type=MESH,
        )
        self.count += 1
        copy.start()
        return copy

    def local(self, source, target):
        copy = pltpu.make_async_copy(source, target, self.local_sem.at[self.locals])
        self.locals += 1
        copy.start()
        return copy


def half_of(ref, which):
    width = ref.shape[-1] // 2
    lead = (slice(None),) * (len(ref.shape) - 1)
    return ref.at[lead + (pl.ds(which * width, width),)]


def run_all(*steps):
    waiting = list(steps)
    while waiting:
        for step in list(waiting):
            try:
                next(step)
            except StopIteration:
                waiting.remove(step)


def gather(copies, group, own, slot, split=True, source=None):
    s = group.slot
    core_copies = []
    sent = []

    def push(ref, *devices):
        out = [copies.send(ref, ref, device) for device in devices]
        sent.extend(out)
        return out

    def to_core(ref):
        if group.core is not None:
            core_copies.extend(push(ref, group.core))

    def core_wait(count):
        for copy in core_copies[:count]:
            copy.wait_recv()
        del core_copies[:count]

    home = slot(s(0, 0))
    source = own if source is None else source
    first = [copies.send(source, home, d) for d in (group.right, group.left, group.mate)]
    sent.extend(first)
    kept = None
    if own is not None:
        kept = copies.local(own, home)
        if group.core is not None:
            core_copies.append(copies.send(own, home, group.core))
            sent.append(core_copies[0])
    from_left, from_right, from_mate = first
    yield []
    from_left.wait_recv()
    left_unit = slot(s(3, 0))
    far = push(half_of(left_unit, 0) if split else left_unit, group.right)
    to_core(left_unit)
    from_right.wait_recv()
    right_unit = slot(s(1, 0))
    if split:
        far += push(half_of(right_unit, 1), group.left)
    to_core(right_unit)
    from_mate.wait_recv()
    mate_unit = slot(s(0, 1))
    mate_left, mate_right = push(mate_unit, group.right, group.left)
    to_core(mate_unit)
    if own is not None:
        core_wait(1)
        kept.wait()
    yield [(0, 0)]
    for copy in far:
        copy.wait_recv()
    far_unit = slot(s(2, 0))
    (mate_far,) = push(far_unit, group.mate)
    to_core(far_unit)
    yield []
    mate_left.wait_recv()
    to_core(slot(s(3, 1)))
    mate_right.wait_recv()
    to_core(slot(s(1, 1)))
    core_wait(3)
    yield [(3, 0), (1, 0), (0, 1)]
    mate_far.wait_recv()
    to_core(slot(s(2, 1)))
    core_wait(3)
    yield [(2, 0), (3, 1), (1, 1)]
    core_wait(1)
    yield [(2, 1)]
    for copy in sent:
        copy.wait_send()


def add_rows(target, sources, step=16):
    rows = target.shape[0]

    def body(i, carry):
        at = pl.ds(pl.multiple_of(i * step, step), step)
        total = sources[0][at, :].astype(f32)
        for source in sources[1:]:
            total = total + source[at, :].astype(f32)
        target[at, :] = total.astype(target.dtype)
        return carry

    lax.fori_loop(0, rows // step, body, 0)


def reduce_scratch(rows, width, core):
    unit = pltpu.VMEM((4, rows, width), bf16)
    shapes = [
        pltpu.VMEM((4, rows, width // 2), bf16),
        unit,
        unit,
        pltpu.VMEM((2, rows, width), bf16),
    ]
    if core:
        shapes += [
            pltpu.VMEM((8, rows, width), bf16),
            pltpu.VMEM((2, rows, width), bf16),
        ]
    return shapes


def reduce(copies, group, part, scratch, result):
    far, near, outgoing, mates = scratch[:4]
    core = group.core is not None
    sent = []

    def send(source, target, device):
        copy = copies.send(source, target, device)
        sent.append(copy)
        return copy

    order = [(2, 1), (2, 0), (1, 1), (3, 1), (1, 0), (3, 0), (0, 1), (0, 0)]
    arrived = {}
    if core:
        from_core, far_units = scratch[4:]
        for n, (dr, dq) in enumerate(order):
            arrived[dr, dq] = (send(part(dr, dq, 1), from_core.at[n], group.core), n)
        yield

    def terms(dr, dq):
        if not core:
            return [part(dr, dq)]
        copy, n = arrived[dr, dq]
        copy.wait_recv()
        return [part(dr, dq, 0), from_core.at[n]]

    far_copies = {}
    for dq in (1, 0):
        unit = terms(2, dq)
        if core:
            add_rows(far_units.at[dq], unit)
            unit = [far_units.at[dq]]
        far_copies[dq, 0] = send(half_of(unit[0], 0), far.at[dq * 2], group.right)
        far_copies[dq, 1] = send(half_of(unit[0], 1), far.at[dq * 2 + 1], group.left)
    yield
    near_copies = {}
    for dq in (1, 0):
        for way, (dr, device) in enumerate(((1, group.right), (3, group.left))):
            unit = terms(dr, dq)
            far_copies[dq, way].wait_recv()
            held = outgoing.at[dq * 2 + way]
            there = far.at[dq * 2 + way]
            add_rows(half_of(held, way), [half_of(u, way) for u in unit] + [there])
            add_rows(half_of(held, 1 - way), [half_of(u, 1 - way) for u in unit])
            near_copies[dq, way] = send(held, near.at[dq * 2 + way], device)
        yield
    unit = terms(0, 1)
    for way in (0, 1):
        near_copies[1, way].wait_recv()
    add_rows(mates.at[0], unit + [near.at[2], near.at[3]])
    to_mate = send(mates.at[0], mates.at[1], group.mate)
    yield
    unit = terms(0, 0)
    for way in (0, 1):
        near_copies[0, way].wait_recv()
    to_mate.wait_recv()
    add_rows(result, unit + [near.at[0], near.at[1], mates.at[1]])
    for copy in sent:
        copy.wait_send()


def sems(remote, local):
    return [
        pltpu.SemaphoreType.DMA((remote,)),
        pltpu.SemaphoreType.DMA((remote,)),
        pltpu.SemaphoreType.DMA((max(local, 1),)),
    ]


def params(collective, limit=48):
    return pltpu.CompilerParams(
        collective_id=collective, has_side_effects=True, vmem_limit_bytes=limit * MIB
    )


def rows_at(i, step=16):
    return pl.ds(pl.multiple_of(i * step, step), step)


def each_rows(rows, step, body):
    def run(i, carry):
        body(rows_at(i, step))
        return carry

    lax.fori_loop(0, rows // step, run, 0)


def prepare_head(values, gain, cosine, sine):
    half_size = values.shape[1] // 2
    mean = jnp.mean(values * values, axis=-1, keepdims=True)
    scaled = values * lax.rsqrt(mean + epsilon) * gain
    return scaled * cosine + pltpu.roll(scaled, half_size, 1) * sine


def forward_kernel(
    scale,
    tokens,
    cosine,
    sine,
    pack_a,
    pack_b,
    mlp_a,
    mlp_b,
    mlp_c,
    normed_out,
    query_raw,
    kv_raw,
    gate_raw,
    queries,
    kv_out,
    attended,
    lse,
    gated,
    normed_mlp,
    resid,
    wide_kvo,
    wide_qg,
    w_out_out,
    wide_a,
    wide_b,
    wide_c,
    gain_wide,
    gain_head,
    normed,
    inverse,
    w_kvo,
    w_qg,
    w_out,
    kv_own,
    kv_all,
    acc,
    rows_all,
    own,
    send_sem,
    recv_sem,
    local_sem,
):
    copies = Copies(send_sem, recv_sem, local_sem)
    tensor, batch = Group("tensor"), Group("batch")
    b = lax.axis_index("batch")
    rows, width = tokens.shape
    cols = query_raw.shape[1]
    own_rows = resid.shape[0]
    seqs, head_rows, head = queries.shape
    heads = query_raw.shape[1] // head
    seq_dev = rows // seqs
    enter(tensor.others + near(batch))

    def batch_gather(source, target, split=True):
        return gather(copies, batch, source, lambda s: target.at[s], split)

    a_steps = batch_gather(pack_a, w_kvo)
    b_steps = batch_gather(pack_b, w_qg)
    next(a_steps)
    next(b_steps)

    def invert(at):
        values = tokens[at, :].astype(f32)
        mean = jnp.mean(values * values, axis=-1, keepdims=True)
        inverse[at, :] = jnp.broadcast_to(lax.rsqrt(mean + epsilon), (16, 128))

    each_rows(rows, 16, invert)
    next(a_steps)
    next(b_steps)
    for _ in a_steps:
        pass
    depth = pack_b.shape[0]
    half = tensor.c * 8
    kept = [copies.local(w_kvo, wide_kvo)]
    out_home = copies.local(w_kvo.at[:, pl.ds(0, depth), pl.ds(cols, cols)], w_out.at[tensor.t])
    wide_out_steps = gather(
        copies,
        tensor,
        None,
        lambda s: w_out.at[s, pl.ds(half, 8)],
        source=w_kvo.at[pl.ds(half, 8), pl.ds(0, depth), pl.ds(cols, cols)],
    )
    next(wide_out_steps)
    gain_wide[...] = jnp.zeros_like(gain_wide)
    gain_head[...] = jnp.zeros_like(gain_head)
    total = jnp.zeros((16, 128), f32)
    for n in range(16):
        entry = w_kvo[n, depth:, 0:128].astype(f32)
        gain_wide[0:2, n * 128 : (n + 1) * 128] = entry[0:2]
        total = total + entry
    gain_head[0:2, :] = total[2:4]

    def normalise(at):
        scaled = tokens[at, :].astype(f32) * inverse[at, 0:1] * gain_wide[0:1, :]
        normed[at, :] = scaled.astype(bf16)

    each_rows(rows, 16, normalise)
    kept.append(copies.local(normed, normed_out))

    def project(weights, at):
        return jnp.dot(normed[at, :], weights.reshape(width, cols), preferred_element_type=f32)

    for s in range(seqs):
        at = pl.ds(s * seq_dev, seq_dev)
        raw = project(w_kvo[:, 0:depth, 0:cols], at)
        kv_raw[at, :] = raw
        key = prepare_head(raw[:, :head], gain_head[1:2, :], cosine[...], sine[...])
        kv_own[at, :head] = key.astype(bf16)
        kv_own[at, head:] = raw[:, head:].astype(bf16)
    all_steps = batch_gather(kv_own, kv_all)
    next(all_steps)
    for _ in b_steps:
        pass
    kept.append(copies.local(w_qg, wide_qg))
    for s in range(seqs):
        at = pl.ds(s * seq_dev, seq_dev)
        raw = project(w_qg[:, :, 0:cols], at)
        query_raw[at, :] = raw
        for h in range(heads):
            values = prepare_head(
                raw[:, h * head : (h + 1) * head], gain_head[0:1, :], cosine[...], sine[...]
            )
            queries[s, h * seq_dev : (h + 1) * seq_dev, :] = values.astype(bf16)
        gate_raw[at, :] = project(w_qg[:, :, cols:], at)

    factor = scale * math.log2(math.e)
    ones = jnp.ones((2 * seq_dev, head), bf16)
    tile = head_rows // 4
    acc[...] = jnp.zeros_like(acc)

    def block(pair, masked):
        def body(s, carry):
            at = rows_at(s, seq_dev)
            keys = jnp.concatenate(
                [kv_all[pair * 2, at, :head], kv_all[pair * 2 + 1, at, :head]], axis=0
            )
            values = jnp.concatenate(
                [kv_all[pair * 2, at, head:], kv_all[pair * 2 + 1, at, head:]], axis=0
            )
            wide = jnp.concatenate([values, ones], axis=1)
            for i in range(4):
                here = pl.ds(i * tile, tile)
                scores = lax.dot_general(
                    queries[s, here, :], keys, (((1,), (1,)), ((), ())), preferred_element_type=f32
                )
                weights = jnp.exp2(scores * factor)
                if masked:
                    row = lax.broadcasted_iota(jnp.int32, scores.shape, 0) + (i * tile) % seq_dev
                    col = lax.broadcasted_iota(jnp.int32, scores.shape, 1)
                    ahead = (pair * 2 - b) * seq_dev
                    weights = jnp.where(col + ahead <= row, weights, 0.0)
                acc[s, here, :] += jnp.dot(weights.astype(bf16), wide, preferred_element_type=f32)
            return carry

        lax.fori_loop(0, seqs, body, 0)

    here = batch.chip(0, 0)

    def attend(ready):
        for dr, dq in ready:
            if (dr, dq) == (0, 0):
                block(here, True)
            else:
                pair = batch.chip(dr, dq)

                @pl.when(pair < here)
                def _():
                    block(pair, False)

    mlp_steps = [
        batch_gather(mlp_a, wide_a),
        batch_gather(mlp_b, wide_b),
        batch_gather(mlp_c, wide_c),
    ]
    attend(next(all_steps))
    next(wide_out_steps)
    attend(next(all_steps))
    next(wide_out_steps)
    ready = next(all_steps)
    for step in mlp_steps:
        next(step)
    attend(ready)
    ready = next(all_steps)
    next(wide_out_steps)
    attend(ready)
    attend(next(all_steps))
    for _ in all_steps:
        pass
    kept.append(copies.local(kv_all, kv_out))
    for s in range(seqs):
        sums = acc[s, :, head:]
        lse[s] = jnp.log2(sums).T[0:1, :]
        out = acc[s, :, :head] / sums
        for h in range(heads):
            at, cols = pl.ds(s * seq_dev, seq_dev), pl.ds(h * head, head)
            part = out[h * seq_dev : (h + 1) * seq_dev]
            attended[at, cols] = part
            gated[at, cols] = (part * jax.nn.sigmoid(gate_raw[at, cols])).astype(bf16)

    def unit_rows(ref, slot):
        return ref.at[pl.ds(pl.multiple_of(slot * own_rows, 16), own_rows), :]

    exchanged = [
        copies.send(unit_rows(gated, tensor.slot(*step)), rows_all.at[tensor.t], device)
        for step, device in zip(tensor.steps, tensor.others)
    ]
    rows_all[tensor.t] = unit_rows(gated, tensor.t)[...]
    run_all(wide_out_steps, *[itertools.islice(step, 1) for step in mlp_steps])
    out_home.wait()
    kept.append(copies.local(w_out, w_out_out))
    for copy in exchanged:
        copy.wait_recv()
    resid[...] = unit_rows(tokens, tensor.t)[...].astype(f32)

    def out_term(n, carry):
        resid[...] += lax.dot_general(
            rows_all[n],
            w_out[n].reshape(width, -1),
            (((1,), (1,)), ((), ())),
            preferred_element_type=f32,
        )
        return carry

    lax.fori_loop(0, 8, out_term, 0)

    def normalise_own(at):
        values = resid[at, :]
        mean = jnp.mean(values * values, axis=-1, keepdims=True)
        own[at, :] = (values * lax.rsqrt(mean + epsilon) * gain_wide[1:2, :]).astype(bf16)

    each_rows(own_rows, 16, normalise_own)
    tensor.core = None
    own_steps = gather(copies, tensor, own, lambda s: unit_rows(normed_mlp, s))
    run_all(own_steps, *mlp_steps)
    for copy in exchanged:
        copy.wait_send()
    for copy in kept:
        copy.wait()


def forward(tokens, cosine, sine, packs, mlp_packs, scale, seqs):
    rows, width = tokens.shape
    cols = packs[1].shape[1] // 2
    head = cosine.shape[1]
    own_rows = rows // 8
    heads = cols // head
    shape = jax.ShapeDtypeStruct
    weight_a, weight_b = (16,) + packs[0].shape, (16,) + packs[1].shape
    weight_out = (8, 16, packs[1].shape[0], cols)
    outs = [
        (shape((rows, width), bf16), ANY),
        (shape((rows, cols), f32), VM),
        (shape((rows, cols), f32), VM),
        (shape((rows, cols), f32), VM),
        (shape((seqs, heads * rows // seqs, head), bf16), VM),
        (shape((16, rows, cols), bf16), ANY),
        (shape((rows, cols), f32), VM),
        (shape((seqs, 1, heads * rows // seqs), f32), VM),
        (shape((rows, cols), bf16), VM),
        (shape((rows, width), bf16), ANY),
        (shape((own_rows, width), f32), VM),
        (shape(weight_a, bf16), ANY),
        (shape(weight_b, bf16), ANY),
        (shape(weight_out, bf16), ANY),
    ]
    outs += [(shape((16,) + p.shape, bf16), ANY) for p in mlp_packs]
    outs += [(shape((8, width), f32), VM), (shape((8, head), f32), VM)]
    return pl.pallas_call(
        functools.partial(forward_kernel, scale),
        out_shape=[o for o, _ in outs],
        in_specs=[VM] * 3 + [ANY] * 5,
        out_specs=[s for _, s in outs],
        scratch_shapes=[
            pltpu.VMEM((rows, width), bf16),
            pltpu.VMEM((rows, 128), f32),
            pltpu.VMEM(weight_a, bf16),
            pltpu.VMEM(weight_b, bf16),
            pltpu.VMEM(weight_out, bf16),
            pltpu.VMEM((rows, cols), bf16),
            pltpu.VMEM((16, rows, cols), bf16),
            pltpu.VMEM((seqs, heads * rows // seqs, 2 * head), f32),
            pltpu.VMEM((8, own_rows, cols), bf16),
            pltpu.VMEM((own_rows, width), bf16),
        ]
        + sems(24 * 12, 24),
        name="forward",
        compiler_params=params(1, 56),
    )(tokens, cosine, sine, *packs, *mlp_packs)


def backward_kernel(
    scale, q_ref, qt_ref, do_ref, dot_ref, lse_ref, delta_ref, kv_ref, dq_ref, dkv_ref, acc_ref
):
    b = lax.axis_index("batch")
    seqs, rows, head = q_ref.shape
    slots, both, _ = kv_ref.shape
    seq_dev = both // seqs
    factor = scale * math.log2(math.e)

    def clear(slot, carry):
        dkv_ref[slot] = jnp.zeros(dkv_ref.shape[1:], dkv_ref.dtype)
        return carry

    lax.fori_loop(b + 1, slots, clear, 0)
    for s in range(seqs):
        at = pl.ds(s * seq_dev, seq_dev)

        def block(slot, masked):
            keys = kv_ref[slot, at, :head]
            values = kv_ref[slot, at, head:]
            scores = jnp.dot(keys, qt_ref[s], preferred_element_type=f32)
            probs = jnp.exp2(scores * factor - lse_ref[s])
            if masked:
                key = lax.broadcasted_iota(jnp.int32, scores.shape, 0)
                col = lax.broadcasted_iota(jnp.int32, scores.shape, 1)
                row = jnp.where(col >= seq_dev, col - seq_dev, col)
                probs = jnp.where(key <= row, probs, 0.0)
            grad_probs = jnp.dot(values, dot_ref[s], preferred_element_type=f32)
            grad_scores = (probs * (grad_probs - delta_ref[s]) * scale).astype(bf16)
            dkv_ref[slot, at, :head] = jnp.dot(
                grad_scores, q_ref[s], preferred_element_type=f32
            ).astype(bf16)
            dkv_ref[slot, at, head:] = jnp.dot(
                probs.astype(bf16), do_ref[s], preferred_element_type=f32
            ).astype(bf16)
            acc_ref[...] += lax.dot_general(
                keys, grad_scores, (((0,), (0,)), ((), ())), preferred_element_type=f32
            )

        acc_ref[...] = jnp.zeros_like(acc_ref)

        def body(slot, carry):
            block(slot, False)
            return carry

        lax.fori_loop(0, b, body, 0)
        block(b, True)
        dq_ref[s] = acc_ref[...].T


def attention_backward(queries, grad_att, lse, delta, kv_all, scale):
    return pl.pallas_call(
        functools.partial(backward_kernel, scale),
        out_shape=[
            jax.ShapeDtypeStruct(queries.shape, f32),
            jax.ShapeDtypeStruct(kv_all.shape, bf16),
        ],
        in_specs=[VM] * 7,
        out_specs=[VM] * 2,
        scratch_shapes=[pltpu.VMEM((queries.shape[2], queries.shape[1]), f32)],
        name="attention_backward",
        compiler_params=pltpu.CompilerParams(vmem_limit_bytes=48 * MIB),
    )(
        queries,
        queries.transpose(0, 2, 1),
        grad_att,
        grad_att.transpose(0, 2, 1),
        lse,
        delta,
        kv_all,
    )


def norm_back(values, gain, grad):
    inverse = lax.rsqrt(jnp.mean(values * values, axis=-1, keepdims=True) + epsilon)
    scaled = grad * gain
    unit = values * inverse
    inner = jnp.mean(scaled * unit, axis=-1, keepdims=True)
    return (scaled - unit * inner) * inverse, grad * unit


def mlp_back_kernel(
    part, resid, grad_final, gain, weight_part, low, grad_resid, gain_grad, weight_grad, *rest
):
    scratch, scratch_w = rest[:4], rest[4:10]
    own, total = rest[10], rest[11]
    copies = Copies(*rest[12:])
    tensor, batch = Group("tensor", False), Group("batch")
    rows = resid.shape[0]
    depth = weight_grad.shape[0]
    enter(near(tensor, batch))

    def along():
        def unit(dr, dq):
            return part.at[pl.ds(pl.multiple_of(tensor.slot(dr, dq) * rows, 16), rows), :]

        yield from reduce(copies, tensor, unit, scratch, grad_resid)
        total[...] = jnp.zeros_like(total)

        def body(i, carry):
            at = rows_at(i)
            back, terms = norm_back(resid[at, :], gain[...], grad_resid[at, :])
            back = grad_final[at, :] + back
            total[...] += terms
            grad_resid[at, :] = back
            own[at, :] = back.astype(bf16)
            return carry

        lax.fori_loop(0, rows // 16, body, 0)
        gain_grad[...] = jnp.sum(total[...], axis=0, keepdims=True)
        yield from gather(
            copies, tensor, own, lambda s: low.at[pl.ds(pl.multiple_of(s * rows, 16), rows), :]
        )

    def weight_unit(dr, dq, dc):
        return weight_part.at[
            pl.ds(pl.multiple_of(batch.slot(dr, dq, dc) * depth, 16), depth), :
        ]

    run_all(reduce(copies, batch, weight_unit, scratch_w, weight_grad), along())


def mlp_back(part, resid, grad_final, gain, weight_part):
    rows, width = resid.shape
    depth, columns = weight_part.shape[0] // 16, weight_part.shape[1]
    return pl.pallas_call(
        mlp_back_kernel,
        out_shape=[
            jax.ShapeDtypeStruct(part.shape, bf16),
            jax.ShapeDtypeStruct(resid.shape, f32),
            jax.ShapeDtypeStruct((1, width), f32),
            jax.ShapeDtypeStruct((depth, columns), f32),
        ],
        in_specs=[VM] * 5,
        out_specs=[ANY, VM, VM, VM],
        scratch_shapes=reduce_scratch(rows, width, False)
        + reduce_scratch(depth, columns, True)
        + [pltpu.VMEM((rows, width), bf16), pltpu.VMEM((16, width), f32)]
        + sems(24 * 3, 1),
        name="mlp_grad_and_weights",
        compiler_params=params(4, 56),
    )(part, resid, grad_final, gain, weight_part)


def output_kernel(part, resid, kv_part, output, kv_grad, *rest):
    scratch, scratch_kv = rest[:4], rest[4:10]
    own, final = rest[10], rest[11]
    copies = Copies(*rest[12:])
    tensor, batch = Group("tensor", False), Group("batch")
    rows = resid.shape[0]
    enter(near(tensor, batch))

    def along():
        def unit(dr, dq):
            return part.at[pl.ds(pl.multiple_of(tensor.slot(dr, dq) * rows, 16), rows), :]

        yield from reduce(copies, tensor, unit, scratch, final)
        add_rows(own, [final, resid])
        yield from gather(
            copies, tensor, own, lambda s: output.at[pl.ds(pl.multiple_of(s * rows, 16), rows), :]
        )

    run_all(
        reduce(
            copies,
            batch,
            lambda dr, dq, dc: kv_part.at[batch.slot(dr, dq, dc)],
            scratch_kv,
            kv_grad,
        ),
        along(),
    )


def output_and_kv(part, resid, kv_part):
    rows, width = resid.shape
    return pl.pallas_call(
        output_kernel,
        out_shape=[
            jax.ShapeDtypeStruct(part.shape, bf16),
            jax.ShapeDtypeStruct(kv_part.shape[1:], f32),
        ],
        in_specs=[VM] * 3,
        out_specs=[ANY, VM],
        scratch_shapes=reduce_scratch(rows, width, False)
        + reduce_scratch(kv_part.shape[1], kv_part.shape[2], True)
        + [pltpu.VMEM((rows, width), bf16), pltpu.VMEM((rows, width), f32)]
        + sems(24 * 3, 1),
        name="output_and_kv_grads",
        compiler_params=params(5, 48),
    )(part, resid, kv_part)


def last_kernel(
    part, inputs, grad_resid, gain, gain_terms, weight_part, tokens, weight_grad, sums, *rest
):
    scratch, scratch_w = rest[:4], rest[4:10]
    own, held, total, mine, over_tensor, mine_too, over_batch = rest[10:17]
    copies = Copies(*rest[17:])
    tensor, batch = Group("tensor", False), Group("batch")
    rows, width = inputs.shape
    depth = weight_grad.shape[0]
    enter(near(tensor, batch))

    def small():
        yield from gather(copies, tensor, mine, lambda s: over_tensor.at[s], False)
        total_t = over_tensor[0]
        for n in range(1, 8):
            total_t = total_t + over_tensor[n]
        mine_too[...] = total_t
        yield from gather(copies, batch, mine_too, lambda s: over_batch.at[s], False)
        total_b = over_batch[0]
        for n in range(1, 16):
            total_b = total_b + over_batch[n]
        sums[...] = total_b

    def along():
        def unit(dr, dq):
            return part.at[pl.ds(pl.multiple_of(tensor.slot(dr, dq) * rows, 16), rows), :]

        yield from reduce(copies, tensor, unit, scratch, held)
        total[...] = jnp.zeros_like(total)

        def body(i, carry):
            at = rows_at(i)
            back, terms = norm_back(inputs[at, :], gain[...], held[at, :])
            total[...] += terms
            own[at, :] = (grad_resid[at, :] + back).astype(bf16)
            return carry

        lax.fori_loop(0, rows // 16, body, 0)
        gain_row = jnp.sum(total[...], axis=0, keepdims=True)
        mine[...] = gain_terms[...]
        for n in range(width // 128):
            mine[pl.ds(n, 1), :] = gain_row[:, n * 128 : (n + 1) * 128]
        big = gather(
            copies, tensor, own, lambda s: tokens.at[pl.ds(pl.multiple_of(s * rows, 16), rows), :]
        )
        few = small()
        for _ in big:
            next(few, None)
            yield
        yield from few

    def weight_unit(dr, dq, dc):
        return weight_part.at[
            pl.ds(pl.multiple_of(batch.slot(dr, dq, dc) * depth, 16), depth), :
        ]

    run_all(reduce(copies, batch, weight_unit, scratch_w, weight_grad), along())


def last_step(part, inputs, grad_resid, gain, gain_terms, weight_part):
    rows, width = inputs.shape
    depth, columns = weight_part.shape[0] // 16, weight_part.shape[1]
    few = gain_terms.shape
    return pl.pallas_call(
        last_kernel,
        out_shape=[
            jax.ShapeDtypeStruct(part.shape, bf16),
            jax.ShapeDtypeStruct((depth, columns), f32),
            jax.ShapeDtypeStruct(few, f32),
        ],
        in_specs=[VM] * 6,
        out_specs=[ANY, VM, VM],
        scratch_shapes=reduce_scratch(rows, width, False)
        + reduce_scratch(depth, columns, True)
        + [
            pltpu.VMEM((rows, width), bf16),
            pltpu.VMEM((rows, width), f32),
            pltpu.VMEM((16, width), f32),
            pltpu.VMEM(few, f32),
            pltpu.VMEM((8,) + few, f32),
            pltpu.VMEM(few, f32),
            pltpu.VMEM((16,) + few, f32),
        ]
        + sems(24 * 5, 3),
        name="input_grad_and_weights",
        compiler_params=params(6, 48),
    )(part, inputs, grad_resid, gain, gain_terms, weight_part)


def rms_scale(values, scales):
    return values * lax.rsqrt(jnp.mean(values * values, axis=-1, keepdims=True) + epsilon) * scales


def rotate(values, cosine, sine):
    half_size = values.shape[-1] // 2
    first = values[..., :half_size]
    second = values[..., half_size:]
    return jnp.concatenate(
        [first * cosine - second * sine, second * cosine + first * sine], axis=-1
    )


def head_prepare(values, scales, cosine, sine):
    head_size = scales.shape[0]
    shaped = values.reshape(values.shape[0], values.shape[1] // head_size, head_size)
    return rotate(rms_scale(shaped, scales), cosine, sine).reshape(values.shape)


def gate_apply(attended, gate_raw):
    return attended * jax.nn.sigmoid(gate_raw)


def swiglu(gate_act, up_act):
    return jax.nn.silu(gate_act) * up_act


def dot(left, right):
    return jnp.dot(left, right, preferred_element_type=f32)


def dot_t(left, right):
    return lax.dot_general(left, right, (((1,), (1,)), ((), ())), preferred_element_type=f32)


def t_dot(left, right):
    return lax.dot_general(left, right, (((0,), (0,)), ((), ())), preferred_element_type=f32)


def shards(
    tokens,
    target,
    domain_ids,
    domain_counts,
    weight_index,
    loss_weights,
    w_query,
    w_key,
    w_value,
    w_gate_out,
    w_output,
    w_gate,
    w_up,
    w_down,
    norm_attn,
    norm_mlp,
    gain_query,
    gain_key,
):
    seq_count, seq_dev, width = tokens.shape
    rows = seq_count * seq_dev
    members = lax.axis_size("tensor")
    batch_count = lax.axis_size("batch")
    b, t = lax.axis_index("batch"), lax.axis_index("tensor")
    own_rows = rows // members
    seq_len = seq_dev * batch_count
    head = gain_query.shape[0] * batch_count
    scale = head ** (-0.5)
    q_cols, k_cols = w_query.shape[1], w_key.shape[1]
    heads = q_cols // head

    gains = jnp.zeros((2, head), bf16)
    gains = lax.dynamic_update_slice(
        gains, jnp.stack([gain_query, gain_key]), (0, b * gain_query.shape[0])
    )
    few = jnp.concatenate(
        [norm_attn[None], norm_mlp[None], gains, jnp.zeros((12, head), bf16)], axis=0
    )
    few = jnp.pad(few, ((0, 0), (0, 2 * k_cols + q_cols - head)))
    packs = (
        jnp.concatenate([jnp.concatenate([w_key, w_value, w_output.T], axis=1), few], axis=0),
        jnp.concatenate([w_query, w_gate_out], axis=1),
    )

    half_size = head // 2
    pos_local = (b * seq_dev + jnp.arange(seq_dev, dtype=jnp.int32)).astype(f32)
    inverse_freq = rope_base ** (-jnp.arange(half_size, dtype=f32) / half_size)
    angles = pos_local[:, None] * inverse_freq[None, :]
    cosine, sine = jnp.cos(angles), jnp.sin(angles)
    cosine_wide = jnp.concatenate([cosine, cosine], axis=1)
    sine_wide = jnp.concatenate([-sine, sine], axis=1)

    tokens_low = tokens.reshape(rows, width)
    ff = w_gate.shape[1]
    (
        normed_low,
        query_raw,
        kv_raw,
        gate_raw,
        queries,
        kv_all,
        attended,
        lse,
        gated_low,
        normed_mlp_low,
        resid_own,
        wide_kvo,
        wide_qg,
        w_out_all,
        wide_gate,
        wide_up,
        wide_down,
        gain_wide,
        gain_head,
    ) = forward(
        tokens_low,
        cosine_wide,
        sine_wide,
        packs,
        (w_gate, w_up, w_down.T),
        scale,
        seq_count,
    )
    key_raw = kv_raw[:, :k_cols]
    gain_attn, gain_mlp = gain_wide[0:1], gain_wide[1:2]
    gain_q, gain_k = gain_head[0], gain_head[1]
    depth = w_gate.shape[0]
    w_kvo = wide_kvo[:, :depth].reshape(width, -1)
    w_qg = wide_qg.reshape(width, -1)
    w_proj = jnp.concatenate([w_qg[:, :q_cols], w_kvo[:, : 2 * k_cols], w_qg[:, q_cols:]], axis=1)
    proj_cols = w_proj.shape[1]
    w_out_t = w_kvo[:, 2 * k_cols :]
    wide_gate, wide_up, wide_down = (w.reshape(width, ff) for w in (wide_gate, wide_up, wide_down))
    row_cosine = jnp.tile(cosine, (seq_count, 1))[:, None, :]
    row_sine = jnp.tile(sine, (seq_count, 1))[:, None, :]
    inputs_own = lax.dynamic_slice_in_dim(tokens_low, t * own_rows, own_rows, 0).astype(f32)

    def prepare(values, scales):
        return head_prepare(values, scales, row_cosine, row_sine)

    def by_head(values):
        shaped = values.reshape(seq_count, seq_dev, heads, head)
        return shaped.transpose(0, 2, 1, 3).reshape(seq_count, heads * seq_dev, head)

    def by_row(values):
        shaped = values.reshape(seq_count, heads, seq_dev, head)
        return shaped.transpose(0, 2, 1, 3).reshape(rows, heads * head)

    domain_range = jnp.arange(domain_counts.shape[0], dtype=jnp.int32)
    level_pick = (
        weight_index[:, None] == jnp.arange(loss_weights.shape[0], dtype=jnp.int32)[None, :]
    ).astype(f32)
    domain_factor = (
        jnp.sum(level_pick * loss_weights[None, :], axis=1) * seq_len / domain_counts.astype(f32)
    )
    seq_pick = (domain_ids[:, None] == domain_range[None, :]).astype(f32)
    seq_weight = jnp.sum(seq_pick * domain_factor[None, :], axis=1)
    row_weight = jnp.repeat(seq_weight, seq_dev)[:, None]
    target_low = target.reshape(rows, width)
    grad_final_low = (target_low.astype(f32) * row_weight).astype(bf16)
    grad_final_own = lax.dynamic_slice_in_dim(target_low, t * own_rows, own_rows, 0).astype(
        f32
    ) * lax.dynamic_slice_in_dim(row_weight, t * own_rows, own_rows, 0)

    gate_act = dot(normed_mlp_low, wide_gate)
    up_act = dot(normed_mlp_low, wide_up)
    hidden_low = swiglu(gate_act, up_act).astype(bf16)
    down_part = dot_t(hidden_low, wide_down).astype(bf16)
    grad_hidden = dot(grad_final_low, wide_down)
    _, swiglu_back = jax.vjp(swiglu, gate_act, up_act)
    grad_gate_act, grad_up_act = swiglu_back(grad_hidden)
    grad_gate_low = grad_gate_act.astype(bf16)
    grad_up_low = grad_up_act.astype(bf16)
    mlp_input_part = (dot_t(grad_gate_low, wide_gate) + dot_t(grad_up_low, wide_up)).astype(bf16)
    mlp_weight_part = jnp.concatenate(
        [
            t_dot(normed_mlp_low, grad_gate_low).astype(bf16),
            t_dot(normed_mlp_low, grad_up_low).astype(bf16),
            t_dot(grad_final_low, hidden_low).astype(bf16),
        ],
        axis=1,
    )
    grad_resid_low, grad_resid_own, norm_mlp_terms, mlp_weight_grad = mlp_back(
        mlp_input_part, resid_own, grad_final_own, gain_mlp, mlp_weight_part
    )

    grad_gated = dot(grad_resid_low, w_out_t)
    _, gate_back = jax.vjp(gate_apply, attended, gate_raw)
    grad_attended, grad_gate_raw = gate_back(grad_gated)
    grad_att_low = grad_attended.astype(bf16)
    grad_gate_raw_low = grad_gate_raw.astype(bf16)
    grad_att_heads = by_head(grad_att_low)
    delta = jnp.sum(grad_att_heads.astype(f32) * by_head(attended), axis=-1)[:, None, :]
    grad_query_heads, kv_part = attention_backward(
        queries, grad_att_heads, lse, delta, kv_all, scale
    )
    output, kv_grad = output_and_kv(down_part, resid_own, kv_part)

    _, query_back = jax.vjp(prepare, query_raw, gain_q)
    query_pre, grad_gain_q = query_back(by_row(grad_query_heads))
    _, key_back = jax.vjp(prepare, key_raw, gain_k)
    key_pre, grad_gain_k = key_back(kv_grad[:, :k_cols])
    proj_grad_low = jnp.concatenate(
        [
            query_pre.astype(bf16),
            key_pre.astype(bf16),
            kv_grad[:, k_cols:].astype(bf16),
            grad_gate_raw_low,
        ],
        axis=1,
    )
    attn_input_part = dot_t(proj_grad_low, w_proj).astype(bf16)
    attn_weight_part = jnp.concatenate(
        [
            t_dot(normed_low, proj_grad_low).astype(bf16),
            t_dot(grad_resid_low, gated_low).astype(bf16),
        ],
        axis=1,
    )
    norm_rows = width // 128
    gain_terms = jnp.zeros((2 * norm_rows + 8, 128), f32)
    gain_terms = gain_terms.at[norm_rows : 2 * norm_rows].set(norm_mlp_terms.reshape(norm_rows, 128))
    gain_terms = gain_terms.at[2 * norm_rows].set(grad_gain_q)
    gain_terms = gain_terms.at[2 * norm_rows + 1].set(grad_gain_k)
    grad_tokens, attn_weight_grad, sums_all = last_step(
        attn_input_part, inputs_own, grad_resid_own, gain_attn, gain_terms, attn_weight_part
    )

    def own_part(flat, like):
        return lax.dynamic_slice_in_dim(flat, b * like.shape[0], like.shape[0], 0)

    pieces = [0, q_cols, q_cols + k_cols, q_cols + 2 * k_cols, proj_cols, proj_cols + q_cols]
    grads = [attn_weight_grad[:, lo:hi] for lo, hi in zip(pieces[:-1], pieces[1:])]
    return (
        output.reshape(tokens.shape),
        grad_tokens.astype(f32).reshape(tokens.shape),
        grads[0],
        grads[1],
        grads[2],
        grads[3],
        grads[4].T,
        mlp_weight_grad[:, :ff],
        mlp_weight_grad[:, ff : 2 * ff],
        mlp_weight_grad[:, 2 * ff :].T,
        own_part(sums_all[:norm_rows].reshape(-1), norm_attn),
        own_part(sums_all[norm_rows : 2 * norm_rows].reshape(-1), norm_mlp),
        own_part(sums_all[2 * norm_rows], gain_query),
        own_part(sums_all[2 * norm_rows + 1], gain_key),
    )


def solution(mesh):
    in_specs = (
        P(None, "batch", None),
        P(None, "batch", None),
        P(),
        P(),
        P(),
        P(),
        P("batch", "tensor"),
        P("batch", "tensor"),
        P("batch", "tensor"),
        P("batch", "tensor"),
        P("tensor", "batch"),
        P("batch", "tensor"),
        P("batch", "tensor"),
        P("tensor", "batch"),
        P("batch"),
        P("batch"),
        P("batch"),
        P("batch"),
    )
    out_specs = (
        P(None, "batch", None),
        P(None, "batch", None),
        P("batch", "tensor"),
        P("batch", "tensor"),
        P("batch", "tensor"),
        P("batch", "tensor"),
        P("tensor", "batch"),
        P("batch", "tensor"),
        P("batch", "tensor"),
        P("tensor", "batch"),
        P("batch"),
        P("batch"),
        P("batch"),
        P("batch"),
    )
    return jax.shard_map(shards, mesh=mesh, in_specs=in_specs, out_specs=out_specs, check_vma=False)
```

```python
import functools
import itertools
import math

import jax
import jax.numpy as jnp
from jax import lax
from jax.experimental import pallas as pl
from jax.experimental.pallas import tpu as pltpu
from jax.sharding import PartitionSpec as P

MESH = pl.DeviceIdType.MESH
epsilon = 1e-06
rope_base = 1000000.0
f32 = jnp.float32
bf16 = jnp.bfloat16
MIB = 2**20
ANY = pl.BlockSpec(memory_space=pl.ANY)
VM = pl.BlockSpec(memory_space=pltpu.VMEM)


class Group:
    def __init__(self, kind, core=True):
        b = lax.axis_index("batch")
        t = lax.axis_index("tensor")
        c = lax.rem(b, 2)
        self.c, self.t = c, t
        if kind == "tensor":
            r, q = lax.div(t, 2), lax.rem(t, 2)
            self.slot = lambda dr, dq: lax.rem(r + dr, 4) * 2 + lax.rem(q + dq, 2)
            at = lambda dr, dq: (b, self.slot(dr, dq))
        else:
            q, r = lax.div(b, 8), lax.rem(lax.div(b, 2), 4)
            self.chip = lambda dr, dq: lax.rem(q + dq, 2) * 4 + lax.rem(r + dr, 4)
            self.slot = lambda dr, dq, dc=0: self.chip(dr, dq) * 2 + lax.rem(c + dc, 2)
            at = lambda dr, dq: (self.slot(dr, dq), t)
        self.core = (b + 1 - 2 * c, t) if core else None
        self.right, self.left, self.mate = at(1, 0), at(3, 0), at(0, 1)
        self.others = [at(dr, dq) for dr in range(4) for dq in range(2) if dr or dq]
        self.steps = [(dr, dq) for dr in range(4) for dq in range(2) if dr or dq]


def enter(devices):
    barrier = pltpu.get_barrier_semaphore()
    for device in devices:
        pl.semaphore_signal(barrier, inc=1, device_id=device, device_id_type=MESH)
    pl.semaphore_wait(barrier, len(devices))


def near(*groups):
    devices = [d for g in groups for d in (g.right, g.left, g.mate)]
    cores = [g.core for g in groups if g.core is not None]
    return devices + cores[:1]


class Copies:
    def __init__(self, send_sem, recv_sem, local_sem):
        self.send_sem, self.recv_sem, self.local_sem = send_sem, recv_sem, local_sem
        self.count = 0
        self.locals = 0

    def send(self, source, target, device):
        copy = pltpu.make_async_remote_copy(
            src_ref=source,
            dst_ref=target,
            send_sem=self.send_sem.at[self.count],
            recv_sem=self.recv_sem.at[self.count],
            device_id=device,
            device_id_type=MESH,
        )
        self.count += 1
        copy.start()
        return copy

    def local(self, source, target):
        copy = pltpu.make_async_copy(source, target, self.local_sem.at[self.locals])
        self.locals += 1
        copy.start()
        return copy


def half_of(ref, which):
    width = ref.shape[-1] // 2
    lead = (slice(None),) * (len(ref.shape) - 1)
    return ref.at[lead + (pl.ds(which * width, width),)]


def run_all(*steps):
    waiting = list(steps)
    while waiting:
        for step in list(waiting):
            try:
                next(step)
            except StopIteration:
                waiting.remove(step)


def gather(copies, group, own, slot, split=True, source=None):
    s = group.slot
    core_copies = []
    sent = []

    def push(ref, *devices):
        out = [copies.send(ref, ref, device) for device in devices]
        sent.extend(out)
        return out

    def to_core(ref):
        if group.core is not None:
            core_copies.extend(push(ref, group.core))

    def core_wait(count):
        for copy in core_copies[:count]:
            copy.wait_recv()
        del core_copies[:count]

    home = slot(s(0, 0))
    source = own if source is None else source
    first = [copies.send(source, home, d) for d in (group.right, group.left, group.mate)]
    sent.extend(first)
    kept = None
    if own is not None:
        kept = copies.local(own, home)
        if group.core is not None:
            core_copies.append(copies.send(own, home, group.core))
            sent.append(core_copies[0])
    from_left, from_right, from_mate = first
    yield []
    from_left.wait_recv()
    left_unit = slot(s(3, 0))
    far = push(half_of(left_unit, 0) if split else left_unit, group.right)
    to_core(left_unit)
    from_right.wait_recv()
    right_unit = slot(s(1, 0))
    if split:
        far += push(half_of(right_unit, 1), group.left)
    to_core(right_unit)
    from_mate.wait_recv()
    mate_unit = slot(s(0, 1))
    mate_left, mate_right = push(mate_unit, group.right, group.left)
    to_core(mate_unit)
    if own is not None:
        core_wait(1)
        kept.wait()
    yield [(0, 0)]
    for copy in far:
        copy.wait_recv()
    far_unit = slot(s(2, 0))
    (mate_far,) = push(far_unit, group.mate)
    to_core(far_unit)
    yield []
    mate_left.wait_recv()
    to_core(slot(s(3, 1)))
    mate_right.wait_recv()
    to_core(slot(s(1, 1)))
    core_wait(3)
    yield [(3, 0), (1, 0), (0, 1)]
    mate_far.wait_recv()
    to_core(slot(s(2, 1)))
    core_wait(3)
    yield [(2, 0), (3, 1), (1, 1)]
    core_wait(1)
    yield [(2, 1)]
    for copy in sent:
        copy.wait_send()


def add_rows(target, sources, step=16):
    def body(at):
        total = sources[0][at, :].astype(f32)
        for source in sources[1:]:
            total = total + source[at, :].astype(f32)
        target[at, :] = total.astype(target.dtype)

    each_rows(target.shape[0], step, body)


def rows_at(i, step=16):
    return pl.ds(pl.multiple_of(i * step, step), step)


def each_rows(rows, step, body):
    def run(i, carry):
        body(rows_at(i, step))
        return carry

    lax.fori_loop(0, rows // step, run, 0)


def reduce_scratch(rows, width, core):
    shapes = [
        pltpu.VMEM((2, rows, width // 2), bf16),
        pltpu.VMEM((4, rows, width), bf16),
        pltpu.VMEM((4 if core else 2, rows, width), bf16),
        pltpu.VMEM((3, rows, width), bf16),
        pltpu.VMEM((2 if core else 1, rows, width), bf16),
    ]
    if core:
        shapes += [pltpu.VMEM((8, rows, width), bf16)]
    return shapes


ORDER = [(2, 1), (1, 1), (3, 1), (2, 0), (1, 0), (3, 0), (0, 1), (0, 0)]


def reduce(copies, group, part, scratch, result, early=False):
    far, near_in, outgoing, mates, far_sums = scratch[:5]
    core = group.core is not None
    sent = []

    def send(source, target, device):
        copy = copies.send(source, target, device)
        sent.append(copy)
        return copy

    arrived = {}

    def to_core(n):
        dr, dq = ORDER[n]
        arrived[dr, dq] = (send(part(dr, dq, 1), scratch[5].at[n], group.core), n)

    def terms(dr, dq):
        if not core:
            return [part(dr, dq)]
        copy, n = arrived[dr, dq]
        copy.wait_recv()
        return [part(dr, dq, 0), scratch[5].at[n]]

    def first():
        unit = terms(2, 1)
        if core:
            add_rows(far_sums.at[1], unit)
            unit = [far_sums.at[1]]
        copy = send(unit[0], mates.at[2], group.mate)
        others = []
        for way, (dr, device) in enumerate(((1, group.right), (3, group.left))):
            unit = terms(dr, 1)
            if core:
                add_rows(outgoing.at[2 + way], unit)
                unit = [outgoing.at[2 + way]]
            others.append(send(unit[0], near_in.at[2 + way], device))
        return copy, others

    def second():
        unit = terms(2, 0)
        far_mate.wait_recv()
        add_rows(far_sums.at[0], unit + [mates.at[2]])
        return [
            send(half_of(far_sums.at[0], way), far.at[way], device)
            for way, device in enumerate((group.right, group.left))
        ]

    def third():
        out = []
        for way, (dr, device) in enumerate(((1, group.right), (3, group.left))):
            unit = terms(dr, 0)
            far_copies[way].wait_recv()
            held = outgoing.at[way]
            add_rows(half_of(held, way), [half_of(u, way) for u in unit] + [far.at[way]])
            add_rows(half_of(held, 1 - way), [half_of(u, 1 - way) for u in unit])
            out.append(send(held, near_in.at[way], device))
        return out

    if early:
        for n in range(3):
            to_core(n)
            yield
        to_core(3)
        far_mate, mate_line = first()
        yield
        to_core(4)
        far_copies = second()
        yield
        to_core(5)
        yield
        to_core(6)
        own_line = third()
        yield
        to_core(7)
    else:
        if core:
            for n in range(8):
                to_core(n)
            yield
        far_mate, mate_line = first()
        yield
        far_copies = second()
        yield
        own_line = third()
    yield
    unit = terms(0, 1)
    for copy in mate_line:
        copy.wait_recv()
    add_rows(mates.at[0], unit + [near_in.at[2], near_in.at[3]])
    to_mate = send(mates.at[0], mates.at[1], group.mate)
    yield
    unit = terms(0, 0)
    for copy in own_line:
        copy.wait_recv()
    to_mate.wait_recv()
    add_rows(result, unit + [near_in.at[0], near_in.at[1], mates.at[1]])
    for copy in sent:
        copy.wait_send()


def sems(remote, local):
    return [
        pltpu.SemaphoreType.DMA((remote,)),
        pltpu.SemaphoreType.DMA((remote,)),
        pltpu.SemaphoreType.DMA((max(local, 1),)),
    ]


def params(collective, limit=48):
    return pltpu.CompilerParams(
        collective_id=collective, has_side_effects=True, vmem_limit_bytes=limit * MIB
    )


def prepare_head(values, gain, cosine, sine):
    half_size = values.shape[1] // 2
    mean = jnp.mean(values * values, axis=-1, keepdims=True)
    scaled = values * lax.rsqrt(mean + epsilon) * gain
    return scaled * cosine + pltpu.roll(scaled, half_size, 1) * sine


def forward_kernel(
    scale,
    tokens,
    cosine,
    sine,
    pack_a,
    pack_b,
    mlp_a,
    mlp_b,
    mlp_c,
    normed_out,
    query_raw,
    kv_raw,
    gate_raw,
    queries,
    kv_out,
    attended,
    lse,
    gated,
    normed_mlp,
    resid,
    wide_kvo,
    wide_qg,
    w_out_out,
    wide_a,
    wide_b,
    wide_c,
    gain_wide,
    gain_head,
    normed,
    inverse,
    w_kvo,
    w_qg,
    w_out,
    kv_own,
    kv_all,
    acc,
    rows_all,
    own,
    send_sem,
    recv_sem,
    local_sem,
):
    copies = Copies(send_sem, recv_sem, local_sem)
    tensor, batch = Group("tensor"), Group("batch")
    b = lax.axis_index("batch")
    rows, width = tokens.shape
    cols = query_raw.shape[1]
    own_rows = resid.shape[0]
    seqs, head_rows, head = queries.shape
    heads = query_raw.shape[1] // head
    seq_dev = rows // seqs
    enter(tensor.others + near(batch))

    def batch_gather(source, target, split=True):
        return gather(copies, batch, source, lambda s: target.at[s], split)

    a_steps = batch_gather(pack_a, w_kvo)
    b_steps = batch_gather(pack_b, w_qg)
    next(a_steps)
    next(b_steps)

    def invert(at):
        values = tokens[at, :].astype(f32)
        mean = jnp.mean(values * values, axis=-1, keepdims=True)
        inverse[at, :] = jnp.broadcast_to(lax.rsqrt(mean + epsilon), (16, 128))

    each_rows(rows, 16, invert)
    next(a_steps)
    next(b_steps)
    for _ in a_steps:
        pass
    depth = pack_b.shape[0]
    half = tensor.c * 8
    kept = [copies.local(w_kvo, wide_kvo)]
    out_home = copies.local(w_kvo.at[:, pl.ds(0, depth), pl.ds(cols, cols)], w_out.at[tensor.t])
    wide_out_steps = gather(
        copies,
        tensor,
        None,
        lambda s: w_out.at[s, pl.ds(half, 8)],
        source=w_kvo.at[pl.ds(half, 8), pl.ds(0, depth), pl.ds(cols, cols)],
    )
    next(wide_out_steps)
    gain_wide[...] = jnp.zeros_like(gain_wide)
    gain_head[...] = jnp.zeros_like(gain_head)
    total = jnp.zeros((16, 128), f32)
    for n in range(16):
        entry = w_kvo[n, depth:, 0:128].astype(f32)
        gain_wide[0:2, n * 128 : (n + 1) * 128] = entry[0:2]
        total = total + entry
    gain_head[0:2, :] = total[2:4]

    def normalise(at):
        scaled = tokens[at, :].astype(f32) * inverse[at, 0:1] * gain_wide[0:1, :]
        normed[at, :] = scaled.astype(bf16)

    each_rows(rows, 16, normalise)
    kept.append(copies.local(normed, normed_out))

    def project(weights, at):
        return jnp.dot(normed[at, :], weights.reshape(width, cols), preferred_element_type=f32)

    for s in range(seqs):
        at = pl.ds(s * seq_dev, seq_dev)
        raw = project(w_kvo[:, 0:depth, 0:cols], at)
        kv_raw[at, :] = raw
        key = prepare_head(raw[:, :head], gain_head[1:2, :], cosine[...], sine[...])
        kv_own[at, :head] = key.astype(bf16)
        kv_own[at, head:] = raw[:, head:].astype(bf16)
    all_steps = batch_gather(kv_own, kv_all)
    next(all_steps)
    for _ in b_steps:
        pass
    kept.append(copies.local(w_qg, wide_qg))
    for s in range(seqs):
        at = pl.ds(s * seq_dev, seq_dev)
        raw = project(w_qg[:, :, 0:cols], at)
        query_raw[at, :] = raw
        for h in range(heads):
            values = prepare_head(
                raw[:, h * head : (h + 1) * head], gain_head[0:1, :], cosine[...], sine[...]
            )
            queries[s, h * seq_dev : (h + 1) * seq_dev, :] = values.astype(bf16)
        gate_raw[at, :] = project(w_qg[:, :, cols:], at)

    factor = scale * math.log2(math.e)
    ones = jnp.ones((2 * seq_dev, head), bf16)
    tile = head_rows // 4
    acc[...] = jnp.zeros_like(acc)

    def block(pair, masked):
        def body(s, carry):
            at = rows_at(s, seq_dev)
            keys = jnp.concatenate(
                [kv_all[pair * 2, at, :head], kv_all[pair * 2 + 1, at, :head]], axis=0
            )
            values = jnp.concatenate(
                [kv_all[pair * 2, at, head:], kv_all[pair * 2 + 1, at, head:]], axis=0
            )
            wide = jnp.concatenate([values, ones], axis=1)
            for i in range(4):
                here = pl.ds(i * tile, tile)
                scores = lax.dot_general(
                    queries[s, here, :], keys, (((1,), (1,)), ((), ())), preferred_element_type=f32
                )
                weights = jnp.exp2(scores * factor)
                if masked:
                    row = lax.broadcasted_iota(jnp.int32, scores.shape, 0) + (i * tile) % seq_dev
                    col = lax.broadcasted_iota(jnp.int32, scores.shape, 1)
                    ahead = (pair * 2 - b) * seq_dev
                    weights = jnp.where(col + ahead <= row, weights, 0.0)
                acc[s, here, :] += jnp.dot(weights.astype(bf16), wide, preferred_element_type=f32)
            return carry

        lax.fori_loop(0, seqs, body, 0)

    here = batch.chip(0, 0)

    def attend(ready):
        for dr, dq in ready:
            if (dr, dq) == (0, 0):
                block(here, True)
            else:
                pair = batch.chip(dr, dq)

                @pl.when(pair < here)
                def _():
                    block(pair, False)

    mlp_steps = [
        batch_gather(mlp_a, wide_a),
        batch_gather(mlp_b, wide_b),
        batch_gather(mlp_c, wide_c),
    ]
    attend(next(all_steps))
    next(wide_out_steps)
    attend(next(all_steps))
    next(wide_out_steps)
    ready = next(all_steps)
    for step in mlp_steps:
        next(step)
    attend(ready)
    ready = next(all_steps)
    next(wide_out_steps)
    attend(ready)
    attend(next(all_steps))
    for _ in all_steps:
        pass
    kept.append(copies.local(kv_all, kv_out))
    for s in range(seqs):
        sums = acc[s, :, head:]
        lse[s] = jnp.log2(sums).T[0:1, :]
        out = acc[s, :, :head] / sums
        for h in range(heads):
            at, cols = pl.ds(s * seq_dev, seq_dev), pl.ds(h * head, head)
            part = out[h * seq_dev : (h + 1) * seq_dev]
            attended[at, cols] = part
            gated[at, cols] = (part * jax.nn.sigmoid(gate_raw[at, cols])).astype(bf16)

    def unit_rows(ref, slot):
        return ref.at[pl.ds(pl.multiple_of(slot * own_rows, 16), own_rows), :]

    exchanged = [
        copies.send(unit_rows(gated, tensor.slot(*step)), rows_all.at[tensor.t], device)
        for step, device in zip(tensor.steps, tensor.others)
    ]
    rows_all[tensor.t] = unit_rows(gated, tensor.t)[...]
    run_all(wide_out_steps, *[itertools.islice(step, 1) for step in mlp_steps])
    out_home.wait()
    kept.append(copies.local(w_out, w_out_out))
    for copy in exchanged:
        copy.wait_recv()
    resid[...] = unit_rows(tokens, tensor.t)[...].astype(f32)

    def out_term(n, carry):
        resid[...] += lax.dot_general(
            rows_all[n],
            w_out[n].reshape(width, -1),
            (((1,), (1,)), ((), ())),
            preferred_element_type=f32,
        )
        return carry

    lax.fori_loop(0, 8, out_term, 0)

    def normalise_own(at):
        values = resid[at, :]
        mean = jnp.mean(values * values, axis=-1, keepdims=True)
        own[at, :] = (values * lax.rsqrt(mean + epsilon) * gain_wide[1:2, :]).astype(bf16)

    each_rows(own_rows, 16, normalise_own)
    tensor.core = None
    own_steps = gather(copies, tensor, own, lambda s: unit_rows(normed_mlp, s))
    run_all(own_steps, *mlp_steps)
    for copy in exchanged:
        copy.wait_send()
    for copy in kept:
        copy.wait()


def forward(tokens, cosine, sine, packs, mlp_packs, scale, seqs):
    rows, width = tokens.shape
    cols = packs[1].shape[1] // 2
    head = cosine.shape[1]
    own_rows = rows // 8
    heads = cols // head
    shape = jax.ShapeDtypeStruct
    weight_a, weight_b = (16,) + packs[0].shape, (16,) + packs[1].shape
    weight_out = (8, 16, packs[1].shape[0], cols)
    outs = [
        (shape((rows, width), bf16), ANY),
        (shape((rows, cols), f32), VM),
        (shape((rows, cols), f32), VM),
        (shape((rows, cols), f32), VM),
        (shape((seqs, heads * rows // seqs, head), bf16), VM),
        (shape((16, rows, cols), bf16), ANY),
        (shape((rows, cols), f32), VM),
        (shape((seqs, 1, heads * rows // seqs), f32), VM),
        (shape((rows, cols), bf16), VM),
        (shape((rows, width), bf16), ANY),
        (shape((own_rows, width), f32), VM),
        (shape(weight_a, bf16), ANY),
        (shape(weight_b, bf16), ANY),
        (shape(weight_out, bf16), ANY),
    ]
    outs += [(shape((16,) + p.shape, bf16), ANY) for p in mlp_packs]
    outs += [(shape((8, width), f32), VM), (shape((8, head), f32), VM)]
    return pl.pallas_call(
        functools.partial(forward_kernel, scale),
        out_shape=[o for o, _ in outs],
        in_specs=[VM] * 3 + [ANY] * 5,
        out_specs=[s for _, s in outs],
        scratch_shapes=[
            pltpu.VMEM((rows, width), bf16),
            pltpu.VMEM((rows, 128), f32),
            pltpu.VMEM(weight_a, bf16),
            pltpu.VMEM(weight_b, bf16),
            pltpu.VMEM(weight_out, bf16),
            pltpu.VMEM((rows, cols), bf16),
            pltpu.VMEM((16, rows, cols), bf16),
            pltpu.VMEM((seqs, heads * rows // seqs, 2 * head), f32),
            pltpu.VMEM((8, own_rows, cols), bf16),
            pltpu.VMEM((own_rows, width), bf16),
        ]
        + sems(24 * 12, 24),
        name="forward",
        compiler_params=params(1, 56),
    )(tokens, cosine, sine, *packs, *mlp_packs)


def dot(left, right):
    return jnp.dot(left, right, preferred_element_type=f32)


def dot_t(left, right):
    return lax.dot_general(left, right, (((1,), (1,)), ((), ())), preferred_element_type=f32)


def t_dot(left, right):
    return lax.dot_general(left, right, (((0,), (0,)), ((), ())), preferred_element_type=f32)


def norm_back(values, gain, grad):
    inverse = lax.rsqrt(jnp.mean(values * values, axis=-1, keepdims=True) + epsilon)
    scaled = grad * gain
    unit = values * inverse
    inner = jnp.mean(scaled * unit, axis=-1, keepdims=True)
    return (scaled - unit * inner) * inverse, grad * unit


def unit_rows(ref, slot, rows):
    return ref.at[pl.ds(pl.multiple_of(slot * rows, 16), rows), :]


def row_unit(group, ref, rows):
    def unit(*step):
        return unit_rows(ref, group.slot(*step), rows)

    return unit


def outer(left, right, target, cols, step=512):
    def body(i, carry):
        at = rows_at(i, step)
        target[at, cols] = t_dot(left[:, at], right[...]).astype(target.dtype)
        return carry

    lax.fori_loop(0, left.shape[1] // step, body, 0)


def mlp_kernel(
    resid,
    grad_final,
    gain,
    normed_in,
    low_in,
    gate_in,
    up_in,
    down_in,
    out_in,
    down_out,
    up_part_out,
    down_part_out,
    gate_grad,
    grad_resid,
    grad_gated,
    gain_grad,
    normed,
    low,
    w_gate,
    w_up,
    w_down,
    w_out,
    hidden,
    grad_gate,
    grad_up,
    part,
    down,
    gate_part,
    up_part,
    down_part,
    own,
    total,
    units,
    gated_in,
    *rest,
):
    scratch_a, scratch_b, scratch_w = rest[:5], rest[5:10], rest[10:16]
    copies = Copies(*rest[16:])
    tensor, batch = Group("tensor", False), Group("batch")
    rows, width = normed.shape
    own_rows = resid.shape[0]
    ff = hidden.shape[1]
    half = width // 2
    depth = gate_grad.shape[0]
    loads = [
        copies.local(a, b)
        for a, b in (
            (normed_in, normed),
            (gate_in, w_gate),
            (up_in, w_up),
            (low_in, low),
            (down_in, w_down),
            (out_in, w_out),
        )
    ]
    enter(tensor.others + near(batch))
    for load in loads[:5]:
        load.wait()

    def activate(j, carry):
        cols = rows_at(j, 256)
        gate = dot(normed[...], w_gate[:, cols])
        up = dot(normed[...], w_up[:, cols])
        back = dot(low[...], w_down[:, cols])
        sigma = jax.nn.sigmoid(gate)
        silu = gate * sigma
        hidden[:, cols] = (silu * up).astype(bf16)
        grad_up[:, cols] = (back * silu).astype(bf16)
        grad_gate[:, cols] = (back * up * (sigma * (1.0 + gate * (1.0 - sigma)))).astype(bf16)
        return carry

    lax.fori_loop(0, ff // 256, activate, 0)

    def input_part(j, carry):
        cols = rows_at(j, 512)
        value = dot_t(grad_gate[...], w_gate[cols, :]) + dot_t(grad_up[...], w_up[cols, :])
        part[:, cols] = value.astype(bf16)
        return carry

    steps = []
    for n, scratch in enumerate((scratch_a, scratch_b)):
        lax.fori_loop(n * half // 512, (n + 1) * half // 512, input_part, 0)
        cols = pl.ds(n * half, half)
        steps.append(
            reduce(
                copies,
                tensor,
                row_unit(tensor, part.at[:, cols], own_rows),
                scratch,
                grad_resid.at[:, cols],
            )
        )
        next(steps[n])
    outer(normed, grad_gate, gate_part, slice(None))
    weight_steps = reduce(
        copies, batch, row_unit(batch, gate_part, depth), scratch_w, gate_grad
    )
    next(weight_steps)
    next(steps[0])
    next(steps[1])
    outer(normed, grad_up, up_part, slice(None))
    next(steps[0])
    next(steps[1])
    next(weight_steps)
    outer(low, hidden, down_part, slice(None))
    next(steps[0])
    next(steps[1])
    next(weight_steps)

    def down_cols(j, carry):
        cols = rows_at(j, 512)
        down[:, cols] = dot_t(hidden[...], w_down[cols, :]).astype(bf16)
        return carry

    lax.fori_loop(0, width // 512, down_cols, 0)
    kept = [
        copies.local(up_part, up_part_out),
        copies.local(down_part, down_part_out),
        copies.local(down, down_out),
    ]
    run_all(*steps)
    next(weight_steps)
    total[...] = jnp.zeros_like(total)

    def body(at):
        back, terms = norm_back(resid[at, :], gain[...], grad_resid[at, :])
        back = grad_final[at, :] + back
        total[...] += terms
        grad_resid[at, :] = back
        own[at, :] = back.astype(bf16)

    each_rows(own_rows, 16, body)
    gain_grad[...] = jnp.sum(total[...], axis=0, keepdims=True)
    loads[5].wait()

    def gated_unit(n, carry):
        units[n] = dot(own[...], w_out[n].reshape(width, -1)).astype(bf16)
        return carry

    lax.fori_loop(0, 8, gated_unit, 0)
    exchanged = [
        copies.send(units.at[tensor.slot(*step)], gated_in.at[tensor.t], device)
        for step, device in zip(tensor.steps, tensor.others)
    ]
    gated_in[tensor.t] = units[tensor.t]
    for _ in weight_steps:
        pass
    for copy in exchanged:
        copy.wait_recv()
    for n in range(8):
        grad_gated[n * own_rows : (n + 1) * own_rows, :] = gated_in[n]
    for copy in exchanged:
        copy.wait_send()
    for copy in kept:
        copy.wait()


def mlp(resid, grad_final, gain, normed, low, weights, w_out):
    own_rows, width = resid.shape
    rows = normed.shape[0]
    ff = weights[0].shape[1]
    cols = w_out.shape[3]
    depth = width // 16
    shape = jax.ShapeDtypeStruct
    return pl.pallas_call(
        mlp_kernel,
        out_shape=[
            shape((rows, width), bf16),
            shape((width, ff), bf16),
            shape((width, ff), bf16),
            shape((depth, ff), f32),
            shape((own_rows, width), f32),
            shape((rows, cols), bf16),
            shape((1, width), f32),
        ],
        in_specs=[VM] * 3 + [ANY] * 6,
        out_specs=[ANY] * 3 + [VM] * 4,
        scratch_shapes=[pltpu.VMEM((rows, width), bf16)] * 2
        + [pltpu.VMEM((width, ff), bf16)] * 3
        + [pltpu.VMEM(w_out.shape, bf16)]
        + [pltpu.VMEM((rows, ff), bf16)] * 3
        + [pltpu.VMEM((rows, width), bf16)] * 2
        + [pltpu.VMEM((width, ff), bf16)] * 3
        + [
            pltpu.VMEM((own_rows, width), bf16),
            pltpu.VMEM((16, width), f32),
            pltpu.VMEM((8, own_rows, cols), bf16),
            pltpu.VMEM((8, own_rows, cols), bf16),
        ]
        + reduce_scratch(own_rows, width // 2, False) * 2
        + reduce_scratch(depth, ff, True)
        + sems(64, 12),
        name="mlp",
        compiler_params=params(2, 62),
    )(resid, grad_final, gain, normed, low, *weights, w_out)


def attention_kernel(
    scale,
    queries,
    lse,
    attended,
    gate_raw,
    grad_gated,
    grad_resid,
    resid,
    kv_in,
    down_in,
    up_in,
    grad_query,
    kv_grad,
    gate_grad,
    low,
    final,
    up_grad,
    kv_all,
    down,
    up_part,
    own,
    grad_att,
    query_t,
    grad_t,
    delta,
    acc,
    dkv,
    down_sum,
    *rest,
):
    scratch_kv, scratch_d, scratch_w = rest[:6], rest[6:11], rest[11:17]
    copies = Copies(*rest[17:])
    tensor, batch = Group("tensor", False), Group("batch")
    b = lax.axis_index("batch")
    seqs, head_rows, head = queries.shape
    rows, cols = attended.shape
    seq_dev = rows // seqs
    heads = cols // head
    own_rows, width = resid.shape
    depth = up_grad.shape[0]
    factor = scale * math.log2(math.e)
    loads = [copies.local(a, c) for a, c in ((up_in, up_part), (down_in, down), (kv_in, kv_all))]
    enter(near(tensor, batch))

    def round_own(at):
        own[at, :] = grad_resid[at, :].astype(bf16)

    each_rows(own_rows, 16, round_own)
    low_steps = gather(copies, tensor, own, lambda s: unit_rows(low, s, own_rows))
    next(low_steps)
    loads[0].wait()
    up_steps = reduce(copies, batch, row_unit(batch, up_part, depth), scratch_w, up_grad)
    next(up_steps)
    for s in range(seqs):
        at = pl.ds(s * seq_dev, seq_dev)
        for h in range(heads):
            here, there = pl.ds(h * head, head), pl.ds(h * seq_dev, seq_dev)
            sigma = jax.nn.sigmoid(gate_raw[at, here])
            value = grad_gated[at, here].astype(f32)
            out = attended[at, here]
            low_grad = (value * sigma).astype(bf16)
            grad_att[s, there, :] = low_grad
            gate_grad[at, here] = (value * out * (sigma * (1.0 - sigma))).astype(bf16)
            acc[s, there, :] = low_grad.astype(f32) * out
        delta[s] = jnp.sum(acc[s].T, axis=0, keepdims=True)
        grad_t[s] = grad_att[s].astype(f32).T.astype(bf16)
        query_t[s] = queries[s].astype(f32).T.astype(bf16)
    dq = [jnp.zeros((head, head_rows), f32)] * seqs
    for s in range(seqs):
        acc_t = acc.at[s]
        acc_t[...] = jnp.zeros_like(acc_t)
    loads[1].wait()
    loads[2].wait()

    def block(slot, masked):
        for s in range(seqs):
            at = pl.ds(s * seq_dev, seq_dev)
            keys = kv_all[slot, at, :head]
            values = kv_all[slot, at, head:]
            probs = jnp.exp2(dot(keys, query_t[s]) * factor - lse[s])
            if masked:
                key = lax.broadcasted_iota(jnp.int32, probs.shape, 0)
                col = lax.broadcasted_iota(jnp.int32, probs.shape, 1)
                row = jnp.where(col >= seq_dev, col - seq_dev, col)
                probs = jnp.where(key <= row, probs, 0.0)
            grad_probs = dot(values, grad_t[s])
            grad_scores = (probs * (grad_probs - delta[s]) * scale).astype(bf16)
            dkv[slot, at, :head] = dot(grad_scores, queries[s]).astype(bf16)
            dkv[slot, at, head:] = dot(probs.astype(bf16), grad_att[s]).astype(bf16)
            acc[s] += t_dot(grad_scores, keys)

    def pair(chip, own_pair):
        def one(n, carry):
            slot = chip * 2 + n

            @pl.when(slot < b)
            def _():
                block(slot, False)

            if own_pair:

                @pl.when(slot == b)
                def _():
                    block(slot, True)

            @pl.when(slot > b)
            def _():
                dkv[slot] = jnp.zeros(dkv.shape[1:], bf16)

            return carry

        lax.fori_loop(0, 2, one, 0)

    kv_steps = reduce(
        copies,
        batch,
        lambda dr, dq, dc: dkv.at[batch.slot(dr, dq, dc)],
        scratch_kv,
        kv_grad,
        early=True,
    )
    down_steps = reduce(
        copies, tensor, row_unit(tensor, down, own_rows), scratch_d, down_sum
    )
    beside = {
        0: [up_steps],
        1: [low_steps, up_steps],
        2: [down_steps, up_steps],
        3: [low_steps],
        4: [down_steps, up_steps],
        5: [low_steps],
        6: [down_steps, up_steps],
        7: [low_steps, down_steps],
    }
    for n, (dr, dq) in enumerate(ORDER):
        pair(batch.chip(dr, dq), (dr, dq) == (0, 0))
        next(kv_steps)
        for step in beside[n]:
            next(step, None)
    for s in range(seqs):
        for h in range(heads):
            grad_query[s * seq_dev : (s + 1) * seq_dev, h * head : (h + 1) * head] = acc[
                s, h * seq_dev : (h + 1) * seq_dev, :
            ]
    run_all(kv_steps, down_steps, low_steps, up_steps)
    add_rows(final, [down_sum, resid])


def attention_back(
    scale, queries, lse, attended, gate_raw, grad_gated, grad_resid, resid, kv_all, down, up_part
):
    rows, cols = attended.shape
    own_rows, width = resid.shape
    seqs, head_rows, head = queries.shape
    ff = up_part.shape[1]
    depth = width // 16
    shape = jax.ShapeDtypeStruct
    return pl.pallas_call(
        functools.partial(attention_kernel, scale),
        out_shape=[
            shape((rows, cols), f32),
            shape((rows, cols), f32),
            shape((rows, cols), bf16),
            shape((rows, width), bf16),
            shape((own_rows, width), bf16),
            shape((depth, ff), f32),
        ],
        in_specs=[VM] * 7 + [ANY] * 3,
        out_specs=[VM] * 3 + [ANY] + [VM] * 2,
        scratch_shapes=[
            pltpu.VMEM(kv_all.shape, bf16),
            pltpu.VMEM((rows, width), bf16),
            pltpu.VMEM((width, ff), bf16),
            pltpu.VMEM((own_rows, width), bf16),
            pltpu.VMEM(queries.shape, bf16),
            pltpu.VMEM((seqs, head, head_rows), bf16),
            pltpu.VMEM((seqs, head, head_rows), bf16),
            pltpu.VMEM((seqs, 1, head_rows), f32),
            pltpu.VMEM(queries.shape, f32),
            pltpu.VMEM(kv_all.shape, bf16),
            pltpu.VMEM((own_rows, width), f32),
        ]
        + reduce_scratch(rows, cols, True)
        + reduce_scratch(own_rows, width, False)
        + reduce_scratch(depth, ff, True)
        + sems(72, 6),
        name="attention_back",
        compiler_params=params(3, 62),
    )(queries, lse, attended, gate_raw, grad_gated, grad_resid, resid, kv_all, down, up_part)


def last_kernel(
    grad_query,
    kv_grad,
    gate_grad,
    query_raw,
    kv_raw,
    cosine,
    sine,
    gain_wide,
    gain_head,
    inputs,
    grad_resid,
    final,
    gated,
    norm_mlp_grad,
    normed_in,
    low_in,
    kvo_in,
    qg_in,
    down_in,
    tokens,
    output,
    weight_grad,
    down_grad,
    sums,
    normed,
    low,
    w_kvo,
    w_qg,
    down_part,
    qg_low,
    kv_low,
    part,
    weight_part,
    held,
    own,
    total,
    mine,
    over_tensor,
    mine_too,
    over_batch,
    *rest,
):
    scratch, scratch_w, scratch_d = rest[:5], rest[5:11], rest[11:17]
    copies = Copies(*rest[17:])
    tensor, batch = Group("tensor", False), Group("batch")
    rows, width = normed.shape
    own_rows = inputs.shape[0]
    cols = grad_query.shape[1]
    head = gain_head.shape[1]
    seq_dev = cosine.shape[0]
    depth = weight_grad.shape[0]
    loads = [
        copies.local(a, c)
        for a, c in (
            (qg_in, w_qg),
            (kvo_in, w_kvo),
            (down_in, down_part),
            (normed_in, normed),
            (low_in, low),
        )
    ]
    enter(near(tensor, batch))
    output_steps = gather(copies, tensor, final, lambda s: unit_rows(output, s, own_rows))
    next(output_steps)

    def head_back(raw, gain, grad, at):
        back = grad * cosine[...] - pltpu.roll(grad, head // 2, 1) * sine[...]
        values, terms = norm_back(raw, gain, back)
        return values.astype(bf16), jnp.sum(terms, axis=0, keepdims=True)

    mine[...] = jnp.zeros_like(mine)
    norm_rows = width // 128
    for s in range(rows // seq_dev):
        at = pl.ds(s * seq_dev, seq_dev)
        for h in range(cols // head):
            here = pl.ds(h * head, head)
            qg_low[at, here], terms = head_back(
                query_raw[at, here], gain_head[0:1, :], grad_query[at, here], at
            )
            mine[2 * norm_rows : 2 * norm_rows + 1, :] += terms
        kv_low[at, :head], terms = head_back(
            kv_raw[at, :head], gain_head[1:2, :], kv_grad[at, :head], at
        )
        mine[2 * norm_rows + 1 : 2 * norm_rows + 2, :] += terms
        kv_low[at, head:] = kv_grad[at, head:].astype(bf16)
        qg_low[at, cols:] = gate_grad[at, :]
    loads[0].wait()
    loads[1].wait()
    for n in range(4):
        slots = pl.ds(n * 4, 4)
        value = dot_t(qg_low[...], w_qg[slots].reshape(width // 4, 2 * cols))
        value += dot_t(kv_low[...], w_kvo[slots, :depth, :cols].reshape(width // 4, cols))
        part[:, n * (width // 4) : (n + 1) * (width // 4)] = value.astype(bf16)
    steps = reduce(copies, tensor, row_unit(tensor, part, own_rows), scratch, held)
    next(steps)
    loads[2].wait()
    down_steps = reduce(copies, batch, row_unit(batch, down_part, depth), scratch_d, down_grad)
    next(down_steps)
    loads[3].wait()
    loads[4].wait()
    next(output_steps)
    outer(normed, qg_low, weight_part, slice(0, 2 * cols))
    next(steps)
    next(down_steps)
    outer(normed, kv_low, weight_part, slice(2 * cols, 3 * cols))
    outer(low, gated, weight_part, slice(3 * cols, 4 * cols))
    weight_steps = reduce(
        copies, batch, row_unit(batch, weight_part, depth), scratch_w, weight_grad
    )
    next(weight_steps)
    for n in range(norm_rows):
        mine[norm_rows + n : norm_rows + n + 1, :] = norm_mlp_grad[:, n * 128 : (n + 1) * 128]

    def small():
        yield from gather(copies, tensor, mine, lambda s: over_tensor.at[s], False)
        total_t = over_tensor[0]
        for n in range(1, 8):
            total_t = total_t + over_tensor[n]
        mine_too[...] = total_t
        yield from gather(copies, batch, mine_too, lambda s: over_batch.at[s], False)
        total_b = over_batch[0]
        for n in range(1, 16):
            total_b = total_b + over_batch[n]
        sums[...] = total_b

    def along():
        yield from steps
        total[...] = jnp.zeros_like(total)

        def body(at):
            back, terms = norm_back(inputs[at, :], gain_wide[0:1, :], held[at, :])
            total[...] += terms
            own[at, :] = (grad_resid[at, :] + back).astype(bf16)

        each_rows(own_rows, 16, body)
        gain_row = jnp.sum(total[...], axis=0, keepdims=True)
        for n in range(norm_rows):
            mine[n : n + 1, :] = gain_row[:, n * 128 : (n + 1) * 128]
        big = gather(copies, tensor, own, lambda s: unit_rows(tokens, s, own_rows))
        few = small()
        for _ in big:
            next(few, None)
            yield
        yield from few

    run_all(output_steps, along(), down_steps, weight_steps)


def last_step(scale_free, held_in_hbm, few_shape):
    (grad_query, _, _, query_raw, _, _, _, _, gain_head, inputs, *_) = scale_free
    normed, low, kvo, qg, down_part = held_in_hbm
    own_rows, width = inputs.shape
    rows, cols = grad_query.shape
    ff = down_part.shape[1]
    depth = width // 16
    shape = jax.ShapeDtypeStruct
    return pl.pallas_call(
        last_kernel,
        out_shape=[
            shape((rows, width), bf16),
            shape((rows, width), bf16),
            shape((depth, 4 * cols), f32),
            shape((depth, ff), f32),
            shape(few_shape, f32),
        ],
        in_specs=[VM] * len(scale_free) + [ANY] * len(held_in_hbm),
        out_specs=[ANY] * 2 + [VM] * 3,
        scratch_shapes=[
            pltpu.VMEM((rows, width), bf16),
            pltpu.VMEM((rows, width), bf16),
            pltpu.VMEM(kvo.shape, bf16),
            pltpu.VMEM(qg.shape, bf16),
            pltpu.VMEM((width, ff), bf16),
            pltpu.VMEM((rows, 2 * cols), bf16),
            pltpu.VMEM((rows, cols), bf16),
            pltpu.VMEM((rows, width), bf16),
            pltpu.VMEM((width, 4 * cols), bf16),
            pltpu.VMEM((own_rows, width), f32),
            pltpu.VMEM((own_rows, width), bf16),
            pltpu.VMEM((16, width), f32),
            pltpu.VMEM(few_shape, f32),
            pltpu.VMEM((8,) + few_shape, f32),
            pltpu.VMEM(few_shape, f32),
            pltpu.VMEM((16,) + few_shape, f32),
        ]
        + reduce_scratch(own_rows, width, False)
        + reduce_scratch(depth, 4 * cols, True)
        + reduce_scratch(depth, ff, True)
        + sems(120, 12),
        name="projections_back",
        compiler_params=params(4, 62),
    )(*scale_free, *held_in_hbm)


def shards(
    tokens,
    target,
    domain_ids,
    domain_counts,
    weight_index,
    loss_weights,
    w_query,
    w_key,
    w_value,
    w_gate_out,
    w_output,
    w_gate,
    w_up,
    w_down,
    norm_attn,
    norm_mlp,
    gain_query,
    gain_key,
):
    seq_count, seq_dev, width = tokens.shape
    rows = seq_count * seq_dev
    members = lax.axis_size("tensor")
    batch_count = lax.axis_size("batch")
    b, t = lax.axis_index("batch"), lax.axis_index("tensor")
    own_rows = rows // members
    seq_len = seq_dev * batch_count
    head = gain_query.shape[0] * batch_count
    scale = head ** (-0.5)
    q_cols, k_cols = w_query.shape[1], w_key.shape[1]
    heads = q_cols // head

    gains = jnp.zeros((2, head), bf16)
    gains = lax.dynamic_update_slice(
        gains, jnp.stack([gain_query, gain_key]), (0, b * gain_query.shape[0])
    )
    few = jnp.concatenate(
        [norm_attn[None], norm_mlp[None], gains, jnp.zeros((12, head), bf16)], axis=0
    )
    few = jnp.pad(few, ((0, 0), (0, 2 * k_cols + q_cols - head)))
    packs = (
        jnp.concatenate([jnp.concatenate([w_key, w_value, w_output.T], axis=1), few], axis=0),
        jnp.concatenate([w_query, w_gate_out], axis=1),
    )

    half_size = head // 2
    pos_local = (b * seq_dev + jnp.arange(seq_dev, dtype=jnp.int32)).astype(f32)
    inverse_freq = rope_base ** (-jnp.arange(half_size, dtype=f32) / half_size)
    angles = pos_local[:, None] * inverse_freq[None, :]
    cosine, sine = jnp.cos(angles), jnp.sin(angles)
    cosine_wide = jnp.concatenate([cosine, cosine], axis=1)
    sine_wide = jnp.concatenate([-sine, sine], axis=1)

    tokens_low = tokens.reshape(rows, width)
    ff = w_gate.shape[1]
    (
        normed_low,
        query_raw,
        kv_raw,
        gate_raw,
        queries,
        kv_all,
        attended,
        lse,
        gated_low,
        normed_mlp_low,
        resid_own,
        wide_kvo,
        wide_qg,
        w_out_all,
        wide_gate,
        wide_up,
        wide_down,
        gain_wide,
        gain_head,
    ) = forward(
        tokens_low,
        cosine_wide,
        sine_wide,
        packs,
        (w_gate, w_up, w_down.T),
        scale,
        seq_count,
    )
    inputs_own = lax.dynamic_slice_in_dim(tokens_low, t * own_rows, own_rows, 0).astype(f32)

    domain_range = jnp.arange(domain_counts.shape[0], dtype=jnp.int32)
    level_pick = (
        weight_index[:, None] == jnp.arange(loss_weights.shape[0], dtype=jnp.int32)[None, :]
    ).astype(f32)
    domain_factor = (
        jnp.sum(level_pick * loss_weights[None, :], axis=1) * seq_len / domain_counts.astype(f32)
    )
    seq_pick = (domain_ids[:, None] == domain_range[None, :]).astype(f32)
    seq_weight = jnp.sum(seq_pick * domain_factor[None, :], axis=1)
    row_weight = jnp.repeat(seq_weight, seq_dev)[:, None]
    target_low = target.reshape(rows, width)
    grad_final_low = (target_low.astype(f32) * row_weight).astype(bf16)
    grad_final_own = lax.dynamic_slice_in_dim(target_low, t * own_rows, own_rows, 0).astype(
        f32
    ) * lax.dynamic_slice_in_dim(row_weight, t * own_rows, own_rows, 0)

    weights = [w.reshape(width, ff) for w in (wide_gate, wide_up, wide_down)]
    (
        down_part,
        up_weight_part,
        down_weight_part,
        grad_gate,
        grad_resid_own,
        grad_gated,
        norm_mlp_terms,
    ) = mlp(
        resid_own,
        grad_final_own,
        gain_wide[1:2],
        normed_mlp_low,
        grad_final_low,
        weights,
        w_out_all,
    )
    grad_query_rot, kv_grad, gate_raw_grad, grad_resid_low, final_own, grad_up = attention_back(
        scale,
        queries,
        lse,
        attended,
        gate_raw,
        grad_gated,
        grad_resid_own,
        resid_own,
        kv_all,
        down_part,
        up_weight_part,
    )
    norm_rows = width // 128
    grad_tokens, output, weight_grad, grad_down_t, sums_all = last_step(
        (
            grad_query_rot,
            kv_grad,
            gate_raw_grad,
            query_raw,
            kv_raw,
            cosine_wide,
            sine_wide,
            gain_wide,
            gain_head,
            inputs_own,
            grad_resid_own,
            final_own,
            gated_low,
            norm_mlp_terms,
        ),
        (normed_low, grad_resid_low, wide_kvo, wide_qg, down_weight_part),
        (2 * norm_rows + 8, 128),
    )

    def own_part(flat, like):
        return lax.dynamic_slice_in_dim(flat, b * like.shape[0], like.shape[0], 0)

    return (
        output.reshape(tokens.shape),
        grad_tokens.astype(f32).reshape(tokens.shape),
        weight_grad[:, :q_cols],
        weight_grad[:, 2 * q_cols : 2 * q_cols + k_cols],
        weight_grad[:, 2 * q_cols + k_cols : 2 * q_cols + 2 * k_cols],
        weight_grad[:, q_cols : 2 * q_cols],
        weight_grad[:, 2 * q_cols + 2 * k_cols :].T,
        grad_gate,
        grad_up,
        grad_down_t.T,
        own_part(sums_all[:norm_rows].reshape(-1), norm_attn),
        own_part(sums_all[norm_rows : 2 * norm_rows].reshape(-1), norm_mlp),
        own_part(sums_all[2 * norm_rows], gain_query),
        own_part(sums_all[2 * norm_rows + 1], gain_key),
    )


def solution(mesh):
    in_specs = (
        P(None, "batch", None),
        P(None, "batch", None),
        P(),
        P(),
        P(),
        P(),
        P("batch", "tensor"),
        P("batch", "tensor"),
        P("batch", "tensor"),
        P("batch", "tensor"),
        P("tensor", "batch"),
        P("batch", "tensor"),
        P("batch", "tensor"),
        P("tensor", "batch"),
        P("batch"),
        P("batch"),
        P("batch"),
        P("batch"),
    )
    out_specs = (
        P(None, "batch", None),
        P(None, "batch", None),
        P("batch", "tensor"),
        P("batch", "tensor"),
        P("batch", "tensor"),
        P("batch", "tensor"),
        P("tensor", "batch"),
        P("batch", "tensor"),
        P("batch", "tensor"),
        P("tensor", "batch"),
        P("batch"),
        P("batch"),
        P("batch"),
        P("batch"),
    )
    return jax.shard_map(shards, mesh=mesh, in_specs=in_specs, out_specs=out_specs, check_vma=False)
```

```python
import functools
import itertools
import math

import jax
import jax.numpy as jnp
from jax import lax
from jax.experimental import pallas as pl
from jax.experimental.pallas import tpu as pltpu
from jax.sharding import PartitionSpec as P

MESH = pl.DeviceIdType.MESH
epsilon = 1e-06
rope_base = 1000000.0
f32 = jnp.float32
bf16 = jnp.bfloat16
MIB = 2**20
ANY = pl.BlockSpec(memory_space=pl.ANY)
VM = pl.BlockSpec(memory_space=pltpu.VMEM)


class Group:
    def __init__(self, kind, core=True):
        b = lax.axis_index("batch")
        t = lax.axis_index("tensor")
        c = lax.rem(b, 2)
        self.c, self.t = c, t
        if kind == "tensor":
            r, q = lax.div(t, 2), lax.rem(t, 2)
            self.slot = lambda dr, dq: lax.rem(r + dr, 4) * 2 + lax.rem(q + dq, 2)
            at = lambda dr, dq: (b, self.slot(dr, dq))
        else:
            q, r = lax.div(b, 8), lax.rem(lax.div(b, 2), 4)
            self.chip = lambda dr, dq: lax.rem(q + dq, 2) * 4 + lax.rem(r + dr, 4)
            self.slot = lambda dr, dq, dc=0: self.chip(dr, dq) * 2 + lax.rem(c + dc, 2)
            at = lambda dr, dq: (self.slot(dr, dq), t)
        self.core = (b + 1 - 2 * c, t) if core else None
        self.right, self.left, self.mate = at(1, 0), at(3, 0), at(0, 1)
        self.others = [at(dr, dq) for dr in range(4) for dq in range(2) if dr or dq]
        self.steps = [(dr, dq) for dr in range(4) for dq in range(2) if dr or dq]


def enter(devices):
    barrier = pltpu.get_barrier_semaphore()
    for device in devices:
        pl.semaphore_signal(barrier, inc=1, device_id=device, device_id_type=MESH)
    pl.semaphore_wait(barrier, len(devices))


def near(*groups):
    devices = [d for g in groups for d in (g.right, g.left, g.mate)]
    cores = [g.core for g in groups if g.core is not None]
    return devices + cores[:1]


class Copies:
    def __init__(self, send_sem, recv_sem, local_sem):
        self.send_sem, self.recv_sem, self.local_sem = send_sem, recv_sem, local_sem
        self.count = 0
        self.locals = 0

    def send(self, source, target, device):
        copy = pltpu.make_async_remote_copy(
            src_ref=source,
            dst_ref=target,
            send_sem=self.send_sem.at[self.count],
            recv_sem=self.recv_sem.at[self.count],
            device_id=device,
            device_id_type=MESH,
        )
        self.count += 1
        copy.start()
        return copy

    def local(self, source, target):
        copy = pltpu.make_async_copy(source, target, self.local_sem.at[self.locals])
        self.locals += 1
        copy.start()
        return copy


def half_of(ref, which):
    width = ref.shape[-1] // 2
    lead = (slice(None),) * (len(ref.shape) - 1)
    return ref.at[lead + (pl.ds(which * width, width),)]


def run_all(*steps):
    waiting = list(steps)
    while waiting:
        for step in list(waiting):
            try:
                next(step)
            except StopIteration:
                waiting.remove(step)


def gather(copies, group, own, slot, split=True, source=None, by_mate=True):
    s = group.slot
    core_copies = []
    sent = []

    def push(ref, *devices):
        out = [copies.send(ref, ref, device) for device in devices]
        sent.extend(out)
        return out

    def to_core(ref):
        if group.core is not None:
            core_copies.extend(push(ref, group.core))

    def core_wait(count):
        for copy in core_copies[:count]:
            copy.wait_recv()
        del core_copies[:count]

    def onward(unit, way):
        if way == 0:
            return push(half_of(unit, 0) if split else unit, group.right)
        return push(half_of(unit, 1), group.left) if split else []

    home = slot(s(0, 0))
    source = own if source is None else source
    first = [copies.send(source, home, d) for d in (group.right, group.left, group.mate)]
    sent.extend(first)
    kept = None
    if own is not None:
        kept = copies.local(own, home)
        if group.core is not None:
            core_copies.append(copies.send(own, home, group.core))
            sent.append(core_copies[0])
    from_left, from_right, from_mate = first
    yield []
    far = []
    for way, copy in enumerate((from_left, from_right)):
        copy.wait_recv()
        unit = slot(s(3 - 2 * way, 0))
        far += onward(unit, way)
        to_core(unit)
    from_mate.wait_recv()
    mate_unit = slot(s(0, 1))
    mate_line = push(mate_unit, group.right, group.left)
    to_core(mate_unit)
    if own is not None:
        core_wait(1)
        kept.wait()
    yield [(0, 0)]
    mate_far = []
    for copy in far:
        copy.wait_recv()
    if by_mate:
        mate_far += push(slot(s(2, 0)), group.mate)
    to_core(slot(s(2, 0)))
    yield []
    for way, copy in enumerate(mate_line):
        copy.wait_recv()
        unit = slot(s(3 - 2 * way, 1))
        if not by_mate:
            mate_far += onward(unit, way)
        to_core(unit)
    core_wait(3)
    yield [(3, 0), (1, 0), (0, 1)]
    for copy in mate_far:
        copy.wait_recv()
    to_core(slot(s(2, 1)))
    core_wait(3)
    yield [(2, 0), (3, 1), (1, 1)]
    core_wait(1)
    yield [(2, 1)]
    for copy in sent:
        copy.wait_send()


def add_rows(target, sources, step=16):
    def body(at):
        total = sources[0][at, :].astype(f32)
        for source in sources[1:]:
            total = total + source[at, :].astype(f32)
        target[at, :] = total.astype(target.dtype)

    each_rows(target.shape[0], step, body)


def rows_at(i, step=16):
    return pl.ds(pl.multiple_of(i * step, step), step)


def each_rows(rows, step, body):
    def run(i, carry):
        body(rows_at(i, step))
        return carry

    lax.fori_loop(0, rows // step, run, 0)


def reduce_scratch(rows, width, core):
    shapes = [
        pltpu.VMEM((4, rows, width // 2), bf16),
        pltpu.VMEM((4, rows, width), bf16),
        pltpu.VMEM((4, rows, width), bf16),
        pltpu.VMEM((3, rows, width), bf16),
        pltpu.VMEM((2, rows, width), bf16),
    ]
    if core:
        shapes += [pltpu.VMEM((8, rows, width), bf16)]
    return shapes


ORDER = [(2, 1), (1, 1), (3, 1), (2, 0), (1, 0), (3, 0), (0, 1), (0, 0)]


def reduce(copies, group, part, scratch, result, early=False, by_mate=True):
    far, near_in, outgoing, mates, far_sums = scratch[:5]
    core = group.core is not None
    sent = []

    def send(source, target, device):
        copy = copies.send(source, target, device)
        sent.append(copy)
        return copy

    arrived = {}

    def to_core(n):
        dr, dq = ORDER[n]
        arrived[dr, dq] = (send(part(dr, dq, 1), scratch[5].at[n], group.core), n)

    def terms(dr, dq):
        if not core:
            return [part(dr, dq)]
        copy, n = arrived[dr, dq]
        copy.wait_recv()
        return [part(dr, dq, 0), scratch[5].at[n]]

    sides = ((1, group.right), (3, group.left))

    def far_sends(unit, line):
        return [
            send(half_of(unit, way), far.at[line * 2 + way], device)
            for way, (_, device) in enumerate(sides)
        ]

    def line_sends(line, far_copies):
        out = []
        for way, (dr, device) in enumerate(sides):
            unit = terms(dr, line)
            held = outgoing.at[line * 2 + way]
            if far_copies is not None:
                far_copies[way].wait_recv()
                there = far.at[line * 2 + way]
                add_rows(half_of(held, way), [half_of(u, way) for u in unit] + [there])
                add_rows(half_of(held, 1 - way), [half_of(u, 1 - way) for u in unit])
            elif core:
                add_rows(held, unit)
            else:
                held = unit[0]
            out.append(send(held, near_in.at[line * 2 + way], device))
        return out

    def first():
        unit = terms(2, 1)
        if core:
            add_rows(far_sums.at[1], unit)
            unit = [far_sums.at[1]]
        if by_mate:
            return send(unit[0], mates.at[2], group.mate), line_sends(1, None)
        return None, far_sends(unit[0], 1)

    def second():
        unit = terms(2, 0)
        if by_mate:
            far_mate.wait_recv()
            unit = unit + [mates.at[2]]
        if len(unit) > 1:
            add_rows(far_sums.at[0], unit)
            unit = [far_sums.at[0]]
        return far_sends(unit[0], 0)

    def third():
        return line_sends(0, far_copies)

    if early:
        for n in range(3):
            to_core(n)
            yield
        to_core(3)
        far_mate, mate_line = first()
        yield
        to_core(4)
        far_copies = second()
        yield
        to_core(5)
        yield
        to_core(6)
        own_line = third()
        yield
        to_core(7)
    else:
        if core:
            for n in range(8):
                to_core(n)
            yield
        far_mate, mate_line = first()
        yield
        far_copies = second()
        yield
        if not by_mate:
            mate_line = line_sends(1, mate_line)
        own_line = third()
    yield
    unit = terms(0, 1)
    for copy in mate_line:
        copy.wait_recv()
    add_rows(mates.at[0], unit + [near_in.at[2], near_in.at[3]])
    to_mate = send(mates.at[0], mates.at[1], group.mate)
    yield
    unit = terms(0, 0)
    for copy in own_line:
        copy.wait_recv()
    to_mate.wait_recv()
    add_rows(result, unit + [near_in.at[0], near_in.at[1], mates.at[1]])
    for copy in sent:
        copy.wait_send()


def sems(remote, local):
    return [
        pltpu.SemaphoreType.DMA((remote,)),
        pltpu.SemaphoreType.DMA((remote,)),
        pltpu.SemaphoreType.DMA((max(local, 1),)),
    ]


def params(collective, limit=48):
    return pltpu.CompilerParams(
        collective_id=collective, has_side_effects=True, vmem_limit_bytes=limit * MIB
    )


def prepare_head(values, gain, cosine, sine):
    half_size = values.shape[1] // 2
    mean = jnp.mean(values * values, axis=-1, keepdims=True)
    scaled = values * lax.rsqrt(mean + epsilon) * gain
    return scaled * cosine + pltpu.roll(scaled, half_size, 1) * sine


def forward_kernel(
    scale,
    tokens,
    cosine,
    sine,
    seq_weight,
    norm_attn,
    norm_mlp,
    gain_query,
    gain_key,
    w_output,
    w_down,
    w_query,
    w_key,
    w_value,
    w_gate_out,
    mlp_a,
    mlp_b,
    target_in,
    normed_out,
    query_raw,
    kv_raw,
    gate_raw,
    queries,
    kv_out,
    attended,
    lse,
    gated,
    normed_mlp,
    resid,
    wide_kvo,
    wide_qg,
    w_out_out,
    wide_a,
    wide_b,
    wide_c,
    gain_wide,
    gain_head,
    inputs_own,
    grad_final,
    low_out,
    normed,
    inverse,
    pack_a,
    pack_b,
    mlp_c,
    few,
    target,
    low,
    w_kvo,
    w_qg,
    w_out,
    kv_own,
    kv_all,
    acc,
    rows_all,
    own,
    send_sem,
    recv_sem,
    local_sem,
):
    copies = Copies(send_sem, recv_sem, local_sem)
    tensor, batch = Group("tensor"), Group("batch")
    b = lax.axis_index("batch")
    rows, width = tokens.shape
    cols = query_raw.shape[1]
    own_rows = resid.shape[0]
    seqs, head_rows, head = queries.shape
    heads = query_raw.shape[1] // head
    seq_dev = rows // seqs
    depth, key_cols = w_key.shape
    packing = [
        copies.local(source, place)
        for source, place in (
            (w_key, pack_a.at[pl.ds(0, depth), pl.ds(0, key_cols)]),
            (w_value, pack_a.at[pl.ds(0, depth), pl.ds(key_cols, key_cols)]),
            (w_query, pack_b.at[:, pl.ds(0, cols)]),
            (w_gate_out, pack_b.at[:, pl.ds(cols, cols)]),
        )
    ]
    target_load = copies.local(target_in, target)

    def flipped(values):
        return values.astype(f32).T.astype(bf16)

    pack_a[0:depth, cols:] = flipped(w_output[...])
    few[...] = jnp.zeros_like(few)
    share = gain_query.shape[1]
    few[0:1, :] = norm_attn[...].astype(f32)
    few[1:2, :] = norm_mlp[...].astype(f32)
    few[2:3, 0:share] = gain_query[...].astype(f32)
    few[3:4, 0:share] = gain_key[...].astype(f32)
    placed = pltpu.roll(few[...], b * share, 1)
    row = lax.broadcasted_iota(jnp.int32, placed.shape, 0)
    pack_a[depth:, :] = jnp.zeros((16, pack_a.shape[1]), bf16)
    pack_a[depth:, 0:128] = jnp.where(row < 2, few[...], placed).astype(bf16)
    enter(tensor.others + near(batch))

    def batch_gather(source, target, split=True):
        return gather(copies, batch, source, lambda s: target.at[s], split)

    for copy in packing:
        copy.wait()
    a_steps = batch_gather(pack_a, w_kvo)
    b_steps = batch_gather(pack_b, w_qg)
    next(a_steps)
    next(b_steps)

    def invert(at):
        values = tokens[at, :].astype(f32)
        mean = jnp.mean(values * values, axis=-1, keepdims=True)
        inverse[at, :] = jnp.broadcast_to(lax.rsqrt(mean + epsilon), (32, 128))

    each_rows(rows, 32, invert)
    mlp_c[...] = flipped(w_down[...])
    next(a_steps)
    next(b_steps)
    for _ in a_steps:
        pass
    half = tensor.c * 8
    kept = [copies.local(w_kvo, wide_kvo)]
    out_home = copies.local(w_kvo.at[:, pl.ds(0, depth), pl.ds(cols, cols)], w_out.at[tensor.t])
    wide_out_steps = gather(
        copies,
        tensor,
        None,
        lambda s: w_out.at[s, pl.ds(half, 8)],
        source=w_kvo.at[pl.ds(half, 8), pl.ds(0, depth), pl.ds(cols, cols)],
        by_mate=False,
    )
    next(wide_out_steps)
    gain_wide[...] = jnp.zeros_like(gain_wide)
    gain_head[...] = jnp.zeros_like(gain_head)
    total = jnp.zeros((16, 128), f32)
    for n in range(16):
        entry = w_kvo[n, depth:, 0:128].astype(f32)
        gain_wide[0:2, n * 128 : (n + 1) * 128] = entry[0:2]
        total = total + entry
    gain_head[0:2, :] = total[2:4]

    def normalise(at):
        scaled = tokens[at, :].astype(f32) * inverse[at, 0:1] * gain_wide[0:1, :]
        normed[at, :] = scaled.astype(bf16)

    each_rows(rows, 32, normalise)
    kept.append(copies.local(normed, normed_out))

    def project(weights, at):
        return jnp.dot(normed[at, :], weights.reshape(width, cols), preferred_element_type=f32)

    for s in range(seqs):
        at = pl.ds(s * seq_dev, seq_dev)
        raw = project(w_kvo[:, 0:depth, 0:cols], at)
        kv_raw[at, :] = raw
        key = prepare_head(raw[:, :head], gain_head[1:2, :], cosine[...], sine[...])
        kv_own[at, :head] = key.astype(bf16)
        kv_own[at, head:] = raw[:, head:].astype(bf16)
    all_steps = batch_gather(kv_own, kv_all)
    next(all_steps)
    for _ in b_steps:
        pass
    kept.append(copies.local(w_qg, wide_qg))
    for s in range(seqs):
        at = pl.ds(s * seq_dev, seq_dev)
        raw = project(w_qg[:, :, 0:cols], at)
        query_raw[at, :] = raw
        for h in range(heads):
            values = prepare_head(
                raw[:, h * head : (h + 1) * head], gain_head[0:1, :], cosine[...], sine[...]
            )
            queries[s, h * seq_dev : (h + 1) * seq_dev, :] = values.astype(bf16)
        gate_raw[at, :] = project(w_qg[:, :, cols:], at)

    target_load.wait()
    for s in range(seqs):

        def weigh(at):
            at = pl.ds(s * seq_dev + at.start, at.size)
            low[at, :] = (target[at, :].astype(f32) * seq_weight[s : s + 1, 0:1]).astype(bf16)

        each_rows(seq_dev, 32, weigh)
    kept.append(copies.local(low, low_out))
    own_weight = jnp.where(tensor.t < 4, seq_weight[0:1, 0:1], seq_weight[1:2, 0:1])

    def weigh_own(at):
        there = pl.ds(pl.multiple_of(tensor.t * own_rows + at.start, 16), at.size)
        inputs_own[at, :] = tokens[there, :]
        grad_final[at, :] = target[there, :].astype(f32) * own_weight

    each_rows(own_rows, 16, weigh_own)
    factor = scale * math.log2(math.e)
    ones = jnp.ones((2 * seq_dev, head), bf16)
    tile = head_rows // 4
    acc[...] = jnp.zeros_like(acc)

    def block(pair, masked):
        def body(s, carry):
            at = rows_at(s, seq_dev)
            keys = jnp.concatenate(
                [kv_all[pair * 2, at, :head], kv_all[pair * 2 + 1, at, :head]], axis=0
            )
            values = jnp.concatenate(
                [kv_all[pair * 2, at, head:], kv_all[pair * 2 + 1, at, head:]], axis=0
            )
            wide = jnp.concatenate([values, ones], axis=1)
            for i in range(4):
                here = pl.ds(i * tile, tile)
                scores = lax.dot_general(
                    queries[s, here, :], keys, (((1,), (1,)), ((), ())), preferred_element_type=f32
                )
                weights = jnp.exp2(scores * factor)
                if masked:
                    row = lax.broadcasted_iota(jnp.int32, scores.shape, 0) + (i * tile) % seq_dev
                    col = lax.broadcasted_iota(jnp.int32, scores.shape, 1)
                    ahead = (pair * 2 - b) * seq_dev
                    weights = jnp.where(col + ahead <= row, weights, 0.0)
                acc[s, here, :] += jnp.dot(weights.astype(bf16), wide, preferred_element_type=f32)
            return carry

        lax.fori_loop(0, seqs, body, 0)

    here = batch.chip(0, 0)

    def attend(ready):
        for dr, dq in ready:
            if (dr, dq) == (0, 0):
                block(here, True)
            else:
                pair = batch.chip(dr, dq)

                @pl.when(pair < here)
                def _():
                    block(pair, False)

    mlp_steps = [
        batch_gather(mlp_a, wide_a),
        batch_gather(mlp_b, wide_b),
        batch_gather(mlp_c, wide_c),
    ]
    attend(next(all_steps))
    next(wide_out_steps)
    attend(next(all_steps))
    next(wide_out_steps)
    ready = next(all_steps)
    for step in mlp_steps:
        next(step)
    attend(ready)
    ready = next(all_steps)
    next(wide_out_steps)
    attend(ready)
    attend(next(all_steps))
    for _ in all_steps:
        pass
    kept.append(copies.local(kv_all, kv_out))
    for s in range(seqs):
        sums = acc[s, :, head:]
        lse[s] = jnp.log2(sums).T[0:1, :]
        out = acc[s, :, :head] / sums
        for h in range(heads):
            at, cols = pl.ds(s * seq_dev, seq_dev), pl.ds(h * head, head)
            part = out[h * seq_dev : (h + 1) * seq_dev]
            attended[at, cols] = part
            gated[at, cols] = (part * jax.nn.sigmoid(gate_raw[at, cols])).astype(bf16)

    def unit_rows(ref, slot):
        return ref.at[pl.ds(pl.multiple_of(slot * own_rows, 16), own_rows), :]

    exchanged = [
        copies.send(unit_rows(gated, tensor.slot(*step)), rows_all.at[tensor.t], device)
        for step, device in zip(tensor.steps, tensor.others)
    ]
    rows_all[tensor.t] = unit_rows(gated, tensor.t)[...]
    run_all(wide_out_steps, *[itertools.islice(step, 1) for step in mlp_steps])
    out_home.wait()
    kept.append(copies.local(w_out, w_out_out))
    for copy in exchanged:
        copy.wait_recv()
    resid[...] = unit_rows(tokens, tensor.t)[...].astype(f32)

    def out_term(n, carry):
        resid[...] += lax.dot_general(
            rows_all[n],
            w_out[n].reshape(width, -1),
            (((1,), (1,)), ((), ())),
            preferred_element_type=f32,
        )
        return carry

    lax.fori_loop(0, 8, out_term, 0)

    def normalise_own(at):
        values = resid[at, :]
        mean = jnp.mean(values * values, axis=-1, keepdims=True)
        own[at, :] = (values * lax.rsqrt(mean + epsilon) * gain_wide[1:2, :]).astype(bf16)

    each_rows(own_rows, 16, normalise_own)
    tensor.core = None
    own_steps = gather(
        copies, tensor, own, lambda s: unit_rows(normed_mlp, s), by_mate=False
    )
    run_all(own_steps, *mlp_steps)
    for copy in exchanged:
        copy.wait_send()
    for copy in kept:
        copy.wait()


def forward(scale, seqs, small, weights, target):
    tokens, cosine = small[:2]
    rows, width = tokens.shape
    depth, cols = weights[0].shape
    ff = weights[4].shape[1]
    head = cosine.shape[1]
    own_rows = rows // 8
    heads = cols // head
    shape = jax.ShapeDtypeStruct
    pack_a, pack_b = (depth + 16, 2 * cols), (depth, 2 * cols)
    weight_a, weight_b = (16,) + pack_a, (16,) + pack_b
    weight_out = (8, 16, depth, cols)
    outs = [
        (shape((rows, width), bf16), ANY),
        (shape((rows, cols), f32), VM),
        (shape((rows, cols), f32), VM),
        (shape((rows, cols), f32), VM),
        (shape((seqs, heads * rows // seqs, head), bf16), VM),
        (shape((16, rows, cols), bf16), ANY),
        (shape((rows, cols), f32), VM),
        (shape((seqs, 1, heads * rows // seqs), f32), VM),
        (shape((rows, cols), bf16), VM),
        (shape((rows, width), bf16), ANY),
        (shape((own_rows, width), f32), VM),
        (shape(weight_a, bf16), ANY),
        (shape(weight_b, bf16), ANY),
        (shape(weight_out, bf16), ANY),
    ]
    outs += [(shape((16, depth, ff), bf16), ANY)] * 3
    outs += [
        (shape((8, width), f32), VM),
        (shape((8, head), f32), VM),
        (shape((own_rows, width), bf16), VM),
        (shape((own_rows, width), f32), VM),
        (shape((rows, width), bf16), ANY),
    ]
    return pl.pallas_call(
        functools.partial(forward_kernel, scale),
        out_shape=[o for o, _ in outs],
        in_specs=[VM] * len(small) + [ANY] * 7,
        out_specs=[s for _, s in outs],
        scratch_shapes=[
            pltpu.VMEM((rows, width), bf16),
            pltpu.VMEM((rows, 128), f32),
            pltpu.VMEM(pack_a, bf16),
            pltpu.VMEM(pack_b, bf16),
            pltpu.VMEM((depth, ff), bf16),
            pltpu.VMEM((16, 128), f32),
            pltpu.VMEM((rows, width), bf16),
            pltpu.VMEM((rows, width), bf16),
            pltpu.VMEM(weight_a, bf16),
            pltpu.VMEM(weight_b, bf16),
            pltpu.VMEM(weight_out, bf16),
            pltpu.VMEM((rows, cols), bf16),
            pltpu.VMEM((16, rows, cols), bf16),
            pltpu.VMEM((seqs, heads * rows // seqs, 2 * head), f32),
            pltpu.VMEM((8, own_rows, cols), bf16),
            pltpu.VMEM((own_rows, width), bf16),
        ]
        + sems(24 * 8, 24),
        name="forward",
        compiler_params=params(1, 62),
    )(*small, *weights, target)


def dot(left, right):
    return jnp.dot(left, right, preferred_element_type=f32)


def dot_t(left, right):
    return lax.dot_general(left, right, (((1,), (1,)), ((), ())), preferred_element_type=f32)


def t_dot(left, right):
    return lax.dot_general(left, right, (((0,), (0,)), ((), ())), preferred_element_type=f32)


def norm_back(values, gain, grad):
    inverse = lax.rsqrt(jnp.mean(values * values, axis=-1, keepdims=True) + epsilon)
    scaled = grad * gain
    unit = values * inverse
    inner = jnp.mean(scaled * unit, axis=-1, keepdims=True)
    return (scaled - unit * inner) * inverse, grad * unit


def unit_rows(ref, slot, rows):
    return ref.at[pl.ds(pl.multiple_of(slot * rows, 16), rows), :]


def row_unit(group, ref, rows):
    def unit(*step):
        return unit_rows(ref, group.slot(*step), rows)

    return unit


def outer(left, right, target, cols, step=512):
    def body(i, carry):
        at = rows_at(i, step)
        target[at, cols] = t_dot(left[:, at], right[...]).astype(target.dtype)
        return carry

    lax.fori_loop(0, left.shape[1] // step, body, 0)


def mlp_kernel(
    resid,
    grad_final,
    gain_wide,
    normed_in,
    low_in,
    gate_in,
    up_in,
    down_in,
    out_in,
    down_out,
    up_part_out,
    down_part_out,
    gate_grad,
    grad_resid,
    grad_gated,
    gain_grad,
    normed,
    low,
    w_gate,
    w_up,
    w_down,
    w_out,
    hidden,
    grad_gate,
    grad_up,
    part,
    down,
    gate_part,
    up_part,
    down_part,
    own,
    total,
    units,
    gated_in,
    *rest,
):
    scratch_a, scratch_b, scratch_w = rest[:5], rest[5:10], rest[10:16]
    copies = Copies(*rest[16:])
    tensor, batch = Group("tensor", False), Group("batch")
    rows, width = normed.shape
    own_rows = resid.shape[0]
    ff = hidden.shape[1]
    half = width // 2
    depth = gate_grad.shape[0]
    loads = [
        copies.local(a, b)
        for a, b in (
            (normed_in, normed),
            (gate_in, w_gate),
            (up_in, w_up),
            (low_in, low),
            (down_in, w_down),
            (out_in, w_out),
        )
    ]
    enter(tensor.others + near(batch))
    for load in loads[:5]:
        load.wait()

    def activate(j, carry):
        cols = rows_at(j, 256)
        gate = dot(normed[...], w_gate[:, cols])
        up = dot(normed[...], w_up[:, cols])
        back = dot(low[...], w_down[:, cols])
        sigma = jax.nn.sigmoid(gate)
        silu = gate * sigma
        hidden[:, cols] = (silu * up).astype(bf16)
        grad_up[:, cols] = (back * silu).astype(bf16)
        grad_gate[:, cols] = (back * up * (sigma * (1.0 + gate * (1.0 - sigma)))).astype(bf16)
        return carry

    lax.fori_loop(0, ff // 256, activate, 0)

    def input_part(j, carry):
        cols = rows_at(j, 512)
        value = dot_t(grad_gate[...], w_gate[cols, :]) + dot_t(grad_up[...], w_up[cols, :])
        part[:, cols] = value.astype(bf16)
        return carry

    steps = []
    for n, scratch in enumerate((scratch_a, scratch_b)):
        lax.fori_loop(n * half // 512, (n + 1) * half // 512, input_part, 0)
        cols = pl.ds(n * half, half)
        steps.append(
            reduce(
                copies,
                tensor,
                row_unit(tensor, part.at[:, cols], own_rows),
                scratch,
                grad_resid.at[:, cols],
            )
        )
        next(steps[n])
    outer(normed, grad_gate, gate_part, slice(None))
    weight_steps = reduce(
        copies, batch, row_unit(batch, gate_part, depth), scratch_w, gate_grad, by_mate=False
    )
    next(weight_steps)
    next(steps[0])
    next(steps[1])
    outer(normed, grad_up, up_part, slice(None))
    next(steps[0])
    next(steps[1])
    next(weight_steps)
    outer(low, hidden, down_part, slice(None))
    next(steps[0])
    next(steps[1])
    next(weight_steps)

    def down_cols(j, carry):
        cols = rows_at(j, 512)
        down[:, cols] = dot_t(hidden[...], w_down[cols, :]).astype(bf16)
        return carry

    lax.fori_loop(0, width // 512, down_cols, 0)
    kept = [
        copies.local(up_part, up_part_out),
        copies.local(down_part, down_part_out),
        copies.local(down, down_out),
    ]
    run_all(*steps)
    next(weight_steps)
    total[...] = jnp.zeros_like(total)

    def body(at):
        back, terms = norm_back(resid[at, :], gain_wide[1:2, :], grad_resid[at, :])
        back = grad_final[at, :] + back
        total[...] += terms
        grad_resid[at, :] = back
        own[at, :] = back.astype(bf16)

    each_rows(own_rows, 16, body)
    gain_grad[...] = jnp.sum(total[...], axis=0, keepdims=True)
    loads[5].wait()

    def gated_unit(n, carry):
        units[n] = dot(own[...], w_out[n].reshape(width, -1)).astype(bf16)
        return carry

    lax.fori_loop(0, 8, gated_unit, 0)
    exchanged = [
        copies.send(units.at[tensor.slot(*step)], gated_in.at[tensor.t], device)
        for step, device in zip(tensor.steps, tensor.others)
    ]
    gated_in[tensor.t] = units[tensor.t]
    for _ in weight_steps:
        pass
    for copy in exchanged:
        copy.wait_recv()
    for n in range(8):
        grad_gated[n * own_rows : (n + 1) * own_rows, :] = gated_in[n]
    for copy in exchanged:
        copy.wait_send()
    for copy in kept:
        copy.wait()


def mlp(resid, grad_final, gain, normed, low, weights, w_out):
    own_rows, width = resid.shape
    rows = normed.shape[0]
    ff = weights[0].shape[1]
    cols = w_out.shape[3]
    depth = width // 16
    shape = jax.ShapeDtypeStruct
    return pl.pallas_call(
        mlp_kernel,
        out_shape=[
            shape((rows, width), bf16),
            shape((width, ff), bf16),
            shape((width, ff), bf16),
            shape((depth, ff), f32),
            shape((own_rows, width), f32),
            shape((rows, cols), bf16),
            shape((1, width), f32),
        ],
        in_specs=[VM] * 3 + [ANY] * 6,
        out_specs=[ANY] * 3 + [VM] * 4,
        scratch_shapes=[pltpu.VMEM((rows, width), bf16)] * 2
        + [pltpu.VMEM((width, ff), bf16)] * 3
        + [pltpu.VMEM(w_out.shape, bf16)]
        + [pltpu.VMEM((rows, ff), bf16)] * 3
        + [pltpu.VMEM((rows, width), bf16)] * 2
        + [pltpu.VMEM((width, ff), bf16)] * 3
        + [
            pltpu.VMEM((own_rows, width), bf16),
            pltpu.VMEM((16, width), f32),
            pltpu.VMEM((8, own_rows, cols), bf16),
            pltpu.VMEM((8, own_rows, cols), bf16),
        ]
        + reduce_scratch(own_rows, width // 2, False) * 2
        + reduce_scratch(depth, ff, True)
        + sems(64, 12),
        name="mlp",
        compiler_params=params(2, 62),
    )(resid, grad_final, gain, normed, low, *weights, w_out)


def attention_kernel(
    scale,
    queries,
    lse,
    attended,
    gate_raw,
    grad_gated,
    grad_resid,
    resid,
    kv_in,
    down_in,
    up_in,
    grad_query,
    kv_grad,
    gate_grad,
    low,
    final,
    up_grad,
    kv_all,
    down,
    up_part,
    own,
    grad_att,
    query_t,
    grad_t,
    delta,
    acc,
    dkv,
    down_sum,
    *rest,
):
    scratch_kv, scratch_d, scratch_w = rest[:6], rest[6:11], rest[11:17]
    copies = Copies(*rest[17:])
    tensor, batch = Group("tensor", False), Group("batch")
    b = lax.axis_index("batch")
    seqs, head_rows, head = queries.shape
    rows, cols = attended.shape
    seq_dev = rows // seqs
    heads = cols // head
    own_rows, width = resid.shape
    depth = up_grad.shape[0]
    factor = scale * math.log2(math.e)
    loads = [copies.local(a, c) for a, c in ((up_in, up_part), (down_in, down), (kv_in, kv_all))]
    enter(near(tensor, batch))

    def round_own(at):
        own[at, :] = grad_resid[at, :].astype(bf16)

    each_rows(own_rows, 16, round_own)
    low_steps = gather(
        copies, tensor, own, lambda s: unit_rows(low, s, own_rows), by_mate=False
    )
    next(low_steps)
    loads[0].wait()
    up_steps = reduce(
        copies, batch, row_unit(batch, up_part, depth), scratch_w, up_grad, by_mate=False
    )
    next(up_steps)
    for s in range(seqs):
        at = pl.ds(s * seq_dev, seq_dev)
        for h in range(heads):
            here, there = pl.ds(h * head, head), pl.ds(h * seq_dev, seq_dev)
            sigma = jax.nn.sigmoid(gate_raw[at, here])
            value = grad_gated[at, here].astype(f32)
            out = attended[at, here]
            low_grad = (value * sigma).astype(bf16)
            grad_att[s, there, :] = low_grad
            gate_grad[at, here] = (value * out * (sigma * (1.0 - sigma))).astype(bf16)
            acc[s, there, :] = low_grad.astype(f32) * out
        delta[s] = jnp.sum(acc[s].T, axis=0, keepdims=True)
        grad_t[s] = grad_att[s].astype(f32).T.astype(bf16)
        query_t[s] = queries[s].astype(f32).T.astype(bf16)
    for s in range(seqs):
        acc_t = acc.at[s]
        acc_t[...] = jnp.zeros_like(acc_t)
    loads[1].wait()
    loads[2].wait()

    def block(slot, masked):
        for s in range(seqs):
            at = pl.ds(s * seq_dev, seq_dev)
            keys = kv_all[slot, at, :head]
            values = kv_all[slot, at, head:]
            probs = jnp.exp2(dot(keys, query_t[s]) * factor - lse[s])
            if masked:
                key = lax.broadcasted_iota(jnp.int32, probs.shape, 0)
                col = lax.broadcasted_iota(jnp.int32, probs.shape, 1)
                row = jnp.where(col >= seq_dev, col - seq_dev, col)
                probs = jnp.where(key <= row, probs, 0.0)
            grad_probs = dot(values, grad_t[s])
            grad_scores = (probs * (grad_probs - delta[s])).astype(bf16)
            dkv[slot, at, :head] = (dot(grad_scores, queries[s]) * scale).astype(bf16)
            dkv[slot, at, head:] = dot(probs.astype(bf16), grad_att[s]).astype(bf16)
            acc[s] += t_dot(grad_scores, keys)

    def pair(chip, own_pair):
        def one(n, carry):
            slot = chip * 2 + n

            @pl.when(slot < b)
            def _():
                block(slot, False)

            if own_pair:

                @pl.when(slot == b)
                def _():
                    block(slot, True)

            @pl.when(slot > b)
            def _():
                dkv[slot] = jnp.zeros(dkv.shape[1:], bf16)

            return carry

        lax.fori_loop(0, 2, one, 0)

    kv_steps = reduce(
        copies,
        batch,
        lambda dr, dq, dc: dkv.at[batch.slot(dr, dq, dc)],
        scratch_kv,
        kv_grad,
        early=True,
    )
    down_steps = reduce(
        copies, tensor, row_unit(tensor, down, own_rows), scratch_d, down_sum, by_mate=False
    )
    beside = {
        0: [up_steps],
        1: [low_steps, up_steps],
        2: [down_steps, up_steps],
        3: [low_steps],
        4: [down_steps, up_steps],
        5: [low_steps],
        6: [down_steps, up_steps],
        7: [low_steps, down_steps],
    }
    for n, (dr, dq) in enumerate(ORDER):
        pair(batch.chip(dr, dq), (dr, dq) == (0, 0))
        next(kv_steps)
        for step in beside[n]:
            next(step, None)
    for s in range(seqs):
        for h in range(heads):
            grad_query[s * seq_dev : (s + 1) * seq_dev, h * head : (h + 1) * head] = (
                acc[s, h * seq_dev : (h + 1) * seq_dev, :] * scale
            )
    run_all(kv_steps, down_steps, low_steps, up_steps)
    add_rows(final, [down_sum, resid])


def attention_back(
    scale, queries, lse, attended, gate_raw, grad_gated, grad_resid, resid, kv_all, down, up_part
):
    rows, cols = attended.shape
    own_rows, width = resid.shape
    seqs, head_rows, head = queries.shape
    ff = up_part.shape[1]
    depth = width // 16
    shape = jax.ShapeDtypeStruct
    return pl.pallas_call(
        functools.partial(attention_kernel, scale),
        out_shape=[
            shape((rows, cols), f32),
            shape((rows, cols), f32),
            shape((rows, cols), bf16),
            shape((rows, width), bf16),
            shape((own_rows, width), bf16),
            shape((depth, ff), f32),
        ],
        in_specs=[VM] * 7 + [ANY] * 3,
        out_specs=[VM] * 3 + [ANY] + [VM] * 2,
        scratch_shapes=[
            pltpu.VMEM(kv_all.shape, bf16),
            pltpu.VMEM((rows, width), bf16),
            pltpu.VMEM((width, ff), bf16),
            pltpu.VMEM((own_rows, width), bf16),
            pltpu.VMEM(queries.shape, bf16),
            pltpu.VMEM((seqs, head, head_rows), bf16),
            pltpu.VMEM((seqs, head, head_rows), bf16),
            pltpu.VMEM((seqs, 1, head_rows), f32),
            pltpu.VMEM(queries.shape, f32),
            pltpu.VMEM(kv_all.shape, bf16),
            pltpu.VMEM((own_rows, width), f32),
        ]
        + reduce_scratch(rows, cols, True)
        + reduce_scratch(own_rows, width, False)
        + reduce_scratch(depth, ff, True)
        + sems(72, 6),
        name="attention_back",
        compiler_params=params(3, 62),
    )(queries, lse, attended, gate_raw, grad_gated, grad_resid, resid, kv_all, down, up_part)


def last_kernel(
    grad_query,
    kv_grad,
    gate_grad,
    query_raw,
    kv_raw,
    cosine,
    sine,
    gain_wide,
    gain_head,
    inputs,
    grad_resid,
    final,
    gated,
    norm_mlp_grad,
    normed_in,
    low_in,
    kvo_in,
    qg_in,
    down_in,
    tokens,
    output,
    query_grad,
    key_grad,
    value_grad,
    gate_out_grad,
    out_grad,
    down_grad,
    norm_attn_grad,
    norm_mlp_out,
    gain_query_grad,
    gain_key_grad,
    normed,
    low,
    w_kvo,
    w_qg,
    down_part,
    weight_grad,
    down_sum,
    qg_low,
    kv_low,
    part,
    weight_part,
    held,
    own,
    total,
    mine,
    over_tensor,
    shares,
    over_batch,
    *rest,
):
    scratch, scratch_w, scratch_d = rest[:5], rest[5:11], rest[11:17]
    copies = Copies(*rest[17:])
    tensor, batch = Group("tensor", False), Group("batch")
    rows, width = normed.shape
    own_rows = inputs.shape[0]
    cols = grad_query.shape[1]
    head = gain_head.shape[1]
    seq_dev = cosine.shape[0]
    depth = weight_grad.shape[0]
    loads = [
        copies.local(a, c)
        for a, c in (
            (qg_in, w_qg),
            (kvo_in, w_kvo),
            (down_in, down_part),
            (normed_in, normed),
            (low_in, low),
        )
    ]
    b = lax.axis_index("batch")
    members = [(0, dq, dr, dc) for dc in range(2) for dq, dr in [(0, 0)] + batch_steps(batch)][1:]
    batch_others = [(batch.slot(dr, dq, dc), batch.t) for _, dq, dr, dc in members]
    enter(tensor.others + batch_others)

    def place(ref):
        def unit(slot):
            seq, rest = lax.div(slot, 4), lax.rem(slot, 4)
            return ref.at[seq, pl.ds(pl.multiple_of(rest * own_rows, 16), own_rows), :]

        return unit

    output_steps = gather(copies, tensor, final, place(output))
    next(output_steps)

    def head_back(raw, gain, grad, at):
        back = grad * cosine[...] - pltpu.roll(grad, head // 2, 1) * sine[...]
        values, terms = norm_back(raw, gain, back)
        return values.astype(bf16), jnp.sum(terms, axis=0, keepdims=True)

    mine[...] = jnp.zeros_like(mine)
    norm_rows = width // 128
    for s in range(rows // seq_dev):
        at = pl.ds(s * seq_dev, seq_dev)
        for h in range(cols // head):
            here = pl.ds(h * head, head)
            qg_low[at, here], terms = head_back(
                query_raw[at, here], gain_head[0:1, :], grad_query[at, here], at
            )
            mine[2 * norm_rows : 2 * norm_rows + 1, :] += terms
        kv_low[at, :head], terms = head_back(
            kv_raw[at, :head], gain_head[1:2, :], kv_grad[at, :head], at
        )
        mine[2 * norm_rows + 1 : 2 * norm_rows + 2, :] += terms
        kv_low[at, head:] = kv_grad[at, head:].astype(bf16)
        qg_low[at, cols:] = gate_grad[at, :]
    loads[0].wait()
    loads[1].wait()
    for n in range(4):
        slots = pl.ds(n * 4, 4)
        value = dot_t(qg_low[...], w_qg[slots].reshape(width // 4, 2 * cols))
        value += dot_t(kv_low[...], w_kvo[slots, :depth, :cols].reshape(width // 4, cols))
        part[:, n * (width // 4) : (n + 1) * (width // 4)] = value.astype(bf16)
    steps = reduce(copies, tensor, row_unit(tensor, part, own_rows), scratch, held)
    next(steps)
    loads[2].wait()
    down_steps = reduce(
        copies, batch, row_unit(batch, down_part, depth), scratch_d, down_sum, by_mate=False
    )
    next(down_steps)
    loads[3].wait()
    loads[4].wait()
    next(output_steps)
    outer(normed, qg_low, weight_part, slice(0, 2 * cols))
    next(steps)
    next(down_steps)
    outer(normed, kv_low, weight_part, slice(2 * cols, 3 * cols))
    outer(low, gated, weight_part, slice(3 * cols, 4 * cols))
    weight_steps = reduce(
        copies, batch, row_unit(batch, weight_part, depth), scratch_w, weight_grad, by_mate=False
    )
    next(weight_steps)
    for n in range(norm_rows):
        mine[norm_rows + n : norm_rows + n + 1, :] = norm_mlp_grad[:, n * 128 : (n + 1) * 128]

    share = gain_query_grad.shape[1]

    def small():
        first = [
            copies.send(mine, over_tensor.at[tensor.t], device) for device in tensor.others
        ]
        over_tensor[tensor.t] = mine[...]
        yield
        for copy in first:
            copy.wait_recv()
        total_t = over_tensor[0]
        for n in range(1, 8):
            total_t = total_t + over_tensor[n]
        for n in range(16):
            shares[n, 0:1, :] = total_t[n : n + 1]
            shares[n, 1:2, :] = total_t[norm_rows + n : norm_rows + n + 1]
            shares[n, 2:4, :] = total_t[2 * norm_rows : 2 * norm_rows + 2]
            shares[n, 4:8, :] = jnp.zeros((4, 128), f32)
        second = [
            copies.send(shares.at[batch.slot(dr, dq, dc)], over_batch.at[b], device)
            for (_, dq, dr, dc), device in zip(members, batch_others)
        ]
        over_batch[b] = shares[b]
        yield
        for copy in second:
            copy.wait_recv()
        total_b = over_batch[0]
        for n in range(1, 16):
            total_b = total_b + over_batch[n]
        norm_attn_grad[...] = total_b[0:1]
        norm_mlp_out[...] = total_b[1:2]
        heads_own = pltpu.roll(total_b, (128 - share * b) % 128, 1)
        gain_query_grad[...] = heads_own[2:3, 0:share]
        gain_key_grad[...] = heads_own[3:4, 0:share]
        for copy in first + second:
            copy.wait_send()

    def along():
        yield from steps
        total[...] = jnp.zeros_like(total)

        def body(at):
            back, terms = norm_back(
                inputs[at, :].astype(f32), gain_wide[0:1, :], held[at, :]
            )
            total[...] += terms
            own[at, :] = (grad_resid[at, :] + back).astype(bf16)

        each_rows(own_rows, 16, body)
        gain_row = jnp.sum(total[...], axis=0, keepdims=True)
        for n in range(norm_rows):
            mine[n : n + 1, :] = gain_row[:, n * 128 : (n + 1) * 128]
        big = gather(copies, tensor, own, place(tokens))
        few = small()
        for _ in big:
            next(few, None)
            yield
        yield from few

    run_all(output_steps, along(), down_steps, weight_steps)
    query_grad[...] = weight_grad[:, :cols]
    gate_out_grad[...] = weight_grad[:, cols : 2 * cols]
    key_grad[...] = weight_grad[:, 2 * cols : 2 * cols + head]
    value_grad[...] = weight_grad[:, 2 * cols + head : 3 * cols]
    out_grad[...] = weight_grad[:, 3 * cols :].T
    down_grad[...] = down_sum[...].T


def batch_steps(batch):
    return [(dq, dr) for dr, dq in batch.steps]


def last_step(scale_free, held_in_hbm, few_shape, share):
    grad_query, inputs = scale_free[0], scale_free[9]
    seqs = grad_query.shape[0] // scale_free[5].shape[0]
    normed, low, kvo, qg, down_part = held_in_hbm
    own_rows, width = inputs.shape
    rows, cols = grad_query.shape
    ff = down_part.shape[1]
    depth = width // 16
    shape = jax.ShapeDtypeStruct
    return pl.pallas_call(
        last_kernel,
        out_shape=[
            shape((seqs, rows // seqs, width), bf16),
            shape((seqs, rows // seqs, width), bf16),
            shape((depth, cols), f32),
            shape((depth, cols // 2), f32),
            shape((depth, cols // 2), f32),
            shape((depth, cols), f32),
            shape((cols, depth), f32),
            shape((ff, depth), f32),
            shape((1, depth), f32),
            shape((1, depth), f32),
            shape((1, share), f32),
            shape((1, share), f32),
        ],
        in_specs=[VM] * len(scale_free) + [ANY] * len(held_in_hbm),
        out_specs=[ANY] * 2 + [VM] * 10,
        scratch_shapes=[
            pltpu.VMEM((rows, width), bf16),
            pltpu.VMEM((rows, width), bf16),
            pltpu.VMEM(kvo.shape, bf16),
            pltpu.VMEM(qg.shape, bf16),
            pltpu.VMEM((width, ff), bf16),
            pltpu.VMEM((depth, 4 * cols), f32),
            pltpu.VMEM((depth, ff), f32),
            pltpu.VMEM((rows, 2 * cols), bf16),
            pltpu.VMEM((rows, cols), bf16),
            pltpu.VMEM((rows, width), bf16),
            pltpu.VMEM((width, 4 * cols), bf16),
            pltpu.VMEM((own_rows, width), f32),
            pltpu.VMEM((own_rows, width), bf16),
            pltpu.VMEM((16, width), f32),
            pltpu.VMEM(few_shape, f32),
            pltpu.VMEM((8,) + few_shape, f32),
            pltpu.VMEM((16, 8, 128), f32),
            pltpu.VMEM((16, 8, 128), f32),
        ]
        + reduce_scratch(own_rows, width, False)
        + reduce_scratch(depth, 4 * cols, True)
        + reduce_scratch(depth, ff, True)
        + sems(120, 12),
        name="projections_back",
        compiler_params=params(4, 62),
    )(*scale_free, *held_in_hbm)


def shards(
    tokens,
    target,
    domain_ids,
    domain_counts,
    weight_index,
    loss_weights,
    w_query,
    w_key,
    w_value,
    w_gate_out,
    w_output,
    w_gate,
    w_up,
    w_down,
    norm_attn,
    norm_mlp,
    gain_query,
    gain_key,
):
    seq_count, seq_dev, width = tokens.shape
    rows = seq_count * seq_dev
    members = lax.axis_size("tensor")
    batch_count = lax.axis_size("batch")
    b, t = lax.axis_index("batch"), lax.axis_index("tensor")
    own_rows = rows // members
    seq_len = seq_dev * batch_count
    head = gain_query.shape[0] * batch_count
    scale = head ** (-0.5)
    q_cols, k_cols = w_query.shape[1], w_key.shape[1]
    heads = q_cols // head

    half_size = head // 2
    pos_local = (b * seq_dev + jnp.arange(seq_dev, dtype=jnp.int32)).astype(f32)
    inverse_freq = rope_base ** (-jnp.arange(half_size, dtype=f32) / half_size)
    angles = pos_local[:, None] * inverse_freq[None, :]
    cosine, sine = jnp.cos(angles), jnp.sin(angles)
    cosine_wide = jnp.concatenate([cosine, cosine], axis=1)
    sine_wide = jnp.concatenate([-sine, sine], axis=1)

    domain_range = jnp.arange(domain_counts.shape[0], dtype=jnp.int32)
    level_pick = (
        weight_index[:, None] == jnp.arange(loss_weights.shape[0], dtype=jnp.int32)[None, :]
    ).astype(f32)
    domain_factor = (
        jnp.sum(level_pick * loss_weights[None, :], axis=1) * seq_len / domain_counts.astype(f32)
    )
    seq_pick = (domain_ids[:, None] == domain_range[None, :]).astype(f32)
    seq_weight = jnp.sum(seq_pick * domain_factor[None, :], axis=1)
    tokens_low = tokens.reshape(rows, width)
    ff = w_gate.shape[1]
    (
        normed_low,
        query_raw,
        kv_raw,
        gate_raw,
        queries,
        kv_all,
        attended,
        lse,
        gated_low,
        normed_mlp_low,
        resid_own,
        wide_kvo,
        wide_qg,
        w_out_all,
        wide_gate,
        wide_up,
        wide_down,
        gain_wide,
        gain_head,
        inputs_own,
        grad_final_own,
        grad_final_low,
    ) = forward(
        scale,
        seq_count,
        (
            tokens_low,
            cosine_wide,
            sine_wide,
            jnp.broadcast_to(seq_weight[:, None], (seq_count, 128)),
            norm_attn[None],
            norm_mlp[None],
            gain_query[None],
            gain_key[None],
            w_output,
            w_down,
        ),
        (w_query, w_key, w_value, w_gate_out, w_gate, w_up),
        target.reshape(rows, width),
    )

    weights = [w.reshape(width, ff) for w in (wide_gate, wide_up, wide_down)]
    (
        down_part,
        up_weight_part,
        down_weight_part,
        grad_gate,
        grad_resid_own,
        grad_gated,
        norm_mlp_terms,
    ) = mlp(
        resid_own,
        grad_final_own,
        gain_wide,
        normed_mlp_low,
        grad_final_low,
        weights,
        w_out_all,
    )
    grad_query_rot, kv_grad, gate_raw_grad, grad_resid_low, final_own, grad_up = attention_back(
        scale,
        queries,
        lse,
        attended,
        gate_raw,
        grad_gated,
        grad_resid_own,
        resid_own,
        kv_all,
        down_part,
        up_weight_part,
    )
    norm_rows = width // 128
    grad_tokens, output, *grads = last_step(
        (
            grad_query_rot,
            kv_grad,
            gate_raw_grad,
            query_raw,
            kv_raw,
            cosine_wide,
            sine_wide,
            gain_wide,
            gain_head,
            inputs_own,
            grad_resid_own,
            final_own,
            gated_low,
            norm_mlp_terms,
        ),
        (normed_low, grad_resid_low, wide_kvo, wide_qg, down_weight_part),
        (2 * norm_rows + 8, 128),
        gain_query.shape[0],
    )

    return (
        output,
        grad_tokens.astype(f32),
        *grads[:5],
        grad_gate,
        grad_up,
        grads[5],
        *[g.reshape(-1) for g in grads[6:]],
    )


def solution(mesh):
    in_specs = (
        P(None, "batch", None),
        P(None, "batch", None),
        P(),
        P(),
        P(),
        P(),
        P("batch", "tensor"),
        P("batch", "tensor"),
        P("batch", "tensor"),
        P("batch", "tensor"),
        P("tensor", "batch"),
        P("batch", "tensor"),
        P("batch", "tensor"),
        P("tensor", "batch"),
        P("batch"),
        P("batch"),
        P("batch"),
        P("batch"),
    )
    out_specs = (
        P(None, "batch", None),
        P(None, "batch", None),
        P("batch", "tensor"),
        P("batch", "tensor"),
        P("batch", "tensor"),
        P("batch", "tensor"),
        P("tensor", "batch"),
        P("batch", "tensor"),
        P("batch", "tensor"),
        P("tensor", "batch"),
        P("batch"),
        P("batch"),
        P("batch"),
        P("batch"),
    )
    return jax.shard_map(shards, mesh=mesh, in_specs=in_specs, out_specs=out_specs, check_vma=False)
```

```python
import functools
import math

import jax
import jax.numpy as jnp
from jax import lax
from jax.experimental import pallas as pl
from jax.experimental.pallas import tpu as pltpu
from jax.sharding import PartitionSpec as P

MESH = pl.DeviceIdType.MESH
epsilon = 1e-06
rope_base = 1000000.0
f32 = jnp.float32
bf16 = jnp.bfloat16

FORWARD_ORDER = "ntwntwnmtnwtntDFXwabcWRE"
MLP_ORDER = "GxUxwDxwR"
ATTENTION_ORDER = "PkuPklPkduPkPkdluPkPkduPkkkkkld"
LAST_ORDER = "oxdw" * 12

MIB = 2**20
ANY = pl.BlockSpec(memory_space=pl.ANY)
VM = pl.BlockSpec(memory_space=pltpu.VMEM)
SM = pl.BlockSpec(memory_space=pltpu.SMEM)


class Group:
    def __init__(self, kind, core=True):
        b = lax.axis_index("batch")
        t = lax.axis_index("tensor")
        c = lax.rem(b, 2)
        self.c, self.t = c, t
        if kind == "tensor":
            r, q = lax.div(t, 2), lax.rem(t, 2)
            self.slot = lambda dr, dq: lax.rem(r + dr, 4) * 2 + lax.rem(q + dq, 2)
            at = lambda dr, dq: (b, self.slot(dr, dq))
        else:
            q, r = lax.div(b, 8), lax.rem(lax.div(b, 2), 4)
            self.chip = lambda dr, dq: lax.rem(q + dq, 2) * 4 + lax.rem(r + dr, 4)
            self.slot = lambda dr, dq, dc=0: self.chip(dr, dq) * 2 + lax.rem(c + dc, 2)
            at = lambda dr, dq: (self.slot(dr, dq), t)
        self.core = (b + 1 - 2 * c, t) if core else None
        self.right, self.left, self.mate = at(1, 0), at(3, 0), at(0, 1)
        self.others = [at(dr, dq) for dr in range(4) for dq in range(2) if dr or dq]
        self.steps = [(dr, dq) for dr in range(4) for dq in range(2) if dr or dq]


def enter(devices):
    barrier = pltpu.get_barrier_semaphore()
    for device in devices:
        pl.semaphore_signal(barrier, inc=1, device_id=device, device_id_type=MESH)
    pl.semaphore_wait(barrier, len(devices))


def near(*groups):
    devices = [d for g in groups for d in (g.right, g.left, g.mate)]
    cores = [g.core for g in groups if g.core is not None]
    return devices + cores[:1]


class Copies:
    def __init__(self, send_sem, recv_sem, local_sem):
        self.send_sem, self.recv_sem, self.local_sem = send_sem, recv_sem, local_sem
        self.count = 0
        self.locals = 0

    def send(self, source, target, device):
        copy = pltpu.make_async_remote_copy(
            src_ref=source,
            dst_ref=target,
            send_sem=self.send_sem.at[self.count],
            recv_sem=self.recv_sem.at[self.count],
            device_id=device,
            device_id_type=MESH,
        )
        self.count += 1
        copy.start()
        return copy

    def local(self, source, target):
        copy = pltpu.make_async_copy(source, target, self.local_sem.at[self.locals])
        self.locals += 1
        copy.start()
        return copy


def half_of(ref, which):
    width = ref.shape[-1] // 2
    lead = (slice(None),) * (len(ref.shape) - 1)
    return ref.at[lead + (pl.ds(which * width, width),)]


def run_all(*steps):
    waiting = list(steps)
    while waiting:
        for step in list(waiting):
            try:
                next(step)
            except StopIteration:
                waiting.remove(step)


def gather(copies, group, own, slot, split=True, source=None, by_mate=True):
    s = group.slot
    core_copies = []
    sent = []

    def push(ref, *devices):
        out = [copies.send(ref, ref, device) for device in devices]
        sent.extend(out)
        return out

    def to_core(ref):
        if group.core is not None:
            core_copies.extend(push(ref, group.core))

    def core_wait(count):
        for copy in core_copies[:count]:
            copy.wait_recv()
        del core_copies[:count]

    def onward(unit, way):
        if way == 0:
            return push(half_of(unit, 0) if split else unit, group.right)
        return push(half_of(unit, 1), group.left) if split else []

    home = slot(s(0, 0))
    source = own if source is None else source
    first = [copies.send(source, home, d) for d in (group.right, group.left, group.mate)]
    sent.extend(first)
    kept = None
    if own is not None:
        kept = copies.local(own, home)
        if group.core is not None:
            core_copies.append(copies.send(own, home, group.core))
            sent.append(core_copies[0])
    from_left, from_right, from_mate = first
    yield []
    far = []
    for way, copy in enumerate((from_left, from_right)):
        copy.wait_recv()
        unit = slot(s(3 - 2 * way, 0))
        far += onward(unit, way)
        to_core(unit)
    from_mate.wait_recv()
    mate_unit = slot(s(0, 1))
    mate_line = push(mate_unit, group.right, group.left)
    to_core(mate_unit)
    if own is not None:
        core_wait(1)
        kept.wait()
    yield [(0, 0)]
    mate_far = []
    for copy in far:
        copy.wait_recv()
    if by_mate:
        mate_far += push(slot(s(2, 0)), group.mate)
    to_core(slot(s(2, 0)))
    yield []
    for way, copy in enumerate(mate_line):
        copy.wait_recv()
        unit = slot(s(3 - 2 * way, 1))
        if not by_mate:
            mate_far += onward(unit, way)
        to_core(unit)
    core_wait(3)
    yield [(3, 0), (1, 0), (0, 1)]
    for copy in mate_far:
        copy.wait_recv()
    to_core(slot(s(2, 1)))
    core_wait(3)
    yield [(2, 0), (3, 1), (1, 1)]
    core_wait(1)
    yield [(2, 1)]
    for copy in sent:
        copy.wait_send()


def chunk(ref, n, count):
    width = ref.shape[-1] // count
    return ref.at[:, pl.ds(n * width, width)]


def lockstep(steps):
    waiting = list(steps)
    while waiting:
        for step in list(waiting):
            try:
                next(step)
            except StopIteration:
                waiting.remove(step)
        yield


def add_rows(target, sources, step=16):
    def body(at):
        total = sources[0][at, :].astype(f32)
        for source in sources[1:]:
            total = total + source[at, :].astype(f32)
        target[at, :] = total.astype(target.dtype)

    each_rows(target.shape[0], step, body)


def rows_at(i, step=16):
    return pl.ds(pl.multiple_of(i * step, step), step)


def each_rows(rows, step, body):
    def run(i, carry):
        body(rows_at(i, step))
        return carry

    lax.fori_loop(0, rows // step, run, 0)


def reduce_scratch(rows, width, core):
    shapes = [
        pltpu.VMEM((4, rows, width // 2), bf16),
        pltpu.VMEM((4, rows, width), bf16),
        pltpu.VMEM((4, rows, width), bf16),
        pltpu.VMEM((3, rows, width), bf16),
        pltpu.VMEM((2, rows, width), bf16),
    ]
    if core:
        shapes += [pltpu.VMEM((8, rows, width), bf16)]
    return shapes


ORDER = [(2, 1), (1, 1), (3, 1), (2, 0), (1, 0), (3, 0), (0, 1), (0, 0)]


def reduce(copies, group, part, scratch, result, early=False, by_mate=True):
    far, near_in, outgoing, mates, far_sums = scratch[:5]
    core = group.core is not None
    sent = []

    def send(source, target, device):
        copy = copies.send(source, target, device)
        sent.append(copy)
        return copy

    arrived = {}

    def to_core(n):
        dr, dq = ORDER[n]
        arrived[dr, dq] = (send(part(dr, dq, 1), scratch[5].at[n], group.core), n)

    def terms(dr, dq):
        if not core:
            return [part(dr, dq)]
        copy, n = arrived[dr, dq]
        copy.wait_recv()
        return [part(dr, dq, 0), scratch[5].at[n]]

    sides = ((1, group.right), (3, group.left))

    def far_sends(unit, line):
        return [
            send(half_of(unit, way), far.at[line * 2 + way], device)
            for way, (_, device) in enumerate(sides)
        ]

    def line_sends(line, far_copies):
        out = []
        for way, (dr, device) in enumerate(sides):
            unit = terms(dr, line)
            held = outgoing.at[line * 2 + way]
            if far_copies is not None:
                far_copies[way].wait_recv()
                there = far.at[line * 2 + way]
                add_rows(half_of(held, way), [half_of(u, way) for u in unit] + [there])
                add_rows(half_of(held, 1 - way), [half_of(u, 1 - way) for u in unit])
            elif core:
                add_rows(held, unit)
            else:
                held = unit[0]
            out.append(send(held, near_in.at[line * 2 + way], device))
        return out

    def first():
        unit = terms(2, 1)
        if core:
            add_rows(far_sums.at[1], unit)
            unit = [far_sums.at[1]]
        if by_mate:
            return send(unit[0], mates.at[2], group.mate), line_sends(1, None)
        return None, far_sends(unit[0], 1)

    def second():
        unit = terms(2, 0)
        if by_mate:
            far_mate.wait_recv()
            unit = unit + [mates.at[2]]
        if len(unit) > 1:
            add_rows(far_sums.at[0], unit)
            unit = [far_sums.at[0]]
        return far_sends(unit[0], 0)

    def third():
        return line_sends(0, far_copies)

    if early:
        for n in range(3):
            to_core(n)
            yield
        to_core(3)
        far_mate, mate_line = first()
        yield
        to_core(4)
        far_copies = second()
        yield
        to_core(5)
        yield
        to_core(6)
        own_line = third()
        yield
        to_core(7)
    else:
        if core:
            for n in range(8):
                to_core(n)
            yield
        far_mate, mate_line = first()
        yield
        far_copies = second()
        yield
        if not by_mate:
            mate_line = line_sends(1, mate_line)
        own_line = third()
    yield
    unit = terms(0, 1)
    for copy in mate_line:
        copy.wait_recv()
    add_rows(mates.at[0], unit + [near_in.at[2], near_in.at[3]])
    to_mate = send(mates.at[0], mates.at[1], group.mate)
    yield
    unit = terms(0, 0)
    for copy in own_line:
        copy.wait_recv()
    to_mate.wait_recv()
    add_rows(result, unit + [near_in.at[0], near_in.at[1], mates.at[1]])
    for copy in sent:
        copy.wait_send()


def sems(remote, local):
    return [
        pltpu.SemaphoreType.DMA((remote,)),
        pltpu.SemaphoreType.DMA((remote,)),
        pltpu.SemaphoreType.DMA((max(local, 1),)),
    ]


def params(collective, limit=48):
    return pltpu.CompilerParams(
        collective_id=collective, has_side_effects=True, vmem_limit_bytes=limit * MIB
    )


def prepare_head(values, gain, cosine, sine):
    half_size = values.shape[1] // 2
    mean = jnp.mean(values * values, axis=-1, keepdims=True)
    scaled = values * lax.rsqrt(mean + epsilon) * gain
    return scaled * cosine + pltpu.roll(scaled, half_size, 1) * sine


def forward_kernel(
    scale,
    tokens,
    cosine,
    sine,
    domain_ids,
    domain_counts,
    weight_index,
    loss_weights,
    norm_attn,
    norm_mlp,
    gain_query,
    gain_key,
    w_output,
    w_down,
    w_query,
    w_key,
    w_value,
    w_gate_out,
    mlp_a,
    mlp_b,
    target_in,
    normed_out,
    query_raw,
    kv_raw,
    gate_raw,
    queries,
    kv_out,
    attended,
    lse,
    gated,
    normed_mlp,
    resid,
    wide_kvo,
    wide_qg,
    w_out_out,
    wide_a,
    wide_b,
    wide_c,
    gain_wide,
    gain_head,
    inputs_own,
    grad_final,
    low_out,
    normed,
    inverse,
    pack_a,
    pack_b,
    mlp_c,
    few,
    target,
    low,
    w_kvo,
    w_qg,
    w_out,
    kv_own,
    kv_all,
    acc,
    rows_all,
    own,
    send_sem,
    recv_sem,
    local_sem,
):
    copies = Copies(send_sem, recv_sem, local_sem)
    tensor, batch = Group("tensor"), Group("batch")
    b = lax.axis_index("batch")
    rows, width = tokens.shape
    cols = query_raw.shape[1]
    own_rows = resid.shape[0]
    seqs, head_rows, head = queries.shape
    heads = query_raw.shape[1] // head
    seq_dev = rows // seqs
    depth, key_cols = w_key.shape
    packing = [
        copies.local(source, place)
        for source, place in (
            (w_key, pack_a.at[pl.ds(0, depth), pl.ds(0, key_cols)]),
            (w_value, pack_a.at[pl.ds(0, depth), pl.ds(key_cols, key_cols)]),
            (w_query, pack_b.at[:, pl.ds(0, cols)]),
            (w_gate_out, pack_b.at[:, pl.ds(cols, cols)]),
        )
    ]
    target_load = copies.local(target_in, target)

    def flipped(values):
        return values.astype(f32).T.astype(bf16)

    pack_a[0:depth, cols:] = flipped(w_output[...])
    few[...] = jnp.zeros_like(few)
    share = gain_query.shape[1]
    few[0:1, :] = norm_attn[...].astype(f32)
    few[1:2, :] = norm_mlp[...].astype(f32)
    few[2:3, 0:share] = gain_query[...].astype(f32)
    few[3:4, 0:share] = gain_key[...].astype(f32)
    placed = pltpu.roll(few[...], b * share, 1)
    row = lax.broadcasted_iota(jnp.int32, placed.shape, 0)
    pack_a[depth:, :] = jnp.zeros((16, pack_a.shape[1]), bf16)
    pack_a[depth:, 0:128] = jnp.where(row < 2, few[...], placed).astype(bf16)
    enter(tensor.others + near(batch))

    def batch_gather(source, target, by_mate=True):
        return gather(copies, batch, source, lambda s: target.at[s], by_mate=by_mate)

    for copy in packing:
        copy.wait()
    a_steps = batch_gather(pack_a, w_kvo, True)
    b_steps = batch_gather(pack_b, w_qg, False)
    next(a_steps)
    next(b_steps)

    def invert(at):
        values = tokens[at, :].astype(f32)
        mean = jnp.mean(values * values, axis=-1, keepdims=True)
        inverse[at, :] = jnp.broadcast_to(lax.rsqrt(mean + epsilon), (32, 128))

    each_rows(rows, 32, invert)
    mlp_c[...] = flipped(w_down[...])
    next(a_steps)
    next(b_steps)
    for _ in a_steps:
        pass
    half = tensor.c * 8
    kept = [copies.local(w_kvo, wide_kvo)]
    out_home = copies.local(w_kvo.at[:, pl.ds(0, depth), pl.ds(cols, cols)], w_out.at[tensor.t])
    wide_out_steps = gather(
        copies,
        tensor,
        None,
        lambda s: w_out.at[s, pl.ds(half, 8)],
        source=w_kvo.at[pl.ds(half, 8), pl.ds(0, depth), pl.ds(cols, cols)],
        by_mate=False,
    )
    next(wide_out_steps)
    gain_wide[...] = jnp.zeros_like(gain_wide)
    gain_head[...] = jnp.zeros_like(gain_head)
    total = jnp.zeros((16, 128), f32)
    for n in range(16):
        entry = w_kvo[n, depth:, 0:128].astype(f32)
        gain_wide[0:2, n * 128 : (n + 1) * 128] = entry[0:2]
        total = total + entry
    gain_head[0:2, :] = total[2:4]

    def normalise(at):
        scaled = tokens[at, :].astype(f32) * inverse[at, 0:1] * gain_wide[0:1, :]
        normed[at, :] = scaled.astype(bf16)

    each_rows(rows, 32, normalise)
    kept.append(copies.local(normed, normed_out))

    def project(weights, at):
        return jnp.dot(normed[at, :], weights.reshape(width, cols), preferred_element_type=f32)

    for s in range(seqs):
        at = pl.ds(s * seq_dev, seq_dev)
        raw = project(w_kvo[:, 0:depth, 0:cols], at)
        kv_raw[at, :] = raw
        key = prepare_head(raw[:, :head], gain_head[1:2, :], cosine[...], sine[...])
        kv_own[at, :head] = key.astype(bf16)
        kv_own[at, head:] = raw[:, head:].astype(bf16)
    all_steps = batch_gather(kv_own, kv_all, True)
    next(all_steps)
    for _ in b_steps:
        pass
    kept.append(copies.local(w_qg, wide_qg))
    for s in range(seqs):
        at = pl.ds(s * seq_dev, seq_dev)
        raw = project(w_qg[:, :, 0:cols], at)
        query_raw[at, :] = raw
        for h in range(heads):
            values = prepare_head(
                raw[:, h * head : (h + 1) * head], gain_head[0:1, :], cosine[...], sine[...]
            )
            queries[s, h * seq_dev : (h + 1) * seq_dev, :] = values.astype(bf16)
        gate_raw[at, :] = project(w_qg[:, :, cols:], at)

    target_load.wait()
    seq_weights = []
    for s in range(seqs):
        domain = domain_ids[s]
        level = jnp.full((1, 128), loss_weights[weight_index[domain]], f32)
        count = jnp.full((1, 128), domain_counts[domain], jnp.int32).astype(f32)
        seq_weights.append((level * (16 * seq_dev) / count)[:, 0:1])

        def weigh(at):
            at = pl.ds(s * seq_dev + at.start, at.size)
            low[at, :] = (target[at, :].astype(f32) * seq_weights[s]).astype(bf16)

        each_rows(seq_dev, 32, weigh)
    kept.append(copies.local(low, low_out))
    own_weight = jnp.where(tensor.t < 4, seq_weights[0], seq_weights[1])

    def weigh_own(at):
        there = pl.ds(pl.multiple_of(tensor.t * own_rows + at.start, 16), at.size)
        inputs_own[at, :] = tokens[there, :]
        grad_final[at, :] = target[there, :].astype(f32) * own_weight

    each_rows(own_rows, 16, weigh_own)
    factor = scale * math.log2(math.e)
    ones = jnp.ones((2 * seq_dev, head), bf16)
    tile = head_rows // 4
    acc[...] = jnp.zeros_like(acc)

    def block(pair, masked):
        def body(s, carry):
            at = rows_at(s, seq_dev)
            keys = jnp.concatenate(
                [kv_all[pair * 2, at, :head], kv_all[pair * 2 + 1, at, :head]], axis=0
            )
            values = jnp.concatenate(
                [kv_all[pair * 2, at, head:], kv_all[pair * 2 + 1, at, head:]], axis=0
            )
            wide = jnp.concatenate([values, ones], axis=1)
            for i in range(4):
                here = pl.ds(i * tile, tile)
                scores = lax.dot_general(
                    queries[s, here, :], keys, (((1,), (1,)), ((), ())), preferred_element_type=f32
                )
                weights = jnp.exp2(scores * factor)
                if masked:
                    row = lax.broadcasted_iota(jnp.int32, scores.shape, 0) + (i * tile) % seq_dev
                    col = lax.broadcasted_iota(jnp.int32, scores.shape, 1)
                    ahead = (pair * 2 - b) * seq_dev
                    weights = jnp.where(col + ahead <= row, weights, 0.0)
                acc[s, here, :] += jnp.dot(weights.astype(bf16), wide, preferred_element_type=f32)
            return carry

        lax.fori_loop(0, seqs, body, 0)

    here = batch.chip(0, 0)

    def attend(ready):
        for dr, dq in ready:
            if (dr, dq) == (0, 0):
                block(here, True)
            else:
                pair = batch.chip(dr, dq)

                @pl.when(pair < here)
                def _():
                    block(pair, False)

    mlp_steps = [
        batch_gather(mlp_a, wide_a, by_mate=False),
        batch_gather(mlp_b, wide_b, by_mate=False),
        batch_gather(mlp_c, wide_c, by_mate=False),
    ]

    def finish_attention():
        kept.append(copies.local(kv_all, kv_out))
        for s in range(seqs):
            sums = acc[s, :, head:]
            lse[s] = jnp.log2(sums).T[0:1, :]
            out = acc[s, :, :head] / sums
            for h in range(heads):
                at, cols = pl.ds(s * seq_dev, seq_dev), pl.ds(h * head, head)
                part = out[h * seq_dev : (h + 1) * seq_dev]
                attended[at, cols] = part
                gated[at, cols] = (part * jax.nn.sigmoid(gate_raw[at, cols])).astype(bf16)

    def unit_rows(ref, slot):
        return ref.at[pl.ds(pl.multiple_of(slot * own_rows, 16), own_rows), :]

    exchanged = []

    def exchange():
        for step, device in zip(tensor.steps, tensor.others):
            exchanged.append(
                copies.send(unit_rows(gated, tensor.slot(*step)), rows_all.at[tensor.t], device)
            )
        rows_all[tensor.t] = unit_rows(gated, tensor.t)[...]

    def wide_out_ready():
        for _ in wide_out_steps:
            pass
        out_home.wait()
        kept.append(copies.local(w_out, w_out_out))

    def project_out():
        for copy in exchanged:
            copy.wait_recv()
        resid[...] = unit_rows(tokens, tensor.t)[...].astype(f32)

        def out_term(n, carry):
            resid[...] += lax.dot_general(
                rows_all[n],
                w_out[n].reshape(width, -1),
                (((1,), (1,)), ((), ())),
                preferred_element_type=f32,
            )
            return carry

        lax.fori_loop(0, 8, out_term, 0)

        def normalise_own(at):
            values = resid[at, :]
            mean = jnp.mean(values * values, axis=-1, keepdims=True)
            own[at, :] = (values * lax.rsqrt(mean + epsilon) * gain_wide[1:2, :]).astype(bf16)

        each_rows(own_rows, 16, normalise_own)

    own_group = Group("tensor", False)
    own_steps = gather(copies, own_group, own, lambda s: unit_rows(normed_mlp, s))
    ready = []

    def arrive():
        ready[:] = next(all_steps)

    def drain():
        for _ in all_steps:
            pass

    do = {
        "n": arrive,
        "t": lambda: attend(ready),
        "w": lambda: next(wide_out_steps),
        "m": lambda: [next(step) for step in mlp_steps],
        "a": lambda: next(mlp_steps[0]),
        "b": lambda: next(mlp_steps[1]),
        "c": lambda: next(mlp_steps[2]),
        "D": drain,
        "F": finish_attention,
        "X": exchange,
        "W": wide_out_ready,
        "R": project_out,
        "E": lambda: run_all(own_steps, *mlp_steps),
    }
    for key in FORWARD_ORDER:
        do[key]()
    for copy in exchanged:
        copy.wait_send()
    for copy in kept:
        copy.wait()


def forward(scale, seqs, small, weights, target):
    tokens, cosine = small[:2]
    rows, width = tokens.shape
    depth, cols = weights[0].shape
    ff = weights[4].shape[1]
    head = cosine.shape[1]
    own_rows = rows // 8
    heads = cols // head
    shape = jax.ShapeDtypeStruct
    pack_a, pack_b = (depth + 16, 2 * cols), (depth, 2 * cols)
    weight_a, weight_b = (16,) + pack_a, (16,) + pack_b
    weight_out = (8, 16, depth, cols)
    outs = [
        (shape((rows, width), bf16), ANY),
        (shape((rows, cols), f32), VM),
        (shape((rows, cols), f32), VM),
        (shape((rows, cols), f32), VM),
        (shape((seqs, heads * rows // seqs, head), bf16), VM),
        (shape((16, rows, cols), bf16), ANY),
        (shape((rows, cols), f32), VM),
        (shape((seqs, 1, heads * rows // seqs), f32), VM),
        (shape((rows, cols), bf16), VM),
        (shape((rows, width), bf16), ANY),
        (shape((own_rows, width), f32), VM),
        (shape(weight_a, bf16), ANY),
        (shape(weight_b, bf16), ANY),
        (shape(weight_out, bf16), ANY),
    ]
    outs += [(shape((16, depth, ff), bf16), ANY)] * 3
    outs += [
        (shape((8, width), f32), VM),
        (shape((8, head), f32), VM),
        (shape((own_rows, width), bf16), VM),
        (shape((own_rows, width), f32), VM),
        (shape((rows, width), bf16), ANY),
    ]
    return pl.pallas_call(
        functools.partial(forward_kernel, scale),
        out_shape=[o for o, _ in outs],
        in_specs=[VM] * 3 + [SM] * 4 + [VM] * (len(small) - 7) + [ANY] * 7,
        out_specs=[s for _, s in outs],
        scratch_shapes=[
            pltpu.VMEM((rows, width), bf16),
            pltpu.VMEM((rows, 128), f32),
            pltpu.VMEM(pack_a, bf16),
            pltpu.VMEM(pack_b, bf16),
            pltpu.VMEM((depth, ff), bf16),
            pltpu.VMEM((16, 128), f32),
            pltpu.VMEM((rows, width), bf16),
            pltpu.VMEM((rows, width), bf16),
            pltpu.VMEM(weight_a, bf16),
            pltpu.VMEM(weight_b, bf16),
            pltpu.VMEM(weight_out, bf16),
            pltpu.VMEM((rows, cols), bf16),
            pltpu.VMEM((16, rows, cols), bf16),
            pltpu.VMEM((seqs, heads * rows // seqs, 2 * head), f32),
            pltpu.VMEM((8, own_rows, cols), bf16),
            pltpu.VMEM((own_rows, width), bf16),
        ]
        + sems(24 * 8, 24),
        name="forward",
        compiler_params=params(1, 62),
    )(*small, *weights, target)


def dot(left, right):
    return jnp.dot(left, right, preferred_element_type=f32)


def dot_t(left, right):
    return lax.dot_general(left, right, (((1,), (1,)), ((), ())), preferred_element_type=f32)


def t_dot(left, right):
    return lax.dot_general(left, right, (((0,), (0,)), ((), ())), preferred_element_type=f32)


def norm_back(values, gain, grad):
    inverse = lax.rsqrt(jnp.mean(values * values, axis=-1, keepdims=True) + epsilon)
    scaled = grad * gain
    unit = values * inverse
    inner = jnp.mean(scaled * unit, axis=-1, keepdims=True)
    return (scaled - unit * inner) * inverse, grad * unit


def unit_rows(ref, slot, rows):
    return ref.at[pl.ds(pl.multiple_of(slot * rows, 16), rows), :]


def row_unit(group, ref, rows):
    def unit(*step):
        return unit_rows(ref, group.slot(*step), rows)

    return unit


def outer(left, right, target, cols, step=512):
    def body(i, carry):
        at = rows_at(i, step)
        target[at, cols] = t_dot(left[:, at], right[...]).astype(target.dtype)
        return carry

    lax.fori_loop(0, left.shape[1] // step, body, 0)


def mlp_kernel(
    resid,
    grad_final,
    gain_wide,
    normed_in,
    low_in,
    gate_in,
    up_in,
    down_in,
    out_in,
    down_out,
    up_part_out,
    down_part_out,
    gate_grad,
    grad_resid,
    grad_gated,
    gain_grad,
    normed,
    low,
    w_gate,
    w_up,
    w_down,
    w_out,
    hidden,
    grad_gate,
    grad_up,
    part,
    down,
    gate_part,
    up_part,
    down_part,
    own,
    total,
    units,
    gated_in,
    *rest,
):
    scratch, scratch_w = [rest[5 * n : 5 * n + 5] for n in range(4)], rest[20:26]
    copies = Copies(*rest[26:])
    tensor, batch = Group("tensor", False), Group("batch")
    rows, width = normed.shape
    own_rows = resid.shape[0]
    ff = hidden.shape[1]
    depth = gate_grad.shape[0]
    loads = [
        copies.local(a, b)
        for a, b in (
            (normed_in, normed),
            (gate_in, w_gate),
            (up_in, w_up),
            (low_in, low),
            (down_in, w_down),
            (out_in, w_out),
        )
    ]
    enter(tensor.others + near(batch))
    for load in loads[:5]:
        load.wait()

    def activate(j, carry):
        cols = rows_at(j, 256)
        gate = dot(normed[...], w_gate[:, cols])
        up = dot(normed[...], w_up[:, cols])
        back = dot(low[...], w_down[:, cols])
        sigma = jax.nn.sigmoid(gate)
        silu = gate * sigma
        hidden[:, cols] = (silu * up).astype(bf16)
        grad_up[:, cols] = (back * silu).astype(bf16)
        grad_gate[:, cols] = (back * up * (sigma * (1.0 + gate * (1.0 - sigma)))).astype(bf16)
        return carry

    lax.fori_loop(0, ff // 256, activate, 0)

    def input_part(j, carry):
        cols = pl.ds(j * (width // 4), width // 4)
        value = dot_t(grad_gate[...], w_gate[cols, :]) + dot_t(grad_up[...], w_up[cols, :])
        part[:, cols] = value.astype(bf16)
        return carry

    steps = []
    for n in range(4):
        input_part(n, 0)
        steps.append(
            reduce(
                copies,
                tensor,
                row_unit(tensor, chunk(part, n, 4), own_rows),
                scratch[n],
                chunk(grad_resid, n, 4),
            )
        )
        next(steps[n])
    gens = {"x": lockstep(steps)}
    kept = []

    def gate_product():
        outer(normed, grad_gate, gate_part, slice(None))
        gens["w"] = reduce(
            copies, batch, row_unit(batch, gate_part, depth), scratch_w, gate_grad, by_mate=False
        )
        next(gens["w"])

    def up_product():
        outer(normed, grad_up, up_part, slice(None))
        kept.append(copies.local(up_part, up_part_out))

    def down_product():
        outer(low, hidden, down_part, slice(None))
        kept.append(copies.local(down_part, down_part_out))

    def down_rows():
        def down_cols(j, carry):
            cols = rows_at(j, 512)
            down[:, cols] = dot_t(hidden[...], w_down[cols, :]).astype(bf16)
            return carry

        lax.fori_loop(0, width // 512, down_cols, 0)
        kept.append(copies.local(down, down_out))

    do = {"G": gate_product, "U": up_product, "D": down_product, "R": down_rows}
    for key in MLP_ORDER:
        if key in do:
            do[key]()
        else:
            next(gens[key], None)
    for _ in gens["x"]:
        pass
    weight_steps = gens["w"]
    total[...] = jnp.zeros_like(total)

    def body(at):
        back, terms = norm_back(resid[at, :], gain_wide[1:2, :], grad_resid[at, :])
        back = grad_final[at, :] + back
        total[...] += terms
        grad_resid[at, :] = back
        own[at, :] = back.astype(bf16)

    each_rows(own_rows, 16, body)
    gain_grad[...] = jnp.sum(total[...], axis=0, keepdims=True)
    loads[5].wait()

    def gated_unit(n, carry):
        units[n] = dot(own[...], w_out[n].reshape(width, -1)).astype(bf16)
        return carry

    lax.fori_loop(0, 8, gated_unit, 0)
    exchanged = [
        copies.send(units.at[tensor.slot(*step)], gated_in.at[tensor.t], device)
        for step, device in zip(tensor.steps, tensor.others)
    ]
    gated_in[tensor.t] = units[tensor.t]
    for _ in weight_steps:
        pass
    for copy in exchanged:
        copy.wait_recv()
    for n in range(8):
        grad_gated[n * own_rows : (n + 1) * own_rows, :] = gated_in[n]
    for copy in exchanged:
        copy.wait_send()
    for copy in kept:
        copy.wait()


def mlp(resid, grad_final, gain, normed, low, weights, w_out):
    own_rows, width = resid.shape
    rows = normed.shape[0]
    ff = weights[0].shape[1]
    cols = w_out.shape[3]
    depth = width // 16
    shape = jax.ShapeDtypeStruct
    return pl.pallas_call(
        mlp_kernel,
        out_shape=[
            shape((rows, width), bf16),
            shape((width, ff), bf16),
            shape((width, ff), bf16),
            shape((depth, ff), bf16),
            shape((own_rows, width), f32),
            shape((rows, cols), bf16),
            shape((1, width), f32),
        ],
        in_specs=[VM] * 3 + [ANY] * 6,
        out_specs=[ANY] * 3 + [VM] * 4,
        scratch_shapes=[pltpu.VMEM((rows, width), bf16)] * 2
        + [pltpu.VMEM((width, ff), bf16)] * 3
        + [pltpu.VMEM(w_out.shape, bf16)]
        + [pltpu.VMEM((rows, ff), bf16)] * 3
        + [pltpu.VMEM((rows, width), bf16)] * 2
        + [pltpu.VMEM((width, ff), bf16)] * 3
        + [
            pltpu.VMEM((own_rows, width), bf16),
            pltpu.VMEM((16, width), f32),
            pltpu.VMEM((8, own_rows, cols), bf16),
            pltpu.VMEM((8, own_rows, cols), bf16),
        ]
        + reduce_scratch(own_rows, width // 4, False) * 4
        + reduce_scratch(depth, ff, True)
        + sems(100, 12),
        name="mlp",
        compiler_params=params(2, 62),
    )(resid, grad_final, gain, normed, low, *weights, w_out)


def attention_kernel(
    scale,
    queries,
    lse,
    attended,
    gate_raw,
    grad_gated,
    grad_resid,
    resid,
    kv_in,
    down_in,
    up_in,
    grad_query,
    kv_grad,
    gate_grad,
    low,
    final,
    up_grad,
    kv_all,
    down,
    up_part,
    own,
    grad_att,
    query_t,
    grad_t,
    delta,
    acc,
    grad_query_t,
    dkv,
    down_sum,
    *rest,
):
    scratch_kv, scratch_d, scratch_w = rest[:6], rest[6:11], rest[11:17]
    copies = Copies(*rest[17:])
    tensor, batch = Group("tensor", False), Group("batch")
    b = lax.axis_index("batch")
    seqs, head_rows, head = queries.shape
    rows, cols = attended.shape
    seq_dev = rows // seqs
    heads = cols // head
    own_rows, width = resid.shape
    depth = up_grad.shape[0]
    factor = scale * math.log2(math.e)
    loads = [copies.local(a, c) for a, c in ((up_in, up_part), (down_in, down), (kv_in, kv_all))]
    enter(near(tensor, batch))

    def round_own(at):
        own[at, :] = grad_resid[at, :].astype(bf16)

    each_rows(own_rows, 16, round_own)
    low_steps = gather(
        copies, tensor, own, lambda s: unit_rows(low, s, own_rows), by_mate=False
    )
    next(low_steps)
    loads[0].wait()
    up_steps = reduce(
        copies, batch, row_unit(batch, up_part, depth), scratch_w, up_grad, by_mate=False
    )
    next(up_steps)
    for s in range(seqs):
        at = pl.ds(s * seq_dev, seq_dev)
        for h in range(heads):
            here, there = pl.ds(h * head, head), pl.ds(h * seq_dev, seq_dev)
            sigma = jax.nn.sigmoid(gate_raw[at, here])
            value = grad_gated[at, here].astype(f32)
            out = attended[at, here]
            low_grad = (value * sigma).astype(bf16)
            grad_att[s, there, :] = low_grad
            gate_grad[at, here] = (value * out * (sigma * (1.0 - sigma))).astype(bf16)
            acc[s, there, :] = low_grad.astype(f32) * out
        delta[s] = jnp.sum(acc[s].T, axis=0, keepdims=True)
        grad_t[s] = grad_att[s].astype(f32).T.astype(bf16)
        query_t[s] = queries[s].astype(f32).T.astype(bf16)
    for s in range(seqs):
        grad_query_t[s] = jnp.zeros((head, head_rows), f32)
    loads[1].wait()
    loads[2].wait()

    def block(chip, masked):
        for s in range(seqs):
            at = pl.ds(s * seq_dev, seq_dev)
            slots = (chip * 2, chip * 2 + 1)
            keys = jnp.concatenate([kv_all[slot, at, :head] for slot in slots], axis=0)
            values = jnp.concatenate([kv_all[slot, at, head:] for slot in slots], axis=0)
            probs = jnp.exp2(dot(keys, query_t[s]) * factor - lse[s])
            if masked:
                key = lax.broadcasted_iota(jnp.int32, probs.shape, 0)
                col = lax.broadcasted_iota(jnp.int32, probs.shape, 1)
                row = jnp.where(col >= seq_dev, col - seq_dev, col)
                ahead = (chip * 2 - b) * seq_dev
                probs = jnp.where(key + ahead <= row, probs, 0.0)
            grad_probs = dot(values, grad_t[s])
            grad_scores = (probs * (grad_probs - delta[s])).astype(bf16)
            key_part = (dot(grad_scores, queries[s]) * scale).astype(bf16)
            value_part = dot(probs.astype(bf16), grad_att[s]).astype(bf16)
            for n, slot in enumerate(slots):
                here = slice(n * seq_dev, (n + 1) * seq_dev)
                dkv[slot, at, :head] = key_part[here]
                dkv[slot, at, head:] = value_part[here]
            grad_query_t[s] += t_dot(keys, grad_scores)

    def pair(chip, own_pair):
        if own_pair:
            block(chip, True)
            return
        here = batch.chip(0, 0)

        @pl.when(chip < here)
        def _():
            block(chip, False)

        @pl.when(chip > here)
        def _():
            for n in range(2):
                dkv[chip * 2 + n] = jnp.zeros(dkv.shape[1:], bf16)

    kv_steps = reduce(
        copies,
        batch,
        lambda dr, dq, dc: dkv.at[batch.slot(dr, dq, dc)],
        scratch_kv,
        kv_grad,
        early=True,
    )
    down_steps = reduce(
        copies, tensor, row_unit(tensor, down, own_rows), scratch_d, down_sum, by_mate=False
    )
    pairs = iter(ORDER)

    def next_pair():
        dr, dq = next(pairs)
        pair(batch.chip(dr, dq), (dr, dq) == (0, 0))

    gens = {"k": kv_steps, "l": low_steps, "d": down_steps, "u": up_steps}
    for key in ATTENTION_ORDER:
        if key == "P":
            next_pair()
        else:
            next(gens[key], None)
    for s in range(seqs):
        value = grad_query_t[s].T * scale
        for h in range(heads):
            grad_query[s * seq_dev : (s + 1) * seq_dev, h * head : (h + 1) * head] = value[
                h * seq_dev : (h + 1) * seq_dev
            ]
    run_all(kv_steps, down_steps, low_steps, up_steps)
    add_rows(final, [down_sum, resid])


def attention_back(
    scale, queries, lse, attended, gate_raw, grad_gated, grad_resid, resid, kv_all, down, up_part
):
    rows, cols = attended.shape
    own_rows, width = resid.shape
    seqs, head_rows, head = queries.shape
    ff = up_part.shape[1]
    depth = width // 16
    shape = jax.ShapeDtypeStruct
    return pl.pallas_call(
        functools.partial(attention_kernel, scale),
        out_shape=[
            shape((rows, cols), f32),
            shape((rows, cols), f32),
            shape((rows, cols), bf16),
            shape((rows, width), bf16),
            shape((own_rows, width), bf16),
            shape((depth, ff), bf16),
        ],
        in_specs=[VM] * 7 + [ANY] * 3,
        out_specs=[VM] * 3 + [ANY] + [VM] * 2,
        scratch_shapes=[
            pltpu.VMEM(kv_all.shape, bf16),
            pltpu.VMEM((rows, width), bf16),
            pltpu.VMEM((width, ff), bf16),
            pltpu.VMEM((own_rows, width), bf16),
            pltpu.VMEM(queries.shape, bf16),
            pltpu.VMEM((seqs, head, head_rows), bf16),
            pltpu.VMEM((seqs, head, head_rows), bf16),
            pltpu.VMEM((seqs, 1, head_rows), f32),
            pltpu.VMEM(queries.shape, f32),
            pltpu.VMEM((seqs, head, head_rows), f32),
            pltpu.VMEM(kv_all.shape, bf16),
            pltpu.VMEM((own_rows, width), f32),
        ]
        + reduce_scratch(rows, cols, True)
        + reduce_scratch(own_rows, width, False)
        + reduce_scratch(depth, ff, True)
        + sems(72, 6),
        name="attention_back",
        compiler_params=params(3, 62),
    )(queries, lse, attended, gate_raw, grad_gated, grad_resid, resid, kv_all, down, up_part)


def last_kernel(
    share,
    grad_query,
    kv_grad,
    gate_grad,
    query_raw,
    kv_raw,
    cosine,
    sine,
    gain_wide,
    gain_head,
    inputs,
    grad_resid,
    final,
    gated,
    norm_mlp_grad,
    normed_in,
    low_in,
    kvo_in,
    qg_in,
    down_in,
    tokens,
    output,
    weights_out,
    gains_out,
    normed,
    low,
    w_kvo,
    w_qg,
    down_part,
    weight_grad,
    down_sum,
    qg_low,
    kv_low,
    part,
    weight_part,
    held,
    own,
    total,
    mine,
    over_tensor,
    shares,
    over_batch,
    *rest,
):
    scratch, scratch_w, scratch_d = rest[:5], rest[5:11], rest[11:17]
    copies = Copies(*rest[17:])
    tensor, batch = Group("tensor", False), Group("batch")
    rows, width = normed.shape
    own_rows = inputs.shape[0]
    cols = grad_query.shape[1]
    head = gain_head.shape[1]
    seq_dev = cosine.shape[0]
    depth = weight_grad.shape[0]
    loads = [
        copies.local(a, c)
        for a, c in (
            (qg_in, w_qg),
            (kvo_in, w_kvo),
            (down_in, down_part),
            (normed_in, normed),
            (low_in, low),
        )
    ]
    b = lax.axis_index("batch")
    members = [(0, dq, dr, dc) for dc in range(2) for dq, dr in [(0, 0)] + batch_steps(batch)][1:]
    batch_others = [(batch.slot(dr, dq, dc), batch.t) for _, dq, dr, dc in members]
    enter(tensor.others + batch_others)

    def place(ref):
        def unit(slot):
            seq, rest = lax.div(slot, 4), lax.rem(slot, 4)
            return ref.at[seq, pl.ds(pl.multiple_of(rest * own_rows, 16), own_rows), :]

        return unit

    output_steps = gather(copies, tensor, final, place(output), by_mate=False)
    next(output_steps)

    def head_back(raw, gain, grad, at):
        back = grad * cosine[...] - pltpu.roll(grad, head // 2, 1) * sine[...]
        values, terms = norm_back(raw, gain, back)
        return values.astype(bf16), jnp.sum(terms, axis=0, keepdims=True)

    mine[...] = jnp.zeros_like(mine)
    norm_rows = width // 128
    for s in range(rows // seq_dev):
        at = pl.ds(s * seq_dev, seq_dev)
        for h in range(cols // head):
            here = pl.ds(h * head, head)
            qg_low[at, here], terms = head_back(
                query_raw[at, here], gain_head[0:1, :], grad_query[at, here], at
            )
            mine[2 * norm_rows : 2 * norm_rows + 1, :] += terms
        kv_low[at, :head], terms = head_back(
            kv_raw[at, :head], gain_head[1:2, :], kv_grad[at, :head], at
        )
        mine[2 * norm_rows + 1 : 2 * norm_rows + 2, :] += terms
        kv_low[at, head:] = kv_grad[at, head:].astype(bf16)
        qg_low[at, cols:] = gate_grad[at, :]
    loads[0].wait()
    loads[1].wait()
    def part_chunk(n):
        slots = pl.ds(n * 4, 4)
        value = dot_t(qg_low[...], w_qg[slots].reshape(width // 4, 2 * cols))
        value += dot_t(kv_low[...], w_kvo[slots, :depth, :cols].reshape(width // 4, cols))
        part[:, n * (width // 4) : (n + 1) * (width // 4)] = value.astype(bf16)

    for n in range(4):
        part_chunk(n)
    steps = reduce(copies, tensor, row_unit(tensor, part, own_rows), scratch, held)
    next(steps)
    loads[2].wait()
    down_steps = reduce(
        copies, batch, row_unit(batch, down_part, depth), scratch_d, down_sum, by_mate=False
    )
    next(down_steps)
    loads[3].wait()
    loads[4].wait()
    next(steps)
    next(output_steps)
    outer(normed, qg_low, weight_part, slice(0, 2 * cols))
    next(down_steps)
    next(steps)
    outer(normed, kv_low, weight_part, slice(2 * cols, 3 * cols))
    outer(low, gated, weight_part, slice(3 * cols, 4 * cols))
    weight_steps = reduce(
        copies, batch, row_unit(batch, weight_part, depth), scratch_w, weight_grad, by_mate=False
    )
    next(weight_steps)
    for n in range(norm_rows):
        mine[norm_rows + n : norm_rows + n + 1, :] = norm_mlp_grad[:, n * 128 : (n + 1) * 128]

    def small():
        first = [
            copies.send(mine, over_tensor.at[tensor.t], device) for device in tensor.others
        ]
        over_tensor[tensor.t] = mine[...]
        yield
        for copy in first:
            copy.wait_recv()
        total_t = over_tensor[0]
        for n in range(1, 8):
            total_t = total_t + over_tensor[n]
        for n in range(16):
            shares[n, 0:1, :] = total_t[n : n + 1]
            shares[n, 1:2, :] = total_t[norm_rows + n : norm_rows + n + 1]
            shares[n, 2:4, :] = total_t[2 * norm_rows : 2 * norm_rows + 2]
            shares[n, 4:8, :] = jnp.zeros((4, 128), f32)
        second = [
            copies.send(shares.at[batch.slot(dr, dq, dc)], over_batch.at[b], device)
            for (_, dq, dr, dc), device in zip(members, batch_others)
        ]
        over_batch[b] = shares[b]
        yield
        for copy in second:
            copy.wait_recv()
        total_b = over_batch[0]
        for n in range(1, 16):
            total_b = total_b + over_batch[n]
        heads_own = pltpu.roll(total_b, (128 - share * b) % 128, 1)
        row = lax.broadcasted_iota(jnp.int32, total_b.shape, 0)
        gains_out[...] = jnp.where(row < 2, total_b, heads_own).astype(bf16)
        for copy in first + second:
            copy.wait_send()

    def along():
        yield from steps
        total[...] = jnp.zeros_like(total)

        def body(at):
            back, terms = norm_back(
                inputs[at, :].astype(f32), gain_wide[0:1, :], held[at, :]
            )
            total[...] += terms
            own[at, :] = (grad_resid[at, :] + back).astype(bf16)

        each_rows(own_rows, 16, body)
        gain_row = jnp.sum(total[...], axis=0, keepdims=True)
        for n in range(norm_rows):
            mine[n : n + 1, :] = gain_row[:, n * 128 : (n + 1) * 128]
        big = gather(copies, tensor, own, place(tokens))
        few = small()
        for _ in big:
            next(few, None)
            yield
        yield from few

    chain = along()
    gens = {"o": output_steps, "x": chain, "d": down_steps, "w": weight_steps}
    for key in LAST_ORDER:
        next(gens[key], None)
    run_all(chain, output_steps, down_steps, weight_steps)
    weights_out[:, : 4 * cols] = weight_grad[...].astype(bf16)
    weights_out[:, 4 * cols :] = down_sum[...].astype(bf16)


def batch_steps(batch):
    return [(dq, dr) for dr, dq in batch.steps]


def last_step(scale_free, held_in_hbm, few_shape, share):
    grad_query, inputs = scale_free[0], scale_free[9]
    seqs = grad_query.shape[0] // scale_free[5].shape[0]
    normed, low, kvo, qg, down_part = held_in_hbm
    own_rows, width = inputs.shape
    rows, cols = grad_query.shape
    ff = down_part.shape[1]
    depth = width // 16
    shape = jax.ShapeDtypeStruct
    return pl.pallas_call(
        functools.partial(last_kernel, share),
        out_shape=[
            shape((seqs, rows // seqs, width), bf16),
            shape((seqs, rows // seqs, width), bf16),
            shape((depth, 4 * cols + ff), bf16),
            shape((8, 128), bf16),
        ],
        in_specs=[VM] * len(scale_free) + [ANY] * len(held_in_hbm),
        out_specs=[ANY] * 2 + [VM] * 2,
        scratch_shapes=[
            pltpu.VMEM((rows, width), bf16),
            pltpu.VMEM((rows, width), bf16),
            pltpu.VMEM(kvo.shape, bf16),
            pltpu.VMEM(qg.shape, bf16),
            pltpu.VMEM((width, ff), bf16),
            pltpu.VMEM((depth, 4 * cols), f32),
            pltpu.VMEM((depth, ff), f32),
            pltpu.VMEM((rows, 2 * cols), bf16),
            pltpu.VMEM((rows, cols), bf16),
            pltpu.VMEM((rows, width), bf16),
            pltpu.VMEM((width, 4 * cols), bf16),
            pltpu.VMEM((own_rows, width), f32),
            pltpu.VMEM((own_rows, width), bf16),
            pltpu.VMEM((16, width), f32),
            pltpu.VMEM(few_shape, f32),
            pltpu.VMEM((8,) + few_shape, f32),
            pltpu.VMEM((16, 8, 128), f32),
            pltpu.VMEM((16, 8, 128), f32),
        ]
        + reduce_scratch(own_rows, width, False)
        + reduce_scratch(depth, 4 * cols, True)
        + reduce_scratch(depth, ff, True)
        + sems(140, 12),
        name="projections_back",
        compiler_params=params(4, 62),
    )(*scale_free, *held_in_hbm)


def shards(
    tokens,
    target,
    domain_ids,
    domain_counts,
    weight_index,
    loss_weights,
    w_query,
    w_key,
    w_value,
    w_gate_out,
    w_output,
    w_gate,
    w_up,
    w_down,
    norm_attn,
    norm_mlp,
    gain_query,
    gain_key,
):
    seq_count, seq_dev, width = tokens.shape
    rows = seq_count * seq_dev
    members = lax.axis_size("tensor")
    batch_count = lax.axis_size("batch")
    b, t = lax.axis_index("batch"), lax.axis_index("tensor")
    own_rows = rows // members
    seq_len = seq_dev * batch_count
    head = gain_query.shape[0] * batch_count
    scale = head ** (-0.5)
    q_cols, k_cols = w_query.shape[1], w_key.shape[1]
    heads = q_cols // head

    half_size = head // 2
    pos_local = (b * seq_dev + jnp.arange(seq_dev, dtype=jnp.int32)).astype(f32)
    inverse_freq = rope_base ** (-(jnp.arange(head) % half_size).astype(f32) / half_size)
    angles = pos_local[:, None] * inverse_freq[None, :]
    sign = jnp.where(jnp.arange(head) < half_size, -1.0, 1.0).astype(f32)
    cosine_wide, sine_wide = jnp.cos(angles), jnp.sin(angles) * sign

    tokens_low = tokens.reshape(rows, width)
    ff = w_gate.shape[1]
    (
        normed_low,
        query_raw,
        kv_raw,
        gate_raw,
        queries,
        kv_all,
        attended,
        lse,
        gated_low,
        normed_mlp_low,
        resid_own,
        wide_kvo,
        wide_qg,
        w_out_all,
        wide_gate,
        wide_up,
        wide_down,
        gain_wide,
        gain_head,
        inputs_own,
        grad_final_own,
        grad_final_low,
    ) = forward(
        scale,
        seq_count,
        (
            tokens_low,
            cosine_wide,
            sine_wide,
            domain_ids,
            domain_counts,
            weight_index,
            loss_weights,
            norm_attn[None],
            norm_mlp[None],
            gain_query[None],
            gain_key[None],
            w_output,
            w_down,
        ),
        (w_query, w_key, w_value, w_gate_out, w_gate, w_up),
        target.reshape(rows, width),
    )

    weights = [w.reshape(width, ff) for w in (wide_gate, wide_up, wide_down)]
    (
        down_part,
        up_weight_part,
        down_weight_part,
        grad_gate,
        grad_resid_own,
        grad_gated,
        norm_mlp_terms,
    ) = mlp(
        resid_own,
        grad_final_own,
        gain_wide,
        normed_mlp_low,
        grad_final_low,
        weights,
        w_out_all,
    )
    grad_query_rot, kv_grad, gate_raw_grad, grad_resid_low, final_own, grad_up = attention_back(
        scale,
        queries,
        lse,
        attended,
        gate_raw,
        grad_gated,
        grad_resid_own,
        resid_own,
        kv_all,
        down_part,
        up_weight_part,
    )
    norm_rows = width // 128
    grad_tokens, output, weight_grads, gain_grads = last_step(
        (
            grad_query_rot,
            kv_grad,
            gate_raw_grad,
            query_raw,
            kv_raw,
            cosine_wide,
            sine_wide,
            gain_wide,
            gain_head,
            inputs_own,
            grad_resid_own,
            final_own,
            gated_low,
            norm_mlp_terms,
        ),
        (normed_low, grad_resid_low, wide_kvo, wide_qg, down_weight_part),
        (2 * norm_rows + 8, 128),
        gain_query.shape[0],
    )

    pieces = [0, q_cols, 2 * q_cols, 2 * q_cols + k_cols, 2 * q_cols + 2 * k_cols]
    pieces += [3 * q_cols + 2 * k_cols, 3 * q_cols + 2 * k_cols + ff]
    grad_query, grad_gate_out, grad_key, grad_value, grad_output, grad_down = (
        weight_grads[:, lo:hi].astype(f32) for lo, hi in zip(pieces[:-1], pieces[1:])
    )
    gain_grads = gain_grads.astype(f32)
    share = gain_query.shape[0]
    return (
        output,
        grad_tokens.astype(f32),
        grad_query,
        grad_key,
        grad_value,
        grad_gate_out,
        grad_output.T,
        grad_gate.astype(f32),
        grad_up.astype(f32),
        grad_down.T,
        gain_grads[0],
        gain_grads[1],
        gain_grads[2, :share],
        gain_grads[3, :share],
    )


def solution(mesh):
    in_specs = (
        P(None, "batch", None),
        P(None, "batch", None),
        P(),
        P(),
        P(),
        P(),
        P("batch", "tensor"),
        P("batch", "tensor"),
        P("batch", "tensor"),
        P("batch", "tensor"),
        P("tensor", "batch"),
        P("batch", "tensor"),
        P("batch", "tensor"),
        P("tensor", "batch"),
        P("batch"),
        P("batch"),
        P("batch"),
        P("batch"),
    )
    out_specs = (
        P(None, "batch", None),
        P(None, "batch", None),
        P("batch", "tensor"),
        P("batch", "tensor"),
        P("batch", "tensor"),
        P("batch", "tensor"),
        P("tensor", "batch"),
        P("batch", "tensor"),
        P("batch", "tensor"),
        P("tensor", "batch"),
        P("batch"),
        P("batch"),
        P("batch"),
        P("batch"),
    )
    return jax.shard_map(shards, mesh=mesh, in_specs=in_specs, out_specs=out_specs, check_vma=False)
```

```python
import functools
import math

import jax
import jax.numpy as jnp
from jax import lax
from jax.experimental import pallas as pl
from jax.experimental.pallas import tpu as pltpu
from jax.sharding import PartitionSpec as P

MESH = pl.DeviceIdType.MESH
epsilon = 1e-06
rope_base = 1000000.0
f32 = jnp.float32
bf16 = jnp.bfloat16

FORWARD_ORDER = "ntwntwnmtnwtntDFXwabcWRE"
MLP_ORDER = "ffffffff0123wf0123wf0123wf0123wfff"
ATTENTION_ORDER = "PkuPklPkduPkPkdluPkPkduPkkkkkdldl"
LAST_ORDER = "fffffffff0123fowd0123odw0123odw" + "xodw" * 12

MIB = 2**20
ANY = pl.BlockSpec(memory_space=pl.ANY)
VM = pl.BlockSpec(memory_space=pltpu.VMEM)
SM = pl.BlockSpec(memory_space=pltpu.SMEM)


class Group:
    def __init__(self, kind, core=True):
        b = lax.axis_index("batch")
        t = lax.axis_index("tensor")
        c = lax.rem(b, 2)
        self.c, self.t = c, t
        if kind == "tensor":
            r, q = lax.div(t, 2), lax.rem(t, 2)
            self.slot = lambda dr, dq: lax.rem(r + dr, 4) * 2 + lax.rem(q + dq, 2)
            at = lambda dr, dq: (b, self.slot(dr, dq))
        else:
            q, r = lax.div(b, 8), lax.rem(lax.div(b, 2), 4)
            self.chip = lambda dr, dq: lax.rem(q + dq, 2) * 4 + lax.rem(r + dr, 4)
            self.slot = lambda dr, dq, dc=0: self.chip(dr, dq) * 2 + lax.rem(c + dc, 2)
            at = lambda dr, dq: (self.slot(dr, dq), t)
        self.core = (b + 1 - 2 * c, t) if core else None
        self.right, self.left, self.mate = at(1, 0), at(3, 0), at(0, 1)
        self.others = [at(dr, dq) for dr in range(4) for dq in range(2) if dr or dq]
        self.steps = [(dr, dq) for dr in range(4) for dq in range(2) if dr or dq]


def enter(devices):
    barrier = pltpu.get_barrier_semaphore()
    for device in devices:
        pl.semaphore_signal(barrier, inc=1, device_id=device, device_id_type=MESH)
    pl.semaphore_wait(barrier, len(devices))


def near(*groups):
    devices = [d for g in groups for d in (g.right, g.left, g.mate)]
    cores = [g.core for g in groups if g.core is not None]
    return devices + cores[:1]


class Copies:
    def __init__(self, send_sem, recv_sem, local_sem):
        self.send_sem, self.recv_sem, self.local_sem = send_sem, recv_sem, local_sem
        self.count = 0
        self.locals = 0

    def send(self, source, target, device):
        copy = pltpu.make_async_remote_copy(
            src_ref=source,
            dst_ref=target,
            send_sem=self.send_sem.at[self.count],
            recv_sem=self.recv_sem.at[self.count],
            device_id=device,
            device_id_type=MESH,
        )
        self.count += 1
        copy.start()
        return copy

    def local(self, source, target):
        copy = pltpu.make_async_copy(source, target, self.local_sem.at[self.locals])
        self.locals += 1
        copy.start()
        return copy


def half_of(ref, which):
    width = ref.shape[-1] // 2
    lead = (slice(None),) * (len(ref.shape) - 1)
    return ref.at[lead + (pl.ds(which * width, width),)]


def run_all(*steps):
    waiting = list(steps)
    while waiting:
        for step in list(waiting):
            try:
                next(step)
            except StopIteration:
                waiting.remove(step)


def gather(copies, group, own, slot, split=True, source=None, by_mate=True):
    s = group.slot
    core_copies = []
    sent = []

    def push(ref, *devices):
        out = [copies.send(ref, ref, device) for device in devices]
        sent.extend(out)
        return out

    def to_core(ref):
        if group.core is not None:
            core_copies.extend(push(ref, group.core))

    def core_wait(count):
        for copy in core_copies[:count]:
            copy.wait_recv()
        del core_copies[:count]

    def onward(unit, way):
        if way == 0:
            return push(half_of(unit, 0) if split else unit, group.right)
        return push(half_of(unit, 1), group.left) if split else []

    home = slot(s(0, 0))
    source = own if source is None else source
    first = [copies.send(source, home, d) for d in (group.right, group.left, group.mate)]
    sent.extend(first)
    kept = None
    if own is not None:
        kept = copies.local(own, home)
        if group.core is not None:
            core_copies.append(copies.send(own, home, group.core))
            sent.append(core_copies[0])
    from_left, from_right, from_mate = first
    yield []
    far = []
    for way, copy in enumerate((from_left, from_right)):
        copy.wait_recv()
        unit = slot(s(3 - 2 * way, 0))
        far += onward(unit, way)
        to_core(unit)
    from_mate.wait_recv()
    mate_unit = slot(s(0, 1))
    mate_line = push(mate_unit, group.right, group.left)
    to_core(mate_unit)
    if own is not None:
        core_wait(1)
        kept.wait()
    yield [(0, 0)]
    mate_far = []
    for copy in far:
        copy.wait_recv()
    if by_mate:
        mate_far += push(slot(s(2, 0)), group.mate)
    to_core(slot(s(2, 0)))
    yield []
    for way, copy in enumerate(mate_line):
        copy.wait_recv()
        unit = slot(s(3 - 2 * way, 1))
        if not by_mate:
            mate_far += onward(unit, way)
        to_core(unit)
    core_wait(3)
    yield [(3, 0), (1, 0), (0, 1)]
    for copy in mate_far:
        copy.wait_recv()
    to_core(slot(s(2, 1)))
    core_wait(3)
    yield [(2, 0), (3, 1), (1, 1)]
    core_wait(1)
    yield [(2, 1)]
    for copy in sent:
        copy.wait_send()


def chunk(ref, n, count):
    width = ref.shape[-1] // count
    return ref.at[:, pl.ds(n * width, width)]


def add_rows(target, sources, step=16):
    def body(at):
        total = sources[0][at, :].astype(f32)
        for source in sources[1:]:
            total = total + source[at, :].astype(f32)
        target[at, :] = total.astype(target.dtype)

    each_rows(target.shape[0], step, body)


def rows_at(i, step=16):
    return pl.ds(pl.multiple_of(i * step, step), step)


def each_rows(rows, step, body):
    def run(i, carry):
        body(rows_at(i, step))
        return carry

    lax.fori_loop(0, rows // step, run, 0)


def reduce_scratch(rows, width, core):
    shapes = [
        pltpu.VMEM((4, rows, width // 2), bf16),
        pltpu.VMEM((4, rows, width), bf16),
        pltpu.VMEM((4, rows, width), bf16),
        pltpu.VMEM((3, rows, width), bf16),
        pltpu.VMEM((2, rows, width), bf16),
    ]
    if core:
        shapes += [pltpu.VMEM((8, rows, width), bf16)]
    return shapes


ORDER = [(2, 1), (1, 1), (3, 1), (2, 0), (1, 0), (3, 0), (0, 1), (0, 0)]


def reduce(copies, group, part, scratch, result, early=False, by_mate=True):
    far, near_in, outgoing, mates, far_sums = scratch[:5]
    core = group.core is not None
    sent = []

    def send(source, target, device):
        copy = copies.send(source, target, device)
        sent.append(copy)
        return copy

    arrived = {}

    def to_core(n):
        dr, dq = ORDER[n]
        arrived[dr, dq] = (send(part(dr, dq, 1), scratch[5].at[n], group.core), n)

    def terms(dr, dq):
        if not core:
            return [part(dr, dq)]
        copy, n = arrived[dr, dq]
        copy.wait_recv()
        return [part(dr, dq, 0), scratch[5].at[n]]

    sides = ((1, group.right), (3, group.left))

    def far_sends(unit, line):
        return [
            send(half_of(unit, way), far.at[line * 2 + way], device)
            for way, (_, device) in enumerate(sides)
        ]

    def line_sends(line, far_copies):
        out = []
        for way, (dr, device) in enumerate(sides):
            unit = terms(dr, line)
            held = outgoing.at[line * 2 + way]
            if far_copies is not None:
                far_copies[way].wait_recv()
                there = far.at[line * 2 + way]
                add_rows(half_of(held, way), [half_of(u, way) for u in unit] + [there])
                add_rows(half_of(held, 1 - way), [half_of(u, 1 - way) for u in unit])
            elif core:
                add_rows(held, unit)
            else:
                held = unit[0]
            out.append(send(held, near_in.at[line * 2 + way], device))
        return out

    def first():
        unit = terms(2, 1)
        if core:
            add_rows(far_sums.at[1], unit)
            unit = [far_sums.at[1]]
        if by_mate:
            return send(unit[0], mates.at[2], group.mate), line_sends(1, None)
        return None, far_sends(unit[0], 1)

    def second():
        unit = terms(2, 0)
        if by_mate:
            far_mate.wait_recv()
            unit = unit + [mates.at[2]]
        if len(unit) > 1:
            add_rows(far_sums.at[0], unit)
            unit = [far_sums.at[0]]
        return far_sends(unit[0], 0)

    def third():
        return line_sends(0, far_copies)

    if early:
        for n in range(3):
            to_core(n)
            yield
        to_core(3)
        far_mate, mate_line = first()
        yield
        to_core(4)
        far_copies = second()
        yield
        to_core(5)
        yield
        to_core(6)
        own_line = third()
        yield
        to_core(7)
    else:
        if core:
            for n in range(8):
                to_core(n)
            yield
        far_mate, mate_line = first()
        yield
        far_copies = second()
        yield
        if not by_mate:
            mate_line = line_sends(1, mate_line)
        own_line = third()
    yield
    unit = terms(0, 1)
    for copy in mate_line:
        copy.wait_recv()
    add_rows(mates.at[0], unit + [near_in.at[2], near_in.at[3]])
    to_mate = send(mates.at[0], mates.at[1], group.mate)
    yield
    unit = terms(0, 0)
    for copy in own_line:
        copy.wait_recv()
    to_mate.wait_recv()
    add_rows(result, unit + [near_in.at[0], near_in.at[1], mates.at[1]])
    for copy in sent:
        copy.wait_send()


def hoisted(kernel, count):
    def run(*refs):
        sources, rest = refs[:count], refs[count : -count - 1]
        held, sem = refs[-count - 1 : -1], refs[-1]
        loads = [
            pltpu.make_async_copy(source, place, sem.at[n])
            for n, (source, place) in enumerate(zip(sources, held))
        ]
        for load in loads:
            load.start()
        kernel(loads, *held, *rest)

    return run


def hoisted_scratch(arrays):
    held = [pltpu.VMEM(a.shape, a.dtype) for a in arrays]
    return held + [pltpu.SemaphoreType.DMA((len(held),))]


def sems(remote, local):
    return [
        pltpu.SemaphoreType.DMA((remote,)),
        pltpu.SemaphoreType.DMA((remote,)),
        pltpu.SemaphoreType.DMA((max(local, 1),)),
    ]


def params(collective, limit=48):
    return pltpu.CompilerParams(
        collective_id=collective, has_side_effects=True, vmem_limit_bytes=limit * MIB
    )


def prepare_head(values, gain, cosine, sine):
    half_size = values.shape[1] // 2
    mean = jnp.mean(values * values, axis=-1, keepdims=True)
    scaled = values * lax.rsqrt(mean + epsilon) * gain
    return scaled * cosine + pltpu.roll(scaled, half_size, 1) * sine


def forward_kernel(
    scale,
    input_loads,
    tokens,
    cosine,
    sine,
    domain_ids,
    domain_counts,
    weight_index,
    loss_weights,
    norm_attn,
    norm_mlp,
    gain_query,
    gain_key,
    w_output,
    w_down,
    w_query,
    w_key,
    w_value,
    w_gate_out,
    mlp_a,
    mlp_b,
    target_in,
    normed_out,
    query_raw_out,
    kv_raw_out,
    gate_raw_out,
    queries_out,
    kv_out,
    attended_out,
    lse,
    gated,
    normed_mlp,
    resid,
    wide_kvo,
    wide_qg,
    w_out_out,
    wide_a,
    wide_b,
    wide_c,
    gain_wide,
    gain_head,
    inputs_own_out,
    grad_final_out,
    low_out,
    normed,
    inverse,
    pack_a,
    pack_b,
    mlp_c,
    few,
    target,
    low,
    w_kvo,
    w_qg,
    w_out,
    kv_own,
    kv_all,
    acc,
    rows_all,
    own,
    query_raw,
    kv_raw,
    gate_raw,
    attended,
    queries,
    inputs_own,
    grad_final,
    send_sem,
    recv_sem,
    local_sem,
):
    copies = Copies(send_sem, recv_sem, local_sem)
    tensor, batch = Group("tensor"), Group("batch")
    b = lax.axis_index("batch")
    rows, width = tokens.shape
    cols = query_raw.shape[1]
    own_rows = resid.shape[0]
    seqs, head_rows, head = queries.shape
    heads = query_raw.shape[1] // head
    seq_dev = rows // seqs
    depth, key_cols = w_key.shape
    packing = [
        copies.local(source, place)
        for source, place in (
            (w_key, pack_a.at[pl.ds(0, depth), pl.ds(0, key_cols)]),
            (w_value, pack_a.at[pl.ds(0, depth), pl.ds(key_cols, key_cols)]),
            (w_query, pack_b.at[:, pl.ds(0, cols)]),
            (w_gate_out, pack_b.at[:, pl.ds(cols, cols)]),
        )
    ]
    target_load = copies.local(target_in, target)

    def flipped(values):
        return values.astype(f32).T.astype(bf16)

    pack_a[0:depth, cols:] = flipped(w_output[...])
    few[...] = jnp.zeros_like(few)
    share = gain_query.shape[1]
    few[0:1, :] = norm_attn[...].astype(f32)
    few[1:2, :] = norm_mlp[...].astype(f32)
    few[2:3, 0:share] = gain_query[...].astype(f32)
    few[3:4, 0:share] = gain_key[...].astype(f32)
    placed = pltpu.roll(few[...], b * share, 1)
    row = lax.broadcasted_iota(jnp.int32, placed.shape, 0)
    pack_a[depth:, :] = jnp.zeros((16, pack_a.shape[1]), bf16)
    pack_a[depth:, 0:128] = jnp.where(row < 2, few[...], placed).astype(bf16)
    enter(tensor.others + near(batch))

    def batch_gather(source, target, by_mate=True):
        return gather(copies, batch, source, lambda s: target.at[s], by_mate=by_mate)

    for copy in packing:
        copy.wait()
    a_steps = batch_gather(pack_a, w_kvo, True)
    b_steps = batch_gather(pack_b, w_qg, False)
    next(a_steps)
    next(b_steps)

    input_loads[0].wait()

    def invert(at):
        values = tokens[at, :].astype(f32)
        mean = jnp.mean(values * values, axis=-1, keepdims=True)
        inverse[at, :] = jnp.broadcast_to(lax.rsqrt(mean + epsilon), (32, 128))

    each_rows(rows, 32, invert)
    mlp_c[...] = flipped(w_down[...])
    next(a_steps)
    next(b_steps)
    for _ in a_steps:
        pass
    half = tensor.c * 8
    kept = [copies.local(w_kvo, wide_kvo)]
    out_home = copies.local(w_kvo.at[:, pl.ds(0, depth), pl.ds(cols, cols)], w_out.at[tensor.t])
    wide_out_steps = gather(
        copies,
        tensor,
        None,
        lambda s: w_out.at[s, pl.ds(half, 8)],
        source=w_kvo.at[pl.ds(half, 8), pl.ds(0, depth), pl.ds(cols, cols)],
        by_mate=False,
    )
    next(wide_out_steps)
    gain_wide[...] = jnp.zeros_like(gain_wide)
    gain_head[...] = jnp.zeros_like(gain_head)
    total = jnp.zeros((16, 128), f32)
    for n in range(16):
        entry = w_kvo[n, depth:, 0:128].astype(f32)
        gain_wide[0:2, n * 128 : (n + 1) * 128] = entry[0:2]
        total = total + entry
    gain_head[0:2, :] = total[2:4]

    def normalise(at):
        scaled = tokens[at, :].astype(f32) * inverse[at, 0:1] * gain_wide[0:1, :]
        normed[at, :] = scaled.astype(bf16)

    each_rows(rows, 32, normalise)
    kept.append(copies.local(normed, normed_out))

    def project(weights, at):
        return jnp.dot(normed[at, :], weights.reshape(width, cols), preferred_element_type=f32)

    for s in range(seqs):
        at = pl.ds(s * seq_dev, seq_dev)
        raw = project(w_kvo[:, 0:depth, 0:cols], at)
        kv_raw[at, :] = raw
        key = prepare_head(raw[:, :head], gain_head[1:2, :], cosine[...], sine[...])
        kv_own[at, :head] = key.astype(bf16)
        kv_own[at, head:] = raw[:, head:].astype(bf16)
    all_steps = batch_gather(kv_own, kv_all, True)
    next(all_steps)
    for _ in b_steps:
        pass
    kept.append(copies.local(w_qg, wide_qg))
    for s in range(seqs):
        at = pl.ds(s * seq_dev, seq_dev)
        raw = project(w_qg[:, :, 0:cols], at)
        query_raw[at, :] = raw
        for h in range(heads):
            values = prepare_head(
                raw[:, h * head : (h + 1) * head], gain_head[0:1, :], cosine[...], sine[...]
            )
            queries[s, h * seq_dev : (h + 1) * seq_dev, :] = values.astype(bf16)
        gate_raw[at, :] = project(w_qg[:, :, cols:], at)

    target_load.wait()
    seq_weights = []
    for s in range(seqs):
        domain = domain_ids[s]
        level = jnp.full((1, 128), loss_weights[weight_index[domain]], f32)
        count = jnp.full((1, 128), domain_counts[domain], jnp.int32).astype(f32)
        seq_weights.append((level * (16 * seq_dev) / count)[:, 0:1])

        def weigh(at):
            at = pl.ds(s * seq_dev + at.start, at.size)
            low[at, :] = (target[at, :].astype(f32) * seq_weights[s]).astype(bf16)

        each_rows(seq_dev, 32, weigh)
    kept.append(copies.local(low, low_out))
    own_weight = jnp.where(tensor.t < 4, seq_weights[0], seq_weights[1])

    def weigh_own(at):
        there = pl.ds(pl.multiple_of(tensor.t * own_rows + at.start, 16), at.size)
        inputs_own[at, :] = tokens[there, :]
        grad_final[at, :] = target[there, :].astype(f32) * own_weight

    each_rows(own_rows, 16, weigh_own)
    kept += [
        copies.local(value, place)
        for value, place in (
            (query_raw, query_raw_out),
            (kv_raw, kv_raw_out),
            (gate_raw, gate_raw_out),
            (queries, queries_out),
            (inputs_own, inputs_own_out),
            (grad_final, grad_final_out),
        )
    ]
    factor = scale * math.log2(math.e)
    ones = jnp.ones((2 * seq_dev, head), bf16)
    tile = head_rows // 4
    acc[...] = jnp.zeros_like(acc)

    def block(pair, masked):
        def body(s, carry):
            at = rows_at(s, seq_dev)
            keys = jnp.concatenate(
                [kv_all[pair * 2, at, :head], kv_all[pair * 2 + 1, at, :head]], axis=0
            )
            values = jnp.concatenate(
                [kv_all[pair * 2, at, head:], kv_all[pair * 2 + 1, at, head:]], axis=0
            )
            wide = jnp.concatenate([values, ones], axis=1)
            for i in range(4):
                here = pl.ds(i * tile, tile)
                scores = lax.dot_general(
                    queries[s, here, :], keys, (((1,), (1,)), ((), ())), preferred_element_type=f32
                )
                weights = jnp.exp2(scores * factor)
                if masked:
                    row = lax.broadcasted_iota(jnp.int32, scores.shape, 0) + (i * tile) % seq_dev
                    col = lax.broadcasted_iota(jnp.int32, scores.shape, 1)
                    ahead = (pair * 2 - b) * seq_dev
                    weights = jnp.where(col + ahead <= row, weights, 0.0)
                acc[s, here, :] += jnp.dot(weights.astype(bf16), wide, preferred_element_type=f32)
            return carry

        lax.fori_loop(0, seqs, body, 0)

    here = batch.chip(0, 0)

    def attend(ready):
        for dr, dq in ready:
            if (dr, dq) == (0, 0):
                block(here, True)
            else:
                pair = batch.chip(dr, dq)

                @pl.when(pair < here)
                def _():
                    block(pair, False)

    mlp_steps = [
        batch_gather(mlp_a, wide_a, by_mate=False),
        batch_gather(mlp_b, wide_b, by_mate=False),
        batch_gather(mlp_c, wide_c, by_mate=False),
    ]

    def finish_attention():
        kept.append(copies.local(kv_all, kv_out))
        for s in range(seqs):
            sums = acc[s, :, head:]
            lse[s] = jnp.log2(sums).T[0:1, :]
            out = acc[s, :, :head] / sums
            for h in range(heads):
                at, cols = pl.ds(s * seq_dev, seq_dev), pl.ds(h * head, head)
                part = out[h * seq_dev : (h + 1) * seq_dev]
                attended[at, cols] = part
                gated[at, cols] = (part * jax.nn.sigmoid(gate_raw[at, cols])).astype(bf16)

        kept.append(copies.local(attended, attended_out))

    def unit_rows(ref, slot):
        return ref.at[pl.ds(pl.multiple_of(slot * own_rows, 16), own_rows), :]

    exchanged = []

    def exchange():
        for step, device in zip(tensor.steps, tensor.others):
            exchanged.append(
                copies.send(unit_rows(gated, tensor.slot(*step)), rows_all.at[tensor.t], device)
            )
        rows_all[tensor.t] = unit_rows(gated, tensor.t)[...]

    def wide_out_ready():
        for _ in wide_out_steps:
            pass
        out_home.wait()
        kept.append(copies.local(w_out, w_out_out))

    def project_out():
        for copy in exchanged:
            copy.wait_recv()
        resid[...] = unit_rows(tokens, tensor.t)[...].astype(f32)

        def out_term(n, carry):
            resid[...] += lax.dot_general(
                rows_all[n],
                w_out[n].reshape(width, -1),
                (((1,), (1,)), ((), ())),
                preferred_element_type=f32,
            )
            return carry

        lax.fori_loop(0, 8, out_term, 0)

        def normalise_own(at):
            values = resid[at, :]
            mean = jnp.mean(values * values, axis=-1, keepdims=True)
            own[at, :] = (values * lax.rsqrt(mean + epsilon) * gain_wide[1:2, :]).astype(bf16)

        each_rows(own_rows, 16, normalise_own)

    own_group = Group("tensor", False)
    own_steps = gather(copies, own_group, own, lambda s: unit_rows(normed_mlp, s))
    ready = []

    def arrive():
        ready[:] = next(all_steps)

    def drain():
        for _ in all_steps:
            pass

    do = {
        "n": arrive,
        "t": lambda: attend(ready),
        "w": lambda: next(wide_out_steps),
        "m": lambda: [next(step) for step in mlp_steps],
        "a": lambda: next(mlp_steps[0]),
        "b": lambda: next(mlp_steps[1]),
        "c": lambda: next(mlp_steps[2]),
        "D": drain,
        "F": finish_attention,
        "X": exchange,
        "W": wide_out_ready,
        "R": project_out,
        "E": lambda: run_all(own_steps, *mlp_steps),
    }
    for key in FORWARD_ORDER:
        do[key]()
    for copy in exchanged:
        copy.wait_send()
    for copy in kept:
        copy.wait()


def forward(scale, seqs, small, weights, target):
    tokens, cosine = small[:2]
    rows, width = tokens.shape
    depth, cols = weights[0].shape
    ff = weights[4].shape[1]
    head = cosine.shape[1]
    own_rows = rows // 8
    heads = cols // head
    shape = jax.ShapeDtypeStruct
    pack_a, pack_b = (depth + 16, 2 * cols), (depth, 2 * cols)
    weight_a, weight_b = (16,) + pack_a, (16,) + pack_b
    weight_out = (8, 16, depth, cols)
    outs = [
        (shape((rows, width), bf16), ANY),
        (shape((rows, cols), f32), ANY),
        (shape((rows, cols), f32), ANY),
        (shape((rows, cols), f32), ANY),
        (shape((seqs, heads * rows // seqs, head), bf16), ANY),
        (shape((16, rows, cols), bf16), ANY),
        (shape((rows, cols), f32), ANY),
        (shape((seqs, 1, heads * rows // seqs), f32), VM),
        (shape((rows, cols), bf16), VM),
        (shape((rows, width), bf16), ANY),
        (shape((own_rows, width), f32), VM),
        (shape(weight_a, bf16), ANY),
        (shape(weight_b, bf16), ANY),
        (shape(weight_out, bf16), ANY),
    ]
    outs += [(shape((16, depth, ff), bf16), ANY)] * 3
    outs += [
        (shape((8, width), f32), VM),
        (shape((8, head), f32), VM),
        (shape((own_rows, width), bf16), ANY),
        (shape((own_rows, width), f32), ANY),
        (shape((rows, width), bf16), ANY),
    ]
    return pl.pallas_call(
        hoisted(functools.partial(forward_kernel, scale), 1),
        out_shape=[o for o, _ in outs],
        in_specs=[ANY] + [VM] * 2 + [SM] * 4 + [VM] * (len(small) - 7) + [ANY] * 7,
        out_specs=[s for _, s in outs],
        scratch_shapes=[
            pltpu.VMEM((rows, width), bf16),
            pltpu.VMEM((rows, 128), f32),
            pltpu.VMEM(pack_a, bf16),
            pltpu.VMEM(pack_b, bf16),
            pltpu.VMEM((depth, ff), bf16),
            pltpu.VMEM((16, 128), f32),
            pltpu.VMEM((rows, width), bf16),
            pltpu.VMEM((rows, width), bf16),
            pltpu.VMEM(weight_a, bf16),
            pltpu.VMEM(weight_b, bf16),
            pltpu.VMEM(weight_out, bf16),
            pltpu.VMEM((rows, cols), bf16),
            pltpu.VMEM((16, rows, cols), bf16),
            pltpu.VMEM((seqs, heads * rows // seqs, 2 * head), f32),
            pltpu.VMEM((8, own_rows, cols), bf16),
            pltpu.VMEM((own_rows, width), bf16),
            pltpu.VMEM((rows, cols), f32),
            pltpu.VMEM((rows, cols), f32),
            pltpu.VMEM((rows, cols), f32),
            pltpu.VMEM((rows, cols), f32),
            pltpu.VMEM((seqs, heads * rows // seqs, head), bf16),
            pltpu.VMEM((own_rows, width), bf16),
            pltpu.VMEM((own_rows, width), f32),
        ]
        + sems(24 * 8, 32)
        + hoisted_scratch([tokens]),
        name="forward",
        compiler_params=params(1, 62),
    )(*small, *weights, target)


def dot(left, right):
    return jnp.dot(left, right, preferred_element_type=f32)


def dot_t(left, right):
    return lax.dot_general(left, right, (((1,), (1,)), ((), ())), preferred_element_type=f32)


def t_dot(left, right):
    return lax.dot_general(left, right, (((0,), (0,)), ((), ())), preferred_element_type=f32)


def norm_back(values, gain, grad):
    inverse = lax.rsqrt(jnp.mean(values * values, axis=-1, keepdims=True) + epsilon)
    scaled = grad * gain
    unit = values * inverse
    inner = jnp.mean(scaled * unit, axis=-1, keepdims=True)
    return (scaled - unit * inner) * inverse, grad * unit


def unit_rows(ref, slot, rows):
    return ref.at[pl.ds(pl.multiple_of(slot * rows, 16), rows), :]


def row_unit(group, ref, rows):
    def unit(*step):
        return unit_rows(ref, group.slot(*step), rows)

    return unit


def outer(left, right, target, cols, step=512):
    for i in range(left.shape[1] // step):
        at = pl.ds(i * step, step)
        target[at, cols] = t_dot(left[:, at], right[...]).astype(target.dtype)
        yield


def mlp_kernel(
    resid,
    grad_final,
    gain_wide,
    normed_in,
    low_in,
    gate_in,
    up_in,
    down_in,
    out_in,
    down_out,
    up_part_out,
    down_part_out,
    gate_grad,
    grad_resid,
    grad_gated,
    gain_grad,
    normed,
    low,
    w_gate,
    w_up,
    w_down,
    w_out,
    hidden,
    grad_gate,
    grad_up,
    part,
    down,
    gate_part,
    up_part,
    down_part,
    own,
    total,
    units,
    gated_in,
    *rest,
):
    scratch, scratch_w = [rest[5 * n : 5 * n + 5] for n in range(4)], rest[20:26]
    copies = Copies(*rest[26:])
    tensor, batch = Group("tensor", False), Group("batch")
    rows, width = normed.shape
    own_rows = resid.shape[0]
    ff = hidden.shape[1]
    depth = gate_grad.shape[0]
    loads = [
        copies.local(a, b)
        for a, b in (
            (normed_in, normed),
            (gate_in, w_gate),
            (up_in, w_up),
            (low_in, low),
            (down_in, w_down),
            (out_in, w_out),
        )
    ]
    enter(tensor.others + near(batch))
    for load in loads[:5]:
        load.wait()

    def activate(j, carry):
        cols = rows_at(j, 256)
        gate = dot(normed[...], w_gate[:, cols])
        up = dot(normed[...], w_up[:, cols])
        back = dot(low[...], w_down[:, cols])
        sigma = jax.nn.sigmoid(gate)
        silu = gate * sigma
        hidden[:, cols] = (silu * up).astype(bf16)
        grad_up[:, cols] = (back * silu).astype(bf16)
        grad_gate[:, cols] = (back * up * (sigma * (1.0 + gate * (1.0 - sigma)))).astype(bf16)
        return carry

    lax.fori_loop(0, ff // 256, activate, 0)

    def input_part(j, carry):
        cols = pl.ds(j * (width // 4), width // 4)
        value = dot_t(grad_gate[...], w_gate[cols, :]) + dot_t(grad_up[...], w_up[cols, :])
        part[:, cols] = value.astype(bf16)
        return carry

    steps = []
    for n in range(4):
        input_part(n, 0)
        steps.append(
            reduce(
                copies,
                tensor,
                row_unit(tensor, chunk(part, n, 4), own_rows),
                scratch[n],
                chunk(grad_resid, n, 4),
            )
        )
        next(steps[n])
    gens = dict(zip("0123", steps))
    kept = []

    def products():
        yield from outer(normed, grad_gate, gate_part, slice(None))
        gens["w"] = reduce(
            copies, batch, row_unit(batch, gate_part, depth), scratch_w, gate_grad, by_mate=False
        )
        next(gens["w"])
        yield from outer(normed, grad_up, up_part, slice(None))
        kept.append(copies.local(up_part, up_part_out))
        yield from outer(low, hidden, down_part, slice(None))
        kept.append(copies.local(down_part, down_part_out))
        for j in range(4):
            cols = pl.ds(j * (width // 4), width // 4)
            down[:, cols] = dot_t(hidden[...], w_down[cols, :]).astype(bf16)
            yield
        kept.append(copies.local(down, down_out))

    gens["f"] = products()
    for key in MLP_ORDER:
        next(gens.get(key, iter(())), None)
    for step in (gens["f"], *steps):
        for _ in step:
            pass
    weight_steps = gens["w"]
    total[...] = jnp.zeros_like(total)

    def body(at):
        back, terms = norm_back(resid[at, :], gain_wide[1:2, :], grad_resid[at, :])
        back = grad_final[at, :] + back
        total[...] += terms
        grad_resid[at, :] = back
        own[at, :] = back.astype(bf16)

    each_rows(own_rows, 16, body)
    gain_grad[...] = jnp.sum(total[...], axis=0, keepdims=True)
    loads[5].wait()

    def gated_unit(n, carry):
        units[n] = dot(own[...], w_out[n].reshape(width, -1)).astype(bf16)
        return carry

    lax.fori_loop(0, 8, gated_unit, 0)
    exchanged = [
        copies.send(units.at[tensor.slot(*step)], gated_in.at[tensor.t], device)
        for step, device in zip(tensor.steps, tensor.others)
    ]
    gated_in[tensor.t] = units[tensor.t]
    for _ in weight_steps:
        pass
    for copy in exchanged:
        copy.wait_recv()
    for n in range(8):
        grad_gated[n * own_rows : (n + 1) * own_rows, :] = gated_in[n]
    for copy in exchanged:
        copy.wait_send()
    for copy in kept:
        copy.wait()


def mlp(resid, grad_final, gain, normed, low, weights, w_out):
    own_rows, width = resid.shape
    rows = normed.shape[0]
    ff = weights[0].shape[1]
    cols = w_out.shape[3]
    depth = width // 16
    shape = jax.ShapeDtypeStruct
    return pl.pallas_call(
        mlp_kernel,
        out_shape=[
            shape((rows, width), bf16),
            shape((width, ff), bf16),
            shape((width, ff), bf16),
            shape((depth, ff), f32),
            shape((own_rows, width), f32),
            shape((rows, cols), bf16),
            shape((1, width), f32),
        ],
        in_specs=[VM] * 3 + [ANY] * 6,
        out_specs=[ANY] * 3 + [VM] * 4,
        scratch_shapes=[pltpu.VMEM((rows, width), bf16)] * 2
        + [pltpu.VMEM((width, ff), bf16)] * 3
        + [pltpu.VMEM(w_out.shape, bf16)]
        + [pltpu.VMEM((rows, ff), bf16)] * 3
        + [pltpu.VMEM((rows, width), bf16)] * 2
        + [pltpu.VMEM((width, ff), bf16)] * 3
        + [
            pltpu.VMEM((own_rows, width), bf16),
            pltpu.VMEM((16, width), f32),
            pltpu.VMEM((8, own_rows, cols), bf16),
            pltpu.VMEM((8, own_rows, cols), bf16),
        ]
        + reduce_scratch(own_rows, width // 4, False) * 4
        + reduce_scratch(depth, ff, True)
        + sems(100, 12),
        name="mlp",
        compiler_params=params(2, 62),
    )(resid, grad_final, gain, normed, low, *weights, w_out)


def attention_kernel(
    scale,
    input_loads,
    queries,
    attended,
    gate_raw,
    grad_gated,
    grad_resid,
    resid,
    lse,
    kv_in,
    down_in,
    up_in,
    grad_query,
    kv_grad,
    gate_grad,
    low,
    final,
    up_grad,
    kv_all,
    down,
    up_part,
    own,
    grad_att,
    query_t,
    grad_t,
    delta,
    acc,
    grad_query_t,
    dkv,
    down_sum,
    *rest,
):
    scratch_kv, scratch_d, scratch_w = rest[:6], rest[6:11], rest[11:17]
    copies = Copies(*rest[17:])
    tensor, batch = Group("tensor", False), Group("batch")
    b = lax.axis_index("batch")
    seqs, head_rows, head = queries.shape
    rows, cols = attended.shape
    seq_dev = rows // seqs
    heads = cols // head
    own_rows, width = resid.shape
    depth = up_grad.shape[0]
    factor = scale * math.log2(math.e)
    loads = [copies.local(a, c) for a, c in ((up_in, up_part), (down_in, down), (kv_in, kv_all))]
    enter(near(tensor, batch))
    for load in input_loads:
        load.wait()

    def round_own(at):
        own[at, :] = grad_resid[at, :].astype(bf16)

    each_rows(own_rows, 16, round_own)
    low_steps = gather(
        copies, tensor, own, lambda s: unit_rows(low, s, own_rows), by_mate=False
    )
    next(low_steps)
    loads[0].wait()
    up_steps = reduce(
        copies, batch, row_unit(batch, up_part, depth), scratch_w, up_grad, by_mate=False
    )
    next(up_steps)
    for s in range(seqs):
        at = pl.ds(s * seq_dev, seq_dev)
        for h in range(heads):
            here, there = pl.ds(h * head, head), pl.ds(h * seq_dev, seq_dev)
            sigma = jax.nn.sigmoid(gate_raw[at, here])
            value = grad_gated[at, here].astype(f32)
            out = attended[at, here]
            low_grad = (value * sigma).astype(bf16)
            grad_att[s, there, :] = low_grad
            gate_grad[at, here] = (value * out * (sigma * (1.0 - sigma))).astype(bf16)
            acc[s, there, :] = low_grad.astype(f32) * out
        delta[s] = jnp.sum(acc[s].T, axis=0, keepdims=True)
        grad_t[s] = grad_att[s].astype(f32).T.astype(bf16)
        query_t[s] = queries[s].astype(f32).T.astype(bf16)
    for s in range(seqs):
        grad_query_t[s] = jnp.zeros((head, head_rows), f32)
    loads[1].wait()
    loads[2].wait()

    def block(chip, masked):
        for s in range(seqs):
            at = pl.ds(s * seq_dev, seq_dev)
            slots = (chip * 2, chip * 2 + 1)
            keys = jnp.concatenate([kv_all[slot, at, :head] for slot in slots], axis=0)
            values = jnp.concatenate([kv_all[slot, at, head:] for slot in slots], axis=0)
            probs = jnp.exp2(dot(keys, query_t[s]) * factor - lse[s])
            if masked:
                key = lax.broadcasted_iota(jnp.int32, probs.shape, 0)
                col = lax.broadcasted_iota(jnp.int32, probs.shape, 1)
                row = jnp.where(col >= seq_dev, col - seq_dev, col)
                ahead = (chip * 2 - b) * seq_dev
                probs = jnp.where(key + ahead <= row, probs, 0.0)
            grad_probs = dot(values, grad_t[s])
            grad_scores = (probs * (grad_probs - delta[s])).astype(bf16)
            key_part = (dot(grad_scores, queries[s]) * scale).astype(bf16)
            value_part = dot(probs.astype(bf16), grad_att[s]).astype(bf16)
            for n, slot in enumerate(slots):
                here = slice(n * seq_dev, (n + 1) * seq_dev)
                dkv[slot, at, :head] = key_part[here]
                dkv[slot, at, head:] = value_part[here]
            grad_query_t[s] += t_dot(keys, grad_scores)

    def pair(chip, own_pair):
        if own_pair:
            block(chip, True)
            return
        here = batch.chip(0, 0)

        @pl.when(chip < here)
        def _():
            block(chip, False)

        @pl.when(chip > here)
        def _():
            for n in range(2):
                dkv[chip * 2 + n] = jnp.zeros(dkv.shape[1:], bf16)

    kv_steps = reduce(
        copies,
        batch,
        lambda dr, dq, dc: dkv.at[batch.slot(dr, dq, dc)],
        scratch_kv,
        kv_grad,
        early=True,
    )
    down_steps = reduce(
        copies, tensor, row_unit(tensor, down, own_rows), scratch_d, down_sum, by_mate=False
    )
    pairs = iter(ORDER)

    def next_pair():
        dr, dq = next(pairs)
        pair(batch.chip(dr, dq), (dr, dq) == (0, 0))

    gens = {"k": kv_steps, "l": low_steps, "d": down_steps, "u": up_steps}
    for key in ATTENTION_ORDER:
        if key == "P":
            next_pair()
        else:
            next(gens.get(key, iter(())), None)
    for s in range(seqs):
        value = grad_query_t[s].T * scale
        for h in range(heads):
            grad_query[s * seq_dev : (s + 1) * seq_dev, h * head : (h + 1) * head] = value[
                h * seq_dev : (h + 1) * seq_dev
            ]
    run_all(kv_steps, down_steps, low_steps, up_steps)
    add_rows(final, [down_sum, resid])


def attention_back(
    scale, queries, lse, attended, gate_raw, grad_gated, grad_resid, resid, kv_all, down, up_part
):
    rows, cols = attended.shape
    own_rows, width = resid.shape
    seqs, head_rows, head = queries.shape
    ff = up_part.shape[1]
    depth = width // 16
    shape = jax.ShapeDtypeStruct
    hoist = (queries, attended, gate_raw, grad_gated, grad_resid, resid)
    return pl.pallas_call(
        hoisted(functools.partial(attention_kernel, scale), 6),
        out_shape=[
            shape((rows, cols), f32),
            shape((rows, cols), f32),
            shape((rows, cols), bf16),
            shape((rows, width), bf16),
            shape((own_rows, width), bf16),
            shape((depth, ff), f32),
        ],
        in_specs=[ANY] * 6 + [VM] + [ANY] * 3,
        out_specs=[VM] * 3 + [ANY] + [VM] * 2,
        scratch_shapes=[
            pltpu.VMEM(kv_all.shape, bf16),
            pltpu.VMEM((rows, width), bf16),
            pltpu.VMEM((width, ff), bf16),
            pltpu.VMEM((own_rows, width), bf16),
            pltpu.VMEM(queries.shape, bf16),
            pltpu.VMEM((seqs, head, head_rows), bf16),
            pltpu.VMEM((seqs, head, head_rows), bf16),
            pltpu.VMEM((seqs, 1, head_rows), f32),
            pltpu.VMEM(queries.shape, f32),
            pltpu.VMEM((seqs, head, head_rows), f32),
            pltpu.VMEM(kv_all.shape, bf16),
            pltpu.VMEM((own_rows, width), f32),
        ]
        + reduce_scratch(rows, cols, True)
        + reduce_scratch(own_rows, width, False)
        + reduce_scratch(depth, ff, True)
        + sems(72, 6)
        + hoisted_scratch(hoist),
        name="attention_back",
        compiler_params=params(3, 62),
    )(*hoist, lse, kv_all, down, up_part)


def last_kernel(
    share,
    input_loads,
    grad_query,
    kv_grad,
    gate_grad,
    query_raw,
    kv_raw,
    cosine,
    sine,
    gain_wide,
    gain_head,
    inputs,
    grad_resid,
    final,
    gated,
    norm_mlp_grad,
    normed_in,
    low_in,
    kvo_in,
    qg_in,
    down_in,
    tokens,
    output,
    query_grad,
    key_grad,
    value_grad,
    gate_out_grad,
    out_grad,
    down_grad,
    norm_attn_grad,
    norm_mlp_out,
    gain_query_grad,
    gain_key_grad,
    normed,
    low,
    w_kvo,
    w_qg,
    down_part,
    weight_grad,
    down_sum,
    qg_low,
    kv_low,
    part,
    weight_part,
    held,
    own,
    total,
    mine,
    over_tensor,
    shares,
    over_batch,
    *rest,
):
    scratch = [rest[5 * n : 5 * n + 5] for n in range(4)]
    scratch_w, scratch_d = rest[20:26], rest[26:32]
    copies = Copies(*rest[32:])
    tensor, batch = Group("tensor", False), Group("batch")
    rows, width = normed.shape
    own_rows = inputs.shape[0]
    cols = grad_query.shape[1]
    head = gain_head.shape[1]
    seq_dev = cosine.shape[0]
    depth = weight_grad.shape[0]
    loads = [
        copies.local(a, c)
        for a, c in (
            (qg_in, w_qg),
            (kvo_in, w_kvo),
            (down_in, down_part),
            (normed_in, normed),
            (low_in, low),
        )
    ]
    b = lax.axis_index("batch")
    members = [(0, dq, dr, dc) for dc in range(2) for dq, dr in [(0, 0)] + batch_steps(batch)][1:]
    batch_others = [(batch.slot(dr, dq, dc), batch.t) for _, dq, dr, dc in members]
    enter(tensor.others + batch_others)
    for load in input_loads:
        load.wait()

    def place(ref):
        def unit(slot):
            seq, rest = lax.div(slot, 4), lax.rem(slot, 4)
            return ref.at[seq, pl.ds(pl.multiple_of(rest * own_rows, 16), own_rows), :]

        return unit

    output_steps = gather(copies, tensor, final, place(output), by_mate=False)
    next(output_steps)

    def head_back(raw, gain, grad, at):
        back = grad * cosine[...] - pltpu.roll(grad, head // 2, 1) * sine[...]
        values, terms = norm_back(raw, gain, back)
        return values.astype(bf16), jnp.sum(terms, axis=0, keepdims=True)

    mine[...] = jnp.zeros_like(mine)
    norm_rows = width // 128
    for s in range(rows // seq_dev):
        at = pl.ds(s * seq_dev, seq_dev)
        for h in range(cols // head):
            here = pl.ds(h * head, head)
            qg_low[at, here], terms = head_back(
                query_raw[at, here], gain_head[0:1, :], grad_query[at, here], at
            )
            mine[2 * norm_rows : 2 * norm_rows + 1, :] += terms
        kv_low[at, :head], terms = head_back(
            kv_raw[at, :head], gain_head[1:2, :], kv_grad[at, :head], at
        )
        mine[2 * norm_rows + 1 : 2 * norm_rows + 2, :] += terms
        kv_low[at, head:] = kv_grad[at, head:].astype(bf16)
        qg_low[at, cols:] = gate_grad[at, :]
    loads[0].wait()
    loads[1].wait()
    def part_chunk(n):
        slots = pl.ds(n * 4, 4)
        value = dot_t(qg_low[...], w_qg[slots].reshape(width // 4, 2 * cols))
        value += dot_t(kv_low[...], w_kvo[slots, :depth, :cols].reshape(width // 4, cols))
        part[:, n * (width // 4) : (n + 1) * (width // 4)] = value.astype(bf16)

    steps = []
    for n in range(4):
        part_chunk(n)
        steps.append(
            reduce(
                copies,
                tensor,
                row_unit(tensor, chunk(part, n, 4), own_rows),
                scratch[n],
                chunk(held, n, 4),
            )
        )
        next(steps[n])
    gens = dict(zip("0123", steps))
    gens["o"] = output_steps

    def products():
        for load in loads[2:]:
            load.wait()
        gens["d"] = reduce(
            copies, batch, row_unit(batch, down_part, depth), scratch_d, down_sum, by_mate=False
        )
        next(gens["d"])
        yield
        yield from outer(normed, qg_low, weight_part, slice(0, 2 * cols))
        yield from outer(normed, kv_low, weight_part, slice(2 * cols, 3 * cols), 1024)
        yield from outer(low, gated, weight_part, slice(3 * cols, 4 * cols), 1024)
        gens["w"] = reduce(
            copies, batch, row_unit(batch, weight_part, depth), scratch_w, weight_grad, by_mate=False
        )
        next(gens["w"])

    gens["f"] = products()
    for n in range(norm_rows):
        mine[norm_rows + n : norm_rows + n + 1, :] = norm_mlp_grad[:, n * 128 : (n + 1) * 128]

    def small():
        first = [
            copies.send(mine, over_tensor.at[tensor.t], device) for device in tensor.others
        ]
        over_tensor[tensor.t] = mine[...]
        yield
        for copy in first:
            copy.wait_recv()
        total_t = over_tensor[0]
        for n in range(1, 8):
            total_t = total_t + over_tensor[n]
        for n in range(16):
            shares[n, 0:1, :] = total_t[n : n + 1]
            shares[n, 1:2, :] = total_t[norm_rows + n : norm_rows + n + 1]
            shares[n, 2:4, :] = total_t[2 * norm_rows : 2 * norm_rows + 2]
            shares[n, 4:8, :] = jnp.zeros((4, 128), f32)
        second = [
            copies.send(shares.at[batch.slot(dr, dq, dc)], over_batch.at[b], device)
            for (_, dq, dr, dc), device in zip(members, batch_others)
        ]
        over_batch[b] = shares[b]
        yield
        for copy in second:
            copy.wait_recv()
        total_b = over_batch[0]
        for n in range(1, 16):
            total_b = total_b + over_batch[n]
        heads_own = pltpu.roll(total_b, (128 - share * b) % 128, 1)
        norm_attn_grad[...] = total_b[0:1]
        norm_mlp_out[...] = total_b[1:2]
        gain_query_grad[...] = heads_own[2:3, 0:share]
        gain_key_grad[...] = heads_own[3:4, 0:share]
        for copy in first + second:
            copy.wait_send()

    def along():
        for step in steps:
            for _ in step:
                pass
        total[...] = jnp.zeros_like(total)

        def body(at):
            back, terms = norm_back(inputs[at, :].astype(f32), gain_wide[0:1, :], held[at, :])
            total[...] += terms
            own[at, :] = (grad_resid[at, :] + back).astype(bf16)

        each_rows(own_rows, 16, body)
        gain_row = jnp.sum(total[...], axis=0, keepdims=True)
        for n in range(norm_rows):
            mine[n : n + 1, :] = gain_row[:, n * 128 : (n + 1) * 128]
        big = gather(copies, tensor, own, place(tokens))
        few = small()
        for _ in big:
            next(few, None)
            yield
        yield from few

    gens["x"] = along()
    for key in LAST_ORDER:
        next(gens.get(key, iter(())), None)
    for _ in gens["f"]:
        pass
    run_all(*[gens[key] for key in "xodw"])
    query_grad[...] = weight_grad[:, :cols]
    gate_out_grad[...] = weight_grad[:, cols : 2 * cols]
    key_grad[...] = weight_grad[:, 2 * cols : 2 * cols + head]
    value_grad[...] = weight_grad[:, 2 * cols + head : 3 * cols]
    out_grad[...] = weight_grad[:, 3 * cols :].T
    down_grad[...] = down_sum[...].T


def batch_steps(batch):
    return [(dq, dr) for dr, dq in batch.steps]


def last_step(scale_free, held_in_hbm, few_shape, share):
    grad_query, inputs = scale_free[0], scale_free[9]
    seqs = grad_query.shape[0] // scale_free[5].shape[0]
    normed, low, kvo, qg, down_part = held_in_hbm
    own_rows, width = inputs.shape
    rows, cols = grad_query.shape
    ff = down_part.shape[1]
    depth = width // 16
    shape = jax.ShapeDtypeStruct
    return pl.pallas_call(
        hoisted(functools.partial(last_kernel, share), len(scale_free)),
        out_shape=[
            shape((seqs, rows // seqs, width), bf16),
            shape((seqs, rows // seqs, width), bf16),
            shape((depth, cols), f32),
            shape((depth, cols // 2), f32),
            shape((depth, cols // 2), f32),
            shape((depth, cols), f32),
            shape((cols, depth), f32),
            shape((ff, depth), f32),
            shape((1, depth), f32),
            shape((1, depth), f32),
            shape((1, share), f32),
            shape((1, share), f32),
        ],
        in_specs=[ANY] * (len(scale_free) + len(held_in_hbm)),
        out_specs=[ANY] * 2 + [VM] * 10,
        scratch_shapes=[
            pltpu.VMEM((rows, width), bf16),
            pltpu.VMEM((rows, width), bf16),
            pltpu.VMEM(kvo.shape, bf16),
            pltpu.VMEM(qg.shape, bf16),
            pltpu.VMEM((width, ff), bf16),
            pltpu.VMEM((depth, 4 * cols), f32),
            pltpu.VMEM((depth, ff), f32),
            pltpu.VMEM((rows, 2 * cols), bf16),
            pltpu.VMEM((rows, cols), bf16),
            pltpu.VMEM((rows, width), bf16),
            pltpu.VMEM((width, 4 * cols), bf16),
            pltpu.VMEM((own_rows, width), f32),
            pltpu.VMEM((own_rows, width), bf16),
            pltpu.VMEM((16, width), f32),
            pltpu.VMEM(few_shape, f32),
            pltpu.VMEM((8,) + few_shape, f32),
            pltpu.VMEM((16, 8, 128), f32),
            pltpu.VMEM((16, 8, 128), f32),
        ]
        + reduce_scratch(own_rows, width // 4, False) * 4
        + reduce_scratch(depth, 4 * cols, True)
        + reduce_scratch(depth, ff, True)
        + sems(180, 12)
        + hoisted_scratch(scale_free),
        name="projections_back",
        compiler_params=params(4, 62),
    )(*scale_free, *held_in_hbm)


def shards(
    tokens,
    target,
    domain_ids,
    domain_counts,
    weight_index,
    loss_weights,
    w_query,
    w_key,
    w_value,
    w_gate_out,
    w_output,
    w_gate,
    w_up,
    w_down,
    norm_attn,
    norm_mlp,
    gain_query,
    gain_key,
):
    seq_count, seq_dev, width = tokens.shape
    rows = seq_count * seq_dev
    members = lax.axis_size("tensor")
    batch_count = lax.axis_size("batch")
    b, t = lax.axis_index("batch"), lax.axis_index("tensor")
    own_rows = rows // members
    seq_len = seq_dev * batch_count
    head = gain_query.shape[0] * batch_count
    scale = head ** (-0.5)
    q_cols, k_cols = w_query.shape[1], w_key.shape[1]
    heads = q_cols // head

    half_size = head // 2
    pos_local = (b * seq_dev + jnp.arange(seq_dev, dtype=jnp.int32)).astype(f32)
    inverse_freq = rope_base ** (-(jnp.arange(head) % half_size).astype(f32) / half_size)
    angles = pos_local[:, None] * inverse_freq[None, :]
    sign = jnp.where(jnp.arange(head) < half_size, -1.0, 1.0).astype(f32)
    cosine_wide, sine_wide = jnp.cos(angles), jnp.sin(angles) * sign

    tokens_low = tokens.reshape(rows, width)
    ff = w_gate.shape[1]
    (
        normed_low,
        query_raw,
        kv_raw,
        gate_raw,
        queries,
        kv_all,
        attended,
        lse,
        gated_low,
        normed_mlp_low,
        resid_own,
        wide_kvo,
        wide_qg,
        w_out_all,
        wide_gate,
        wide_up,
        wide_down,
        gain_wide,
        gain_head,
        inputs_own,
        grad_final_own,
        grad_final_low,
    ) = forward(
        scale,
        seq_count,
        (
            tokens_low,
            cosine_wide,
            sine_wide,
            domain_ids,
            domain_counts,
            weight_index,
            loss_weights,
            norm_attn[None],
            norm_mlp[None],
            gain_query[None],
            gain_key[None],
            w_output,
            w_down,
        ),
        (w_query, w_key, w_value, w_gate_out, w_gate, w_up),
        target.reshape(rows, width),
    )

    weights = [w.reshape(width, ff) for w in (wide_gate, wide_up, wide_down)]
    (
        down_part,
        up_weight_part,
        down_weight_part,
        grad_gate,
        grad_resid_own,
        grad_gated,
        norm_mlp_terms,
    ) = mlp(
        resid_own,
        grad_final_own,
        gain_wide,
        normed_mlp_low,
        grad_final_low,
        weights,
        w_out_all,
    )
    grad_query_rot, kv_grad, gate_raw_grad, grad_resid_low, final_own, grad_up = attention_back(
        scale,
        queries,
        lse,
        attended,
        gate_raw,
        grad_gated,
        grad_resid_own,
        resid_own,
        kv_all,
        down_part,
        up_weight_part,
    )
    norm_rows = width // 128
    grad_tokens, output, *grads = last_step(
        (
            grad_query_rot,
            kv_grad,
            gate_raw_grad,
            query_raw,
            kv_raw,
            cosine_wide,
            sine_wide,
            gain_wide,
            gain_head,
            inputs_own,
            grad_resid_own,
            final_own,
            gated_low,
            norm_mlp_terms,
        ),
        (normed_low, grad_resid_low, wide_kvo, wide_qg, down_weight_part),
        (2 * norm_rows + 8, 128),
        gain_query.shape[0],
    )

    return (
        output,
        grad_tokens.astype(f32),
        *grads[:5],
        grad_gate,
        grad_up,
        grads[5],
        *[g.reshape(-1) for g in grads[6:]],
    )


def solution(mesh):
    in_specs = (
        P(None, "batch", None),
        P(None, "batch", None),
        P(),
        P(),
        P(),
        P(),
        P("batch", "tensor"),
        P("batch", "tensor"),
        P("batch", "tensor"),
        P("batch", "tensor"),
        P("tensor", "batch"),
        P("batch", "tensor"),
        P("batch", "tensor"),
        P("tensor", "batch"),
        P("batch"),
        P("batch"),
        P("batch"),
        P("batch"),
    )
    out_specs = (
        P(None, "batch", None),
        P(None, "batch", None),
        P("batch", "tensor"),
        P("batch", "tensor"),
        P("batch", "tensor"),
        P("batch", "tensor"),
        P("tensor", "batch"),
        P("batch", "tensor"),
        P("batch", "tensor"),
        P("tensor", "batch"),
        P("batch"),
        P("batch"),
        P("batch"),
        P("batch"),
    )
    return jax.shard_map(shards, mesh=mesh, in_specs=in_specs, out_specs=out_specs, check_vma=False)
```

```python
import functools
import math

import jax
import jax.numpy as jnp
from jax import lax
from jax.experimental import pallas as pl
from jax.experimental.pallas import tpu as pltpu
from jax.sharding import PartitionSpec as P

MESH = pl.DeviceIdType.MESH
epsilon = 1e-06
rope_base = 1000000.0
f32 = jnp.float32
bf16 = jnp.bfloat16

FORWARD_ORDER = "ntwntwnmtnwtntDFXwabcWRE"
MLP_ORDER = "ffffffff0123wf0123wf0123wf0123wfff"
ATTENTION_ORDER = "PkuPklPkduPkPkdluPkPkduPkkkkkdldl"
LAST_ORDER = "fffffffff0123fowd0123odw0123odw" + "xodw" * 12

MIB = 2**20
ANY = pl.BlockSpec(memory_space=pl.ANY)
VM = pl.BlockSpec(memory_space=pltpu.VMEM)
SM = pl.BlockSpec(memory_space=pltpu.SMEM)


class Group:
    def __init__(self, kind, core=True):
        b = lax.axis_index("batch")
        t = lax.axis_index("tensor")
        c = lax.rem(b, 2)
        self.c, self.t = c, t
        if kind == "tensor":
            r, q = lax.div(t, 2), lax.rem(t, 2)
            self.slot = lambda dr, dq: lax.rem(r + dr, 4) * 2 + lax.rem(q + dq, 2)
            at = lambda dr, dq: (b, self.slot(dr, dq))
        else:
            q, r = lax.div(b, 8), lax.rem(lax.div(b, 2), 4)
            self.chip = lambda dr, dq: lax.rem(q + dq, 2) * 4 + lax.rem(r + dr, 4)
            self.slot = lambda dr, dq, dc=0: self.chip(dr, dq) * 2 + lax.rem(c + dc, 2)
            at = lambda dr, dq: (self.slot(dr, dq), t)
        self.core = (b + 1 - 2 * c, t) if core else None
        self.right, self.left, self.mate = at(1, 0), at(3, 0), at(0, 1)
        self.others = [at(dr, dq) for dr in range(4) for dq in range(2) if dr or dq]
        self.steps = [(dr, dq) for dr in range(4) for dq in range(2) if dr or dq]


def enter(devices):
    barrier = pltpu.get_barrier_semaphore()
    for device in devices:
        pl.semaphore_signal(barrier, inc=1, device_id=device, device_id_type=MESH)
    pl.semaphore_wait(barrier, len(devices))


def near(*groups):
    devices = [d for g in groups for d in (g.right, g.left, g.mate)]
    cores = [g.core for g in groups if g.core is not None]
    return devices + cores[:1]


class Copies:
    def __init__(self, send_sem, recv_sem, local_sem):
        self.send_sem, self.recv_sem, self.local_sem = send_sem, recv_sem, local_sem
        self.count = 0
        self.locals = 0

    def send(self, source, target, device):
        copy = pltpu.make_async_remote_copy(
            src_ref=source,
            dst_ref=target,
            send_sem=self.send_sem.at[self.count],
            recv_sem=self.recv_sem.at[self.count],
            device_id=device,
            device_id_type=MESH,
        )
        self.count += 1
        copy.start()
        return copy

    def local(self, source, target):
        copy = pltpu.make_async_copy(source, target, self.local_sem.at[self.locals])
        self.locals += 1
        copy.start()
        return copy


def half_of(ref, which):
    width = ref.shape[-1] // 2
    lead = (slice(None),) * (len(ref.shape) - 1)
    return ref.at[lead + (pl.ds(which * width, width),)]


def run_all(*steps):
    waiting = list(steps)
    while waiting:
        for step in list(waiting):
            try:
                next(step)
            except StopIteration:
                waiting.remove(step)


def gather(copies, group, own, slot, split=True, source=None, by_mate=True):
    s = group.slot
    core_copies = []
    sent = []

    def push(ref, *devices):
        out = [copies.send(ref, ref, device) for device in devices]
        sent.extend(out)
        return out

    def to_core(ref):
        if group.core is not None:
            core_copies.extend(push(ref, group.core))

    def core_wait(count):
        for copy in core_copies[:count]:
            copy.wait_recv()
        del core_copies[:count]

    def onward(unit, way):
        if way == 0:
            return push(half_of(unit, 0) if split else unit, group.right)
        return push(half_of(unit, 1), group.left) if split else []

    home = slot(s(0, 0))
    source = own if source is None else source
    first = [copies.send(source, home, d) for d in (group.right, group.left, group.mate)]
    sent.extend(first)
    kept = None
    if own is not None:
        kept = copies.local(own, home)
        if group.core is not None:
            core_copies.append(copies.send(own, home, group.core))
            sent.append(core_copies[0])
    from_left, from_right, from_mate = first
    yield []
    far = []
    for way, copy in enumerate((from_left, from_right)):
        copy.wait_recv()
        unit = slot(s(3 - 2 * way, 0))
        far += onward(unit, way)
        to_core(unit)
    from_mate.wait_recv()
    mate_unit = slot(s(0, 1))
    mate_line = push(mate_unit, group.right, group.left)
    to_core(mate_unit)
    if own is not None:
        core_wait(1)
        kept.wait()
    yield [(0, 0)]
    mate_far = []
    for copy in far:
        copy.wait_recv()
    if by_mate:
        mate_far += push(slot(s(2, 0)), group.mate)
    to_core(slot(s(2, 0)))
    yield []
    for way, copy in enumerate(mate_line):
        copy.wait_recv()
        unit = slot(s(3 - 2 * way, 1))
        if not by_mate:
            mate_far += onward(unit, way)
        to_core(unit)
    core_wait(3)
    yield [(3, 0), (1, 0), (0, 1)]
    for copy in mate_far:
        copy.wait_recv()
    to_core(slot(s(2, 1)))
    core_wait(3)
    yield [(2, 0), (3, 1), (1, 1)]
    core_wait(1)
    yield [(2, 1)]
    for copy in sent:
        copy.wait_send()


def chunk(ref, n, count):
    width = ref.shape[-1] // count
    return ref.at[:, pl.ds(n * width, width)]


def add_rows(target, sources, step=16):
    def body(at):
        total = sources[0][at, :].astype(f32)
        for source in sources[1:]:
            total = total + source[at, :].astype(f32)
        target[at, :] = total.astype(target.dtype)

    each_rows(target.shape[0], step, body)


def rows_at(i, step=16):
    return pl.ds(pl.multiple_of(i * step, step), step)


def each_rows(rows, step, body):
    def run(i, carry):
        body(rows_at(i, step))
        return carry

    lax.fori_loop(0, rows // step, run, 0)


def reduce_scratch(rows, width, core):
    shapes = [
        pltpu.VMEM((4, rows, width // 2), bf16),
        pltpu.VMEM((4, rows, width), bf16),
        pltpu.VMEM((4, rows, width), bf16),
        pltpu.VMEM((3, rows, width), bf16),
        pltpu.VMEM((2, rows, width), bf16),
    ]
    if core:
        shapes += [pltpu.VMEM((8, rows, width), bf16)]
    return shapes


ORDER = [(2, 1), (1, 1), (3, 1), (2, 0), (1, 0), (3, 0), (0, 1), (0, 0)]


def reduce(copies, group, part, scratch, result, early=False, by_mate=True):
    far, near_in, outgoing, mates, far_sums = scratch[:5]
    core = group.core is not None
    sent = []

    def send(source, target, device):
        copy = copies.send(source, target, device)
        sent.append(copy)
        return copy

    arrived = {}

    def to_core(n):
        dr, dq = ORDER[n]
        arrived[dr, dq] = (send(part(dr, dq, 1), scratch[5].at[n], group.core), n)

    def terms(dr, dq):
        if not core:
            return [part(dr, dq)]
        copy, n = arrived[dr, dq]
        copy.wait_recv()
        return [part(dr, dq, 0), scratch[5].at[n]]

    sides = ((1, group.right), (3, group.left))

    def far_sends(unit, line):
        return [
            send(half_of(unit, way), far.at[line * 2 + way], device)
            for way, (_, device) in enumerate(sides)
        ]

    def line_sends(line, far_copies):
        out = []
        for way, (dr, device) in enumerate(sides):
            unit = terms(dr, line)
            held = outgoing.at[line * 2 + way]
            if far_copies is not None:
                far_copies[way].wait_recv()
                there = far.at[line * 2 + way]
                add_rows(half_of(held, way), [half_of(u, way) for u in unit] + [there])
                add_rows(half_of(held, 1 - way), [half_of(u, 1 - way) for u in unit])
            elif core:
                add_rows(held, unit)
            else:
                held = unit[0]
            out.append(send(held, near_in.at[line * 2 + way], device))
        return out

    def first():
        unit = terms(2, 1)
        if core:
            add_rows(far_sums.at[1], unit)
            unit = [far_sums.at[1]]
        if by_mate:
            return send(unit[0], mates.at[2], group.mate), line_sends(1, None)
        return None, far_sends(unit[0], 1)

    def second():
        unit = terms(2, 0)
        if by_mate:
            far_mate.wait_recv()
            unit = unit + [mates.at[2]]
        if len(unit) > 1:
            add_rows(far_sums.at[0], unit)
            unit = [far_sums.at[0]]
        return far_sends(unit[0], 0)

    def third():
        return line_sends(0, far_copies)

    if early:
        for n in range(3):
            to_core(n)
            yield
        to_core(3)
        far_mate, mate_line = first()
        yield
        to_core(4)
        far_copies = second()
        yield
        to_core(5)
        yield
        to_core(6)
        own_line = third()
        yield
        to_core(7)
    else:
        if core:
            for n in range(8):
                to_core(n)
            yield
        far_mate, mate_line = first()
        yield
        far_copies = second()
        yield
        if not by_mate:
            mate_line = line_sends(1, mate_line)
        own_line = third()
    yield
    unit = terms(0, 1)
    for copy in mate_line:
        copy.wait_recv()
    add_rows(mates.at[0], unit + [near_in.at[2], near_in.at[3]])
    to_mate = send(mates.at[0], mates.at[1], group.mate)
    yield
    unit = terms(0, 0)
    for copy in own_line:
        copy.wait_recv()
    to_mate.wait_recv()
    add_rows(result, unit + [near_in.at[0], near_in.at[1], mates.at[1]])
    for copy in sent:
        copy.wait_send()


def hoisted(kernel, count):
    def run(*refs):
        sources, rest = refs[:count], refs[count : -count - 1]
        held, sem = refs[-count - 1 : -1], refs[-1]
        loads = [
            pltpu.make_async_copy(source, place, sem.at[n])
            for n, (source, place) in enumerate(zip(sources, held))
        ]
        for load in loads:
            load.start()
        kernel(loads, *held, *rest)

    return run


def hoisted_scratch(arrays):
    held = [pltpu.VMEM(a.shape, a.dtype) for a in arrays]
    return held + [pltpu.SemaphoreType.DMA((len(held),))]


def sems(remote, local):
    return [
        pltpu.SemaphoreType.DMA((remote,)),
        pltpu.SemaphoreType.DMA((remote,)),
        pltpu.SemaphoreType.DMA((max(local, 1),)),
    ]


def params(collective, limit=48):
    return pltpu.CompilerParams(
        collective_id=collective, has_side_effects=True, vmem_limit_bytes=limit * MIB
    )


def prepare_head(values, gain, cosine, sine):
    half_size = values.shape[1] // 2
    mean = jnp.mean(values * values, axis=-1, keepdims=True)
    scaled = values * lax.rsqrt(mean + epsilon) * gain
    return scaled * cosine + pltpu.roll(scaled, half_size, 1) * sine


def forward_kernel(
    scale,
    input_loads,
    tokens,
    cosine,
    sine,
    domain_ids,
    domain_counts,
    weight_index,
    loss_weights,
    norm_attn,
    norm_mlp,
    gain_query,
    gain_key,
    w_output,
    w_down,
    w_query,
    w_key,
    w_value,
    w_gate_out,
    mlp_a,
    mlp_b,
    target_in,
    normed_out,
    query_raw_out,
    kv_raw_out,
    gate_raw_out,
    queries_out,
    kv_out,
    attended_out,
    lse,
    gated,
    normed_mlp,
    resid,
    wide_kvo,
    wide_qg,
    w_out_out,
    wide_a,
    wide_b,
    wide_c,
    gain_wide,
    gain_head,
    inputs_own_out,
    grad_final_out,
    low_out,
    normed,
    inverse,
    pack_a,
    pack_b,
    mlp_c,
    few,
    target,
    low,
    w_kvo,
    w_qg,
    w_out,
    kv_own,
    kv_all,
    acc,
    rows_all,
    own,
    query_raw,
    kv_raw,
    gate_raw,
    attended,
    queries,
    inputs_own,
    grad_final,
    send_sem,
    recv_sem,
    local_sem,
):
    copies = Copies(send_sem, recv_sem, local_sem)
    tensor, batch = Group("tensor"), Group("batch")
    b = lax.axis_index("batch")
    rows, width = tokens.shape
    cols = query_raw.shape[1]
    own_rows = resid.shape[0]
    seqs, head_rows, head = queries.shape
    heads = query_raw.shape[1] // head
    seq_dev = rows // seqs
    depth, key_cols = w_key.shape
    packing = [
        copies.local(source, place)
        for source, place in (
            (w_key, pack_a.at[pl.ds(0, depth), pl.ds(0, key_cols)]),
            (w_value, pack_a.at[pl.ds(0, depth), pl.ds(key_cols, key_cols)]),
            (w_query, pack_b.at[:, pl.ds(0, cols)]),
            (w_gate_out, pack_b.at[:, pl.ds(cols, cols)]),
        )
    ]
    target_load = copies.local(target_in, target)

    def flipped(values):
        return values.astype(f32).T.astype(bf16)

    pack_a[0:depth, cols:] = flipped(w_output[...])
    few[...] = jnp.zeros_like(few)
    share = gain_query.shape[1]
    few[0:1, :] = norm_attn[...].astype(f32)
    few[1:2, :] = norm_mlp[...].astype(f32)
    few[2:3, 0:share] = gain_query[...].astype(f32)
    few[3:4, 0:share] = gain_key[...].astype(f32)
    placed = pltpu.roll(few[...], b * share, 1)
    row = lax.broadcasted_iota(jnp.int32, placed.shape, 0)
    pack_a[depth:, :] = jnp.zeros((16, pack_a.shape[1]), bf16)
    pack_a[depth:, 0:128] = jnp.where(row < 2, few[...], placed).astype(bf16)
    enter(tensor.others + near(batch))

    def batch_gather(source, target, by_mate=True):
        return gather(copies, batch, source, lambda s: target.at[s], by_mate=by_mate)

    for copy in packing:
        copy.wait()
    a_steps = batch_gather(pack_a, w_kvo, True)
    b_steps = batch_gather(pack_b, w_qg, False)
    next(a_steps)
    next(b_steps)

    for load in input_loads:
        load.wait()

    def invert(at):
        values = tokens[at, :].astype(f32)
        mean = jnp.mean(values * values, axis=-1, keepdims=True)
        inverse[at, :] = jnp.broadcast_to(lax.rsqrt(mean + epsilon), (32, 128))

    each_rows(rows, 32, invert)
    mlp_c[...] = flipped(w_down[...])
    next(a_steps)
    next(b_steps)
    for _ in a_steps:
        pass
    half = tensor.c * 8
    kept = [copies.local(w_kvo, wide_kvo)]
    out_home = copies.local(w_kvo.at[:, pl.ds(0, depth), pl.ds(cols, cols)], w_out.at[tensor.t])
    wide_out_steps = gather(
        copies,
        tensor,
        None,
        lambda s: w_out.at[s, pl.ds(half, 8)],
        source=w_kvo.at[pl.ds(half, 8), pl.ds(0, depth), pl.ds(cols, cols)],
        by_mate=False,
    )
    next(wide_out_steps)
    gain_wide[...] = jnp.zeros_like(gain_wide)
    gain_head[...] = jnp.zeros_like(gain_head)
    total = jnp.zeros((16, 128), f32)
    for n in range(16):
        entry = w_kvo[n, depth:, 0:128].astype(f32)
        gain_wide[0:2, n * 128 : (n + 1) * 128] = entry[0:2]
        total = total + entry
    gain_head[0:2, :] = total[2:4]

    def normalise(at):
        scaled = tokens[at, :].astype(f32) * inverse[at, 0:1] * gain_wide[0:1, :]
        normed[at, :] = scaled.astype(bf16)

    each_rows(rows, 32, normalise)
    kept.append(copies.local(normed, normed_out))

    def project(weights, at):
        return jnp.dot(normed[at, :], weights.reshape(width, cols), preferred_element_type=f32)

    for s in range(seqs):
        at = pl.ds(s * seq_dev, seq_dev)
        raw = project(w_kvo[:, 0:depth, 0:cols], at)
        kv_raw[at, :] = raw
        key = prepare_head(raw[:, :head], gain_head[1:2, :], cosine[...], sine[...])
        kv_own[at, :head] = key.astype(bf16)
        kv_own[at, head:] = raw[:, head:].astype(bf16)
    all_steps = batch_gather(kv_own, kv_all, True)
    next(all_steps)
    for _ in b_steps:
        pass
    kept.append(copies.local(w_qg, wide_qg))
    for s in range(seqs):
        at = pl.ds(s * seq_dev, seq_dev)
        raw = project(w_qg[:, :, 0:cols], at)
        query_raw[at, :] = raw
        for h in range(heads):
            values = prepare_head(
                raw[:, h * head : (h + 1) * head], gain_head[0:1, :], cosine[...], sine[...]
            )
            queries[s, h * seq_dev : (h + 1) * seq_dev, :] = values.astype(bf16)
        gate_raw[at, :] = project(w_qg[:, :, cols:], at)

    target_load.wait()
    seq_weights = []
    for s in range(seqs):
        domain = domain_ids[s]
        level = jnp.full((1, 128), loss_weights[weight_index[domain]], f32)
        count = jnp.full((1, 128), domain_counts[domain], jnp.int32).astype(f32)
        seq_weights.append((level * (16 * seq_dev) / count)[:, 0:1])

        def weigh(at):
            at = pl.ds(s * seq_dev + at.start, at.size)
            low[at, :] = (target[at, :].astype(f32) * seq_weights[s]).astype(bf16)

        each_rows(seq_dev, 32, weigh)
    kept.append(copies.local(low, low_out))
    own_weight = jnp.where(tensor.t < 4, seq_weights[0], seq_weights[1])

    def weigh_own(at):
        there = pl.ds(pl.multiple_of(tensor.t * own_rows + at.start, 16), at.size)
        inputs_own[at, :] = tokens[there, :]
        grad_final[at, :] = target[there, :].astype(f32) * own_weight

    each_rows(own_rows, 16, weigh_own)
    kept += [
        copies.local(value, place)
        for value, place in (
            (query_raw, query_raw_out),
            (kv_raw, kv_raw_out),
            (gate_raw, gate_raw_out),
            (queries, queries_out),
            (inputs_own, inputs_own_out),
            (grad_final, grad_final_out),
        )
    ]
    factor = scale * math.log2(math.e)
    ones = jnp.ones((2 * seq_dev, head), bf16)
    tile = head_rows // 4
    acc[...] = jnp.zeros_like(acc)

    def block(pair, masked):
        def body(s, carry):
            at = rows_at(s, seq_dev)
            keys = jnp.concatenate(
                [kv_all[pair * 2, at, :head], kv_all[pair * 2 + 1, at, :head]], axis=0
            )
            values = jnp.concatenate(
                [kv_all[pair * 2, at, head:], kv_all[pair * 2 + 1, at, head:]], axis=0
            )
            wide = jnp.concatenate([values, ones], axis=1)
            for i in range(4):
                here = pl.ds(i * tile, tile)
                scores = lax.dot_general(
                    queries[s, here, :], keys, (((1,), (1,)), ((), ())), preferred_element_type=f32
                )
                weights = jnp.exp2(scores * factor)
                if masked:
                    row = lax.broadcasted_iota(jnp.int32, scores.shape, 0) + (i * tile) % seq_dev
                    col = lax.broadcasted_iota(jnp.int32, scores.shape, 1)
                    ahead = (pair * 2 - b) * seq_dev
                    weights = jnp.where(col + ahead <= row, weights, 0.0)
                acc[s, here, :] += jnp.dot(weights.astype(bf16), wide, preferred_element_type=f32)
            return carry

        lax.fori_loop(0, seqs, body, 0)

    here = batch.chip(0, 0)

    def attend(ready):
        for dr, dq in ready:
            if (dr, dq) == (0, 0):
                block(here, True)
            else:
                pair = batch.chip(dr, dq)

                @pl.when(pair < here)
                def _():
                    block(pair, False)

    mlp_steps = [
        batch_gather(mlp_a, wide_a, by_mate=False),
        batch_gather(mlp_b, wide_b, by_mate=False),
        batch_gather(mlp_c, wide_c, by_mate=False),
    ]

    def finish_attention():
        kept.append(copies.local(kv_all, kv_out))
        for s in range(seqs):
            sums = acc[s, :, head:]
            lse[s] = jnp.log2(sums).T[0:1, :]
            out = acc[s, :, :head] / sums
            for h in range(heads):
                at, cols = pl.ds(s * seq_dev, seq_dev), pl.ds(h * head, head)
                part = out[h * seq_dev : (h + 1) * seq_dev]
                attended[at, cols] = part
                gated[at, cols] = (part * jax.nn.sigmoid(gate_raw[at, cols])).astype(bf16)

        kept.append(copies.local(attended, attended_out))

    def unit_rows(ref, slot):
        return ref.at[pl.ds(pl.multiple_of(slot * own_rows, 16), own_rows), :]

    exchanged = []

    def exchange():
        for step, device in zip(tensor.steps, tensor.others):
            exchanged.append(
                copies.send(unit_rows(gated, tensor.slot(*step)), rows_all.at[tensor.t], device)
            )
        rows_all[tensor.t] = unit_rows(gated, tensor.t)[...]

    def wide_out_ready():
        for _ in wide_out_steps:
            pass
        out_home.wait()
        kept.append(copies.local(w_out, w_out_out))

    def project_out():
        for copy in exchanged:
            copy.wait_recv()
        resid[...] = unit_rows(tokens, tensor.t)[...].astype(f32)

        def out_term(n, carry):
            resid[...] += lax.dot_general(
                rows_all[n],
                w_out[n].reshape(width, -1),
                (((1,), (1,)), ((), ())),
                preferred_element_type=f32,
            )
            return carry

        lax.fori_loop(0, 8, out_term, 0)

        def normalise_own(at):
            values = resid[at, :]
            mean = jnp.mean(values * values, axis=-1, keepdims=True)
            own[at, :] = (values * lax.rsqrt(mean + epsilon) * gain_wide[1:2, :]).astype(bf16)

        each_rows(own_rows, 16, normalise_own)

    own_group = Group("tensor", False)
    own_steps = gather(copies, own_group, own, lambda s: unit_rows(normed_mlp, s))
    ready = []

    def arrive():
        ready[:] = next(all_steps)

    def drain():
        for _ in all_steps:
            pass

    do = {
        "n": arrive,
        "t": lambda: attend(ready),
        "w": lambda: next(wide_out_steps),
        "m": lambda: [next(step) for step in mlp_steps],
        "a": lambda: next(mlp_steps[0]),
        "b": lambda: next(mlp_steps[1]),
        "c": lambda: next(mlp_steps[2]),
        "D": drain,
        "F": finish_attention,
        "X": exchange,
        "W": wide_out_ready,
        "R": project_out,
        "E": lambda: run_all(own_steps, *mlp_steps),
    }
    for key in FORWARD_ORDER:
        do[key]()
    for copy in exchanged:
        copy.wait_send()
    for copy in kept:
        copy.wait()


def forward(scale, seqs, small, weights, target):
    tokens, cosine = small[:2]
    rows, width = tokens.shape
    depth, cols = weights[0].shape
    ff = weights[4].shape[1]
    head = cosine.shape[1]
    own_rows = rows // 8
    heads = cols // head
    shape = jax.ShapeDtypeStruct
    pack_a, pack_b = (depth + 16, 2 * cols), (depth, 2 * cols)
    weight_a, weight_b = (16,) + pack_a, (16,) + pack_b
    weight_out = (8, 16, depth, cols)
    outs = [
        (shape((rows, width), bf16), ANY),
        (shape((rows, cols), f32), ANY),
        (shape((rows, cols), f32), ANY),
        (shape((rows, cols), f32), ANY),
        (shape((seqs, heads * rows // seqs, head), bf16), ANY),
        (shape((16, rows, cols), bf16), ANY),
        (shape((rows, cols), f32), ANY),
        (shape((seqs, 1, heads * rows // seqs), f32), VM),
        (shape((rows, cols), bf16), VM),
        (shape((rows, width), bf16), ANY),
        (shape((own_rows, width), f32), VM),
        (shape(weight_a, bf16), ANY),
        (shape(weight_b, bf16), ANY),
        (shape(weight_out, bf16), ANY),
    ]
    outs += [(shape((16, depth, ff), bf16), ANY)] * 3
    outs += [
        (shape((8, width), f32), VM),
        (shape((8, head), f32), VM),
        (shape((own_rows, width), bf16), ANY),
        (shape((own_rows, width), f32), ANY),
        (shape((rows, width), bf16), ANY),
    ]
    return pl.pallas_call(
        hoisted(functools.partial(forward_kernel, scale), 3),
        out_shape=[o for o, _ in outs],
        in_specs=[ANY] * 3 + [SM] * 4 + [VM] * (len(small) - 7) + [ANY] * 7,
        out_specs=[s for _, s in outs],
        scratch_shapes=[
            pltpu.VMEM((rows, width), bf16),
            pltpu.VMEM((rows, 128), f32),
            pltpu.VMEM(pack_a, bf16),
            pltpu.VMEM(pack_b, bf16),
            pltpu.VMEM((depth, ff), bf16),
            pltpu.VMEM((16, 128), f32),
            pltpu.VMEM((rows, width), bf16),
            pltpu.VMEM((rows, width), bf16),
            pltpu.VMEM(weight_a, bf16),
            pltpu.VMEM(weight_b, bf16),
            pltpu.VMEM(weight_out, bf16),
            pltpu.VMEM((rows, cols), bf16),
            pltpu.VMEM((16, rows, cols), bf16),
            pltpu.VMEM((seqs, heads * rows // seqs, 2 * head), f32),
            pltpu.VMEM((8, own_rows, cols), bf16),
            pltpu.VMEM((own_rows, width), bf16),
            pltpu.VMEM((rows, cols), f32),
            pltpu.VMEM((rows, cols), f32),
            pltpu.VMEM((rows, cols), f32),
            pltpu.VMEM((rows, cols), f32),
            pltpu.VMEM((seqs, heads * rows // seqs, head), bf16),
            pltpu.VMEM((own_rows, width), bf16),
            pltpu.VMEM((own_rows, width), f32),
        ]
        + sems(24 * 8, 32)
        + hoisted_scratch(small[:3]),
        name="forward",
        compiler_params=params(1, 62),
    )(*small, *weights, target)


def dot(left, right):
    return jnp.dot(left, right, preferred_element_type=f32)


def dot_t(left, right):
    return lax.dot_general(left, right, (((1,), (1,)), ((), ())), preferred_element_type=f32)


def t_dot(left, right):
    return lax.dot_general(left, right, (((0,), (0,)), ((), ())), preferred_element_type=f32)


def norm_back(values, gain, grad):
    inverse = lax.rsqrt(jnp.mean(values * values, axis=-1, keepdims=True) + epsilon)
    scaled = grad * gain
    unit = values * inverse
    inner = jnp.mean(scaled * unit, axis=-1, keepdims=True)
    return (scaled - unit * inner) * inverse, grad * unit


def unit_rows(ref, slot, rows):
    return ref.at[pl.ds(pl.multiple_of(slot * rows, 16), rows), :]


def row_unit(group, ref, rows):
    def unit(*step):
        return unit_rows(ref, group.slot(*step), rows)

    return unit


def outer(left, right, target, cols, step=512):
    for i in range(left.shape[1] // step):
        at = pl.ds(i * step, step)
        target[at, cols] = t_dot(left[:, at], right[...]).astype(target.dtype)
        yield


def mlp_kernel(
    input_loads,
    resid,
    grad_final,
    gain_wide,
    normed_in,
    low_in,
    gate_in,
    up_in,
    down_in,
    out_in,
    down_out,
    up_part_out,
    down_part_out,
    gate_grad,
    grad_resid,
    grad_gated,
    gain_grad,
    normed,
    low,
    w_gate,
    w_up,
    w_down,
    w_out,
    hidden,
    grad_gate,
    grad_up,
    part,
    down,
    gate_part,
    up_part,
    down_part,
    own,
    total,
    units,
    gated_in,
    *rest,
):
    scratch, scratch_w = [rest[5 * n : 5 * n + 5] for n in range(4)], rest[20:26]
    copies = Copies(*rest[26:])
    tensor, batch = Group("tensor", False), Group("batch")
    rows, width = normed.shape
    own_rows = resid.shape[0]
    ff = hidden.shape[1]
    depth = gate_grad.shape[0]
    loads = [
        copies.local(a, b)
        for a, b in (
            (normed_in, normed),
            (gate_in, w_gate),
            (up_in, w_up),
            (low_in, low),
            (down_in, w_down),
            (out_in, w_out),
        )
    ]
    enter(tensor.others + near(batch))
    for load in input_loads + loads[:5]:
        load.wait()

    def activate(j, carry):
        cols = rows_at(j, 256)
        gate = dot(normed[...], w_gate[:, cols])
        up = dot(normed[...], w_up[:, cols])
        back = dot(low[...], w_down[:, cols])
        sigma = jax.nn.sigmoid(gate)
        silu = gate * sigma
        hidden[:, cols] = (silu * up).astype(bf16)
        grad_up[:, cols] = (back * silu).astype(bf16)
        grad_gate[:, cols] = (back * up * (sigma * (1.0 + gate * (1.0 - sigma)))).astype(bf16)
        return carry

    lax.fori_loop(0, ff // 256, activate, 0)

    def input_part(j, carry):
        cols = pl.ds(j * (width // 4), width // 4)
        value = dot_t(grad_gate[...], w_gate[cols, :]) + dot_t(grad_up[...], w_up[cols, :])
        part[:, cols] = value.astype(bf16)
        return carry

    steps = []
    for n in range(4):
        input_part(n, 0)
        steps.append(
            reduce(
                copies,
                tensor,
                row_unit(tensor, chunk(part, n, 4), own_rows),
                scratch[n],
                chunk(grad_resid, n, 4),
            )
        )
        next(steps[n])
    gens = dict(zip("0123", steps))
    kept = []

    def products():
        yield from outer(normed, grad_gate, gate_part, slice(None))
        gens["w"] = reduce(
            copies, batch, row_unit(batch, gate_part, depth), scratch_w, gate_grad, by_mate=False
        )
        next(gens["w"])
        yield from outer(normed, grad_up, up_part, slice(None))
        kept.append(copies.local(up_part, up_part_out))
        yield from outer(low, hidden, down_part, slice(None))
        kept.append(copies.local(down_part, down_part_out))
        for j in range(4):
            cols = pl.ds(j * (width // 4), width // 4)
            down[:, cols] = dot_t(hidden[...], w_down[cols, :]).astype(bf16)
            yield
        kept.append(copies.local(down, down_out))

    gens["f"] = products()
    for key in MLP_ORDER:
        next(gens.get(key, iter(())), None)
    for step in (gens["f"], *steps):
        for _ in step:
            pass
    weight_steps = gens["w"]
    total[...] = jnp.zeros_like(total)

    def body(at):
        back, terms = norm_back(resid[at, :], gain_wide[1:2, :], grad_resid[at, :])
        back = grad_final[at, :] + back
        total[...] += terms
        grad_resid[at, :] = back
        own[at, :] = back.astype(bf16)

    each_rows(own_rows, 16, body)
    gain_grad[...] = jnp.sum(total[...], axis=0, keepdims=True)
    loads[5].wait()

    def gated_unit(n, carry):
        units[n] = dot(own[...], w_out[n].reshape(width, -1)).astype(bf16)
        return carry

    lax.fori_loop(0, 8, gated_unit, 0)
    exchanged = [
        copies.send(units.at[tensor.slot(*step)], gated_in.at[tensor.t], device)
        for step, device in zip(tensor.steps, tensor.others)
    ]
    gated_in[tensor.t] = units[tensor.t]
    for _ in weight_steps:
        pass
    for copy in exchanged:
        copy.wait_recv()
    for n in range(8):
        grad_gated[n * own_rows : (n + 1) * own_rows, :] = gated_in[n]
    for copy in exchanged:
        copy.wait_send()
    for copy in kept:
        copy.wait()


def mlp(resid, grad_final, gain, normed, low, weights, w_out):
    own_rows, width = resid.shape
    rows = normed.shape[0]
    ff = weights[0].shape[1]
    cols = w_out.shape[3]
    depth = width // 16
    shape = jax.ShapeDtypeStruct
    return pl.pallas_call(
        hoisted(mlp_kernel, 3),
        out_shape=[
            shape((rows, width), bf16),
            shape((width, ff), bf16),
            shape((width, ff), bf16),
            shape((depth, ff), f32),
            shape((own_rows, width), f32),
            shape((rows, cols), bf16),
            shape((1, width), f32),
        ],
        in_specs=[ANY] * 9,
        out_specs=[ANY] * 3 + [VM] * 4,
        scratch_shapes=[pltpu.VMEM((rows, width), bf16)] * 2
        + [pltpu.VMEM((width, ff), bf16)] * 3
        + [pltpu.VMEM(w_out.shape, bf16)]
        + [pltpu.VMEM((rows, ff), bf16)] * 3
        + [pltpu.VMEM((rows, width), bf16)] * 2
        + [pltpu.VMEM((width, ff), bf16)] * 3
        + [
            pltpu.VMEM((own_rows, width), bf16),
            pltpu.VMEM((16, width), f32),
            pltpu.VMEM((8, own_rows, cols), bf16),
            pltpu.VMEM((8, own_rows, cols), bf16),
        ]
        + reduce_scratch(own_rows, width // 4, False) * 4
        + reduce_scratch(depth, ff, True)
        + sems(100, 12)
        + hoisted_scratch([resid, grad_final, gain]),
        name="mlp",
        compiler_params=params(2, 62),
    )(resid, grad_final, gain, normed, low, *weights, w_out)


def attention_kernel(
    scale,
    input_loads,
    queries,
    attended,
    gate_raw,
    grad_gated,
    grad_resid,
    resid,
    lse,
    kv_in,
    down_in,
    up_in,
    grad_query,
    kv_grad,
    gate_grad,
    low,
    final,
    up_grad,
    kv_all,
    down,
    up_part,
    own,
    grad_att,
    query_t,
    grad_t,
    delta,
    acc,
    grad_query_t,
    dkv,
    down_sum,
    *rest,
):
    scratch_kv, scratch_d, scratch_w = rest[:6], rest[6:11], rest[11:17]
    copies = Copies(*rest[17:])
    tensor, batch = Group("tensor", False), Group("batch")
    b = lax.axis_index("batch")
    seqs, head_rows, head = queries.shape
    rows, cols = attended.shape
    seq_dev = rows // seqs
    heads = cols // head
    own_rows, width = resid.shape
    depth = up_grad.shape[0]
    factor = scale * math.log2(math.e)
    loads = [copies.local(a, c) for a, c in ((up_in, up_part), (down_in, down), (kv_in, kv_all))]
    enter(near(tensor, batch))
    for load in input_loads:
        load.wait()

    def round_own(at):
        own[at, :] = grad_resid[at, :].astype(bf16)

    each_rows(own_rows, 16, round_own)
    low_steps = gather(
        copies, tensor, own, lambda s: unit_rows(low, s, own_rows), by_mate=False
    )
    next(low_steps)
    loads[0].wait()
    up_steps = reduce(
        copies, batch, row_unit(batch, up_part, depth), scratch_w, up_grad, by_mate=False
    )
    next(up_steps)
    for s in range(seqs):
        at = pl.ds(s * seq_dev, seq_dev)
        for h in range(heads):
            here, there = pl.ds(h * head, head), pl.ds(h * seq_dev, seq_dev)
            sigma = jax.nn.sigmoid(gate_raw[at, here])
            value = grad_gated[at, here].astype(f32)
            out = attended[at, here]
            low_grad = (value * sigma).astype(bf16)
            grad_att[s, there, :] = low_grad
            gate_grad[at, here] = (value * out * (sigma * (1.0 - sigma))).astype(bf16)
            acc[s, there, :] = low_grad.astype(f32) * out
        delta[s] = jnp.sum(acc[s].T, axis=0, keepdims=True)
        grad_t[s] = grad_att[s].astype(f32).T.astype(bf16)
        query_t[s] = queries[s].astype(f32).T.astype(bf16)
    for s in range(seqs):
        grad_query_t[s] = jnp.zeros((head, head_rows), f32)
    loads[1].wait()
    loads[2].wait()

    def block(chip, masked):
        for s in range(seqs):
            at = pl.ds(s * seq_dev, seq_dev)
            slots = (chip * 2, chip * 2 + 1)
            keys = jnp.concatenate([kv_all[slot, at, :head] for slot in slots], axis=0)
            values = jnp.concatenate([kv_all[slot, at, head:] for slot in slots], axis=0)
            probs = jnp.exp2(dot(keys, query_t[s]) * factor - lse[s])
            if masked:
                key = lax.broadcasted_iota(jnp.int32, probs.shape, 0)
                col = lax.broadcasted_iota(jnp.int32, probs.shape, 1)
                row = jnp.where(col >= seq_dev, col - seq_dev, col)
                ahead = (chip * 2 - b) * seq_dev
                probs = jnp.where(key + ahead <= row, probs, 0.0)
            grad_probs = dot(values, grad_t[s])
            grad_scores = (probs * (grad_probs - delta[s])).astype(bf16)
            key_part = (dot(grad_scores, queries[s]) * scale).astype(bf16)
            value_part = dot(probs.astype(bf16), grad_att[s]).astype(bf16)
            for n, slot in enumerate(slots):
                here = slice(n * seq_dev, (n + 1) * seq_dev)
                dkv[slot, at, :head] = key_part[here]
                dkv[slot, at, head:] = value_part[here]
            grad_query_t[s] += t_dot(keys, grad_scores)

    def pair(chip, own_pair):
        if own_pair:
            block(chip, True)
            return
        here = batch.chip(0, 0)

        @pl.when(chip < here)
        def _():
            block(chip, False)

        @pl.when(chip > here)
        def _():
            for n in range(2):
                dkv[chip * 2 + n] = jnp.zeros(dkv.shape[1:], bf16)

    kv_steps = reduce(
        copies,
        batch,
        lambda dr, dq, dc: dkv.at[batch.slot(dr, dq, dc)],
        scratch_kv,
        kv_grad,
        early=True,
    )
    down_steps = reduce(
        copies, tensor, row_unit(tensor, down, own_rows), scratch_d, down_sum, by_mate=False
    )
    pairs = iter(ORDER)

    def next_pair():
        dr, dq = next(pairs)
        pair(batch.chip(dr, dq), (dr, dq) == (0, 0))

    gens = {"k": kv_steps, "l": low_steps, "d": down_steps, "u": up_steps}
    for key in ATTENTION_ORDER:
        if key == "P":
            next_pair()
        else:
            next(gens.get(key, iter(())), None)
    for s in range(seqs):
        value = grad_query_t[s].T * scale
        for h in range(heads):
            grad_query[s * seq_dev : (s + 1) * seq_dev, h * head : (h + 1) * head] = value[
                h * seq_dev : (h + 1) * seq_dev
            ]
    run_all(kv_steps, down_steps, low_steps, up_steps)
    add_rows(final, [down_sum, resid])


def attention_back(
    scale, queries, lse, attended, gate_raw, grad_gated, grad_resid, resid, kv_all, down, up_part
):
    rows, cols = attended.shape
    own_rows, width = resid.shape
    seqs, head_rows, head = queries.shape
    ff = up_part.shape[1]
    depth = width // 16
    shape = jax.ShapeDtypeStruct
    hoist = (queries, attended, gate_raw, grad_gated, grad_resid, resid)
    return pl.pallas_call(
        hoisted(functools.partial(attention_kernel, scale), 6),
        out_shape=[
            shape((rows, cols), f32),
            shape((rows, cols), f32),
            shape((rows, cols), bf16),
            shape((rows, width), bf16),
            shape((own_rows, width), bf16),
            shape((depth, ff), f32),
        ],
        in_specs=[ANY] * 6 + [VM] + [ANY] * 3,
        out_specs=[VM] * 3 + [ANY] + [VM] * 2,
        scratch_shapes=[
            pltpu.VMEM(kv_all.shape, bf16),
            pltpu.VMEM((rows, width), bf16),
            pltpu.VMEM((width, ff), bf16),
            pltpu.VMEM((own_rows, width), bf16),
            pltpu.VMEM(queries.shape, bf16),
            pltpu.VMEM((seqs, head, head_rows), bf16),
            pltpu.VMEM((seqs, head, head_rows), bf16),
            pltpu.VMEM((seqs, 1, head_rows), f32),
            pltpu.VMEM(queries.shape, f32),
            pltpu.VMEM((seqs, head, head_rows), f32),
            pltpu.VMEM(kv_all.shape, bf16),
            pltpu.VMEM((own_rows, width), f32),
        ]
        + reduce_scratch(rows, cols, True)
        + reduce_scratch(own_rows, width, False)
        + reduce_scratch(depth, ff, True)
        + sems(72, 6)
        + hoisted_scratch(hoist),
        name="attention_back",
        compiler_params=params(3, 62),
    )(*hoist, lse, kv_all, down, up_part)


def last_kernel(
    share,
    input_loads,
    grad_query,
    kv_grad,
    gate_grad,
    query_raw,
    kv_raw,
    cosine,
    sine,
    gain_wide,
    gain_head,
    inputs,
    grad_resid,
    final,
    gated,
    norm_mlp_grad,
    normed_in,
    low_in,
    kvo_in,
    qg_in,
    down_in,
    tokens,
    output,
    query_grad,
    key_grad,
    value_grad,
    gate_out_grad,
    out_grad,
    down_grad,
    norm_attn_grad,
    norm_mlp_out,
    gain_query_grad,
    gain_key_grad,
    normed,
    low,
    w_kvo,
    w_qg,
    down_part,
    weight_grad,
    down_sum,
    qg_low,
    kv_low,
    part,
    weight_part,
    held,
    own,
    total,
    mine,
    over_tensor,
    shares,
    over_batch,
    *rest,
):
    scratch = [rest[5 * n : 5 * n + 5] for n in range(4)]
    scratch_w, scratch_d = rest[20:26], rest[26:32]
    copies = Copies(*rest[32:])
    tensor, batch = Group("tensor", False), Group("batch")
    rows, width = normed.shape
    own_rows = inputs.shape[0]
    cols = grad_query.shape[1]
    head = gain_head.shape[1]
    seq_dev = cosine.shape[0]
    depth = weight_grad.shape[0]
    loads = [
        copies.local(a, c)
        for a, c in (
            (qg_in, w_qg),
            (kvo_in, w_kvo),
            (down_in, down_part),
            (normed_in, normed),
            (low_in, low),
        )
    ]
    b = lax.axis_index("batch")
    members = [(0, dq, dr, dc) for dc in range(2) for dq, dr in [(0, 0)] + batch_steps(batch)][1:]
    batch_others = [(batch.slot(dr, dq, dc), batch.t) for _, dq, dr, dc in members]
    enter(tensor.others + batch_others)
    for load in input_loads:
        load.wait()

    def place(ref):
        def unit(slot):
            seq, rest = lax.div(slot, 4), lax.rem(slot, 4)
            return ref.at[seq, pl.ds(pl.multiple_of(rest * own_rows, 16), own_rows), :]

        return unit

    output_steps = gather(copies, tensor, final, place(output), by_mate=False)
    next(output_steps)

    def head_back(raw, gain, grad, at):
        back = grad * cosine[...] - pltpu.roll(grad, head // 2, 1) * sine[...]
        values, terms = norm_back(raw, gain, back)
        return values.astype(bf16), jnp.sum(terms, axis=0, keepdims=True)

    mine[...] = jnp.zeros_like(mine)
    norm_rows = width // 128
    for s in range(rows // seq_dev):
        at = pl.ds(s * seq_dev, seq_dev)
        for h in range(cols // head):
            here = pl.ds(h * head, head)
            qg_low[at, here], terms = head_back(
                query_raw[at, here], gain_head[0:1, :], grad_query[at, here], at
            )
            mine[2 * norm_rows : 2 * norm_rows + 1, :] += terms
        kv_low[at, :head], terms = head_back(
            kv_raw[at, :head], gain_head[1:2, :], kv_grad[at, :head], at
        )
        mine[2 * norm_rows + 1 : 2 * norm_rows + 2, :] += terms
        kv_low[at, head:] = kv_grad[at, head:].astype(bf16)
        qg_low[at, cols:] = gate_grad[at, :]
    loads[0].wait()
    loads[1].wait()
    def part_chunk(n):
        slots = pl.ds(n * 4, 4)
        value = dot_t(qg_low[...], w_qg[slots].reshape(width // 4, 2 * cols))
        value += dot_t(kv_low[...], w_kvo[slots, :depth, :cols].reshape(width // 4, cols))
        part[:, n * (width // 4) : (n + 1) * (width // 4)] = value.astype(bf16)

    steps = []
    for n in range(4):
        part_chunk(n)
        steps.append(
            reduce(
                copies,
                tensor,
                row_unit(tensor, chunk(part, n, 4), own_rows),
                scratch[n],
                chunk(held, n, 4),
            )
        )
        next(steps[n])
    gens = dict(zip("0123", steps))
    gens["o"] = output_steps

    def products():
        for load in loads[2:]:
            load.wait()
        gens["d"] = reduce(
            copies, batch, row_unit(batch, down_part, depth), scratch_d, down_sum, by_mate=False
        )
        next(gens["d"])
        yield
        yield from outer(normed, qg_low, weight_part, slice(0, 2 * cols))
        yield from outer(normed, kv_low, weight_part, slice(2 * cols, 3 * cols), 1024)
        yield from outer(low, gated, weight_part, slice(3 * cols, 4 * cols), 1024)
        gens["w"] = reduce(
            copies, batch, row_unit(batch, weight_part, depth), scratch_w, weight_grad, by_mate=False
        )
        next(gens["w"])

    gens["f"] = products()
    for n in range(norm_rows):
        mine[norm_rows + n : norm_rows + n + 1, :] = norm_mlp_grad[:, n * 128 : (n + 1) * 128]

    def small():
        first = [
            copies.send(mine, over_tensor.at[tensor.t], device) for device in tensor.others
        ]
        over_tensor[tensor.t] = mine[...]
        yield
        for copy in first:
            copy.wait_recv()
        total_t = over_tensor[0]
        for n in range(1, 8):
            total_t = total_t + over_tensor[n]
        for n in range(16):
            shares[n, 0:1, :] = total_t[n : n + 1]
            shares[n, 1:2, :] = total_t[norm_rows + n : norm_rows + n + 1]
            shares[n, 2:4, :] = total_t[2 * norm_rows : 2 * norm_rows + 2]
            shares[n, 4:8, :] = jnp.zeros((4, 128), f32)
        second = [
            copies.send(shares.at[batch.slot(dr, dq, dc)], over_batch.at[b], device)
            for (_, dq, dr, dc), device in zip(members, batch_others)
        ]
        over_batch[b] = shares[b]
        yield
        for copy in second:
            copy.wait_recv()
        total_b = over_batch[0]
        for n in range(1, 16):
            total_b = total_b + over_batch[n]
        heads_own = pltpu.roll(total_b, (128 - share * b) % 128, 1)
        norm_attn_grad[...] = total_b[0:1]
        norm_mlp_out[...] = total_b[1:2]
        gain_query_grad[...] = heads_own[2:3, 0:share]
        gain_key_grad[...] = heads_own[3:4, 0:share]
        for copy in first + second:
            copy.wait_send()

    def along():
        for step in steps:
            for _ in step:
                pass
        total[...] = jnp.zeros_like(total)

        def body(at):
            back, terms = norm_back(inputs[at, :].astype(f32), gain_wide[0:1, :], held[at, :])
            total[...] += terms
            own[at, :] = (grad_resid[at, :] + back).astype(bf16)

        each_rows(own_rows, 16, body)
        gain_row = jnp.sum(total[...], axis=0, keepdims=True)
        for n in range(norm_rows):
            mine[n : n + 1, :] = gain_row[:, n * 128 : (n + 1) * 128]
        big = gather(copies, tensor, own, place(tokens))
        few = small()
        for _ in big:
            next(few, None)
            yield
        yield from few

    gens["x"] = along()
    for key in LAST_ORDER:
        next(gens.get(key, iter(())), None)
    for _ in gens["f"]:
        pass
    run_all(*[gens[key] for key in "xodw"])
    query_grad[...] = weight_grad[:, :cols]
    gate_out_grad[...] = weight_grad[:, cols : 2 * cols]
    key_grad[...] = weight_grad[:, 2 * cols : 2 * cols + head]
    value_grad[...] = weight_grad[:, 2 * cols + head : 3 * cols]
    out_grad[...] = weight_grad[:, 3 * cols :].T
    down_grad[...] = down_sum[...].T


def batch_steps(batch):
    return [(dq, dr) for dr, dq in batch.steps]


def last_step(scale_free, held_in_hbm, few_shape, share):
    grad_query, inputs = scale_free[0], scale_free[9]
    seqs = grad_query.shape[0] // scale_free[5].shape[0]
    normed, low, kvo, qg, down_part = held_in_hbm
    own_rows, width = inputs.shape
    rows, cols = grad_query.shape
    ff = down_part.shape[1]
    depth = width // 16
    shape = jax.ShapeDtypeStruct
    return pl.pallas_call(
        hoisted(functools.partial(last_kernel, share), len(scale_free)),
        out_shape=[
            shape((seqs, rows // seqs, width), bf16),
            shape((seqs, rows // seqs, width), bf16),
            shape((depth, cols), f32),
            shape((depth, cols // 2), f32),
            shape((depth, cols // 2), f32),
            shape((depth, cols), f32),
            shape((cols, depth), f32),
            shape((ff, depth), f32),
            shape((1, depth), f32),
            shape((1, depth), f32),
            shape((1, share), f32),
            shape((1, share), f32),
        ],
        in_specs=[ANY] * (len(scale_free) + len(held_in_hbm)),
        out_specs=[ANY] * 2 + [VM] * 10,
        scratch_shapes=[
            pltpu.VMEM((rows, width), bf16),
            pltpu.VMEM((rows, width), bf16),
            pltpu.VMEM(kvo.shape, bf16),
            pltpu.VMEM(qg.shape, bf16),
            pltpu.VMEM((width, ff), bf16),
            pltpu.VMEM((depth, 4 * cols), f32),
            pltpu.VMEM((depth, ff), f32),
            pltpu.VMEM((rows, 2 * cols), bf16),
            pltpu.VMEM((rows, cols), bf16),
            pltpu.VMEM((rows, width), bf16),
            pltpu.VMEM((width, 4 * cols), bf16),
            pltpu.VMEM((own_rows, width), f32),
            pltpu.VMEM((own_rows, width), bf16),
            pltpu.VMEM((16, width), f32),
            pltpu.VMEM(few_shape, f32),
            pltpu.VMEM((8,) + few_shape, f32),
            pltpu.VMEM((16, 8, 128), f32),
            pltpu.VMEM((16, 8, 128), f32),
        ]
        + reduce_scratch(own_rows, width // 4, False) * 4
        + reduce_scratch(depth, 4 * cols, True)
        + reduce_scratch(depth, ff, True)
        + sems(180, 12)
        + hoisted_scratch(scale_free),
        name="projections_back",
        compiler_params=params(4, 62),
    )(*scale_free, *held_in_hbm)


def shards(
    tokens,
    target,
    domain_ids,
    domain_counts,
    weight_index,
    loss_weights,
    w_query,
    w_key,
    w_value,
    w_gate_out,
    w_output,
    w_gate,
    w_up,
    w_down,
    norm_attn,
    norm_mlp,
    gain_query,
    gain_key,
):
    seq_count, seq_dev, width = tokens.shape
    rows = seq_count * seq_dev
    members = lax.axis_size("tensor")
    batch_count = lax.axis_size("batch")
    b, t = lax.axis_index("batch"), lax.axis_index("tensor")
    own_rows = rows // members
    seq_len = seq_dev * batch_count
    head = gain_query.shape[0] * batch_count
    scale = head ** (-0.5)
    q_cols, k_cols = w_query.shape[1], w_key.shape[1]
    heads = q_cols // head

    half_size = head // 2
    pos_local = (b * seq_dev + jnp.arange(seq_dev, dtype=jnp.int32)).astype(f32)
    inverse_freq = rope_base ** (-(jnp.arange(head) % half_size).astype(f32) / half_size)
    angles = pos_local[:, None] * inverse_freq[None, :]
    sign = jnp.where(jnp.arange(head) < half_size, -1.0, 1.0).astype(f32)
    cosine_wide, sine_wide = jnp.cos(angles), jnp.sin(angles) * sign

    tokens_low = tokens.reshape(rows, width)
    ff = w_gate.shape[1]
    (
        normed_low,
        query_raw,
        kv_raw,
        gate_raw,
        queries,
        kv_all,
        attended,
        lse,
        gated_low,
        normed_mlp_low,
        resid_own,
        wide_kvo,
        wide_qg,
        w_out_all,
        wide_gate,
        wide_up,
        wide_down,
        gain_wide,
        gain_head,
        inputs_own,
        grad_final_own,
        grad_final_low,
    ) = forward(
        scale,
        seq_count,
        (
            tokens_low,
            cosine_wide,
            sine_wide,
            domain_ids,
            domain_counts,
            weight_index,
            loss_weights,
            norm_attn[None],
            norm_mlp[None],
            gain_query[None],
            gain_key[None],
            w_output,
            w_down,
        ),
        (w_query, w_key, w_value, w_gate_out, w_gate, w_up),
        target.reshape(rows, width),
    )

    weights = [w.reshape(width, ff) for w in (wide_gate, wide_up, wide_down)]
    (
        down_part,
        up_weight_part,
        down_weight_part,
        grad_gate,
        grad_resid_own,
        grad_gated,
        norm_mlp_terms,
    ) = mlp(
        resid_own,
        grad_final_own,
        gain_wide,
        normed_mlp_low,
        grad_final_low,
        weights,
        w_out_all,
    )
    grad_query_rot, kv_grad, gate_raw_grad, grad_resid_low, final_own, grad_up = attention_back(
        scale,
        queries,
        lse,
        attended,
        gate_raw,
        grad_gated,
        grad_resid_own,
        resid_own,
        kv_all,
        down_part,
        up_weight_part,
    )
    norm_rows = width // 128
    grad_tokens, output, *grads = last_step(
        (
            grad_query_rot,
            kv_grad,
            gate_raw_grad,
            query_raw,
            kv_raw,
            cosine_wide,
            sine_wide,
            gain_wide,
            gain_head,
            inputs_own,
            grad_resid_own,
            final_own,
            gated_low,
            norm_mlp_terms,
        ),
        (normed_low, grad_resid_low, wide_kvo, wide_qg, down_weight_part),
        (2 * norm_rows + 8, 128),
        gain_query.shape[0],
    )

    return (
        output,
        grad_tokens.astype(f32),
        *grads[:5],
        grad_gate,
        grad_up,
        grads[5],
        *[g.reshape(-1) for g in grads[6:]],
    )


def solution(mesh):
    in_specs = (
        P(None, "batch", None),
        P(None, "batch", None),
        P(),
        P(),
        P(),
        P(),
        P("batch", "tensor"),
        P("batch", "tensor"),
        P("batch", "tensor"),
        P("batch", "tensor"),
        P("tensor", "batch"),
        P("batch", "tensor"),
        P("batch", "tensor"),
        P("tensor", "batch"),
        P("batch"),
        P("batch"),
        P("batch"),
        P("batch"),
    )
    out_specs = (
        P(None, "batch", None),
        P(None, "batch", None),
        P("batch", "tensor"),
        P("batch", "tensor"),
        P("batch", "tensor"),
        P("batch", "tensor"),
        P("tensor", "batch"),
        P("batch", "tensor"),
        P("batch", "tensor"),
        P("tensor", "batch"),
        P("batch"),
        P("batch"),
        P("batch"),
        P("batch"),
    )
    return jax.shard_map(shards, mesh=mesh, in_specs=in_specs, out_specs=out_specs, check_vma=False)
```
